32 devices in a mesh: dp: 8 (over z, x), mp: 4 (over y, core).
Axes of the slice: x: 2, y: 2, z: 4, core: 2. Of those that a mesh axis runs over, the one named last changes fastest.
Arguments:
- input_field: bfloat16 [8, 192, 512], P('dp'), may hold values from -6 to 6
- variable_ids: int32 [48], replicated, may hold values from 0 to 47, as said below
- lead_bucket: int32 [8], P('dp'), may hold values from 0 to 55
- patch_table: bfloat16 [48, 4, 1024], replicated, may hold values from -3 to 3
- variable_table: bfloat16 [48, 1024], replicated, may hold values from -6 to 6
- variable_query: bfloat16 [1024], replicated, may hold values from -6 to 6
- mix_weights: bfloat16 [1024, 3, 1024], P(None, None, 'mp'), may hold values from -0.1875 to 0.1875
- mix_output: bfloat16 [1024, 1024], P('mp'), may hold values from -0.375 to 0.375
- pos_table: bfloat16 [512, 1024], replicated, may hold values from -6 to 6
- lead_table: bfloat16 [56, 1024], replicated, may hold values from -6 to 6
- first_gain: float32 [1024], replicated, may hold values from 0.5 to 1.5
- first_bias: float32 [1024], replicated, may hold values from -3 to 3
- attn_weights: bfloat16 [1024, 3, 1024], P(None, None, 'mp'), may hold values from -0.1875 to 0.1875
- attn_output: bfloat16 [1024, 1024], P('mp'), may hold values from -1.5 to 1.5
- second_gain: float32 [1024], replicated, may hold values from 0.5 to 1.5
- second_bias: float32 [1024], replicated, may hold values from -3 to 3
- up_weight: bfloat16 [1024, 4096], P(None, 'mp'), may hold values from -0.1875 to 0.1875
- down_weight: bfloat16 [4096, 1024], P('mp'), may hold values from -0.1875 to 0.1875
- cotangent: bfloat16 [4096, 1024], P(('dp', 'mp')), may hold values from -6 to 6
Outputs:
- activations: float32 [4096, 1024], P(('dp', 'mp'))
- field_grad: float32 [8, 192, 512], P('dp', None, 'mp')
- patch_grad: float32 [48, 4, 1024], P(None, None, ('dp', 'mp'))
- variable_grad: float32 [48, 1024], P(None, ('dp', 'mp'))
- query_grad: float32 [1024], P(('dp', 'mp'))
- mix_weights_grad: float32 [1024, 3, 1024], P('dp', None, 'mp')
- mix_output_grad: float32 [1024, 1024], P('mp', 'dp')
- pos_grad: float32 [512, 1024], P('mp', 'dp')
- lead_grad: float32 [56, 1024], P(None, ('dp', 'mp'))
- first_gain_grad: float32 [1024], P(('dp', 'mp'))
- first_bias_grad: float32 [1024], P(('dp', 'mp'))
- attn_weights_grad: float32 [1024, 3, 1024], P('dp', None, 'mp')
- attn_output_grad: float32 [1024, 1024], P('mp', 'dp')
- second_gain_grad: float32 [1024], P(('dp', 'mp'))
- second_bias_grad: float32 [1024], P(('dp', 'mp'))
- up_grad: float32 [1024, 4096], P('dp', 'mp')
- down_grad: float32 [4096, 1024], P('mp', 'dp')
The draws below stay inside these ranges and needn't reach their ends.
Inputs may be any that keep to these rules, and one draw needn't show every extreme that they name: `variable_ids`: 48 distinct table rows; rows 0 and 47 are always among them.
All inputs are finite; a program needn't handle non-finite values.
Results may differ from the reference program's by a relative error of at most 0.025.
Values may be sent and summed in bfloat16 or wider, within the bound.
No kernel may reach another device: no remote copies, remote signals or barrier semaphores. Data moves between devices by JAX's collectives and lax.ppermute only.
A program may use at most 320 MiB of HBM per device.

```python
import math
import jax
import jax.numpy as jnp
import numpy as np
from jax import lax

D = 1024
HEADS = 16
HEAD_DIM = 64
FF = 4096
VTOT = 48
VARS = 48
PATCH = 4
BUCKETS = 56
LEN = 512
SAMPLES = 8


def clipped_normal(key, shape):
    return jax.random.truncated_normal(key, -6.0, 6.0, shape, jnp.float32)


def draw_variable_ids(key, part):
    key = jax.random.fold_in(key, 11)
    first_key, second_key = jax.random.split(key)
    middle = (jax.random.permutation(first_key, VTOT - 2)[:VARS - 2] + 1).astype(jnp.int32)
    chosen = jnp.concatenate([jnp.zeros((1,), jnp.int32), middle, jnp.full((1,), VTOT - 1, jnp.int32)])
    return jax.random.permutation(second_key, chosen).astype(jnp.int32)


def draw_input_field(key, part):
    key = jax.random.fold_in(key, 21)
    return clipped_normal(key, (SAMPLES, VARS * PATCH, LEN)).astype(jnp.bfloat16)


def draw_variable_table(key, part):
    key = jax.random.fold_in(key, 22)
    return clipped_normal(key, (VTOT, D)).astype(jnp.bfloat16)


def draw_variable_query(key, part):
    key = jax.random.fold_in(key, 23)
    return clipped_normal(key, (D,)).astype(jnp.bfloat16)


def draw_pos_table(key, part):
    key = jax.random.fold_in(key, 24)
    return clipped_normal(key, (LEN, D)).astype(jnp.bfloat16)


def draw_lead_table(key, part):
    key = jax.random.fold_in(key, 25)
    return clipped_normal(key, (BUCKETS, D)).astype(jnp.bfloat16)


def draw_cotangent(key, part):
    key = jax.random.fold_in(key, 26)
    return clipped_normal(key, (SAMPLES * LEN, D)).astype(jnp.bfloat16)


def set_ends(entries, rng, low, largest):
    place = [jax.random.randint(jax.random.fold_in(rng, axis), (), 0, length) for axis, length in enumerate(entries.shape)]
    longest = entries.shape.index(max(entries.shape))
    next_to = place[:longest] + [(place[longest] + 1) % entries.shape[longest]] + place[longest + 1:]
    return entries.at[tuple(place)].set(low).at[tuple(next_to)].set(largest)


def levels(stream_key, extent, pieces, smallest, largest):
    factor_of, own = 1.0, jax.random.fold_in(stream_key, 6)
    for position, parts in pieces:
        heights = jnp.exp(jax.random.uniform(jax.random.fold_in(own, position), (parts,), jnp.float32, smallest / len(pieces), largest / len(pieces)))
        factor_of = factor_of * jnp.repeat(heights, extent[position] // parts).reshape([-1 if axis == position else 1 for axis in range(len(extent))])
    return factor_of


def rank_bounds(number_of, skew):
    loads = [(1 << 20) // math.isqrt(standing ** skew) + 1 for standing in range(1, number_of + 1)]
    deviation = 1 + sum(loads) // (1 << 30)
    return np.cumsum(np.array([max(1, weight // deviation) for weight in loads]))


def ranked_ids(stream_key, extent, amount, lean):
    table = rank_bounds(amount, lean)
    ticket = jax.random.randint(jax.random.fold_in(stream_key, 1), extent, 0, int(table[amount - 1]))
    grade = jnp.searchsorted(jnp.asarray(table, jnp.int32), ticket, side="right")
    return jax.random.permutation(jax.random.fold_in(stream_key, 2), amount)[grade].astype(jnp.int32)


def noise(rng, shape, deviation, limit, cuts=(), kind=jnp.bfloat16):
    loudness = levels(rng, shape, cuts, -0.22, 0.18) if cuts else 1.0
    entries = jax.random.normal(rng, shape, jnp.float32) * deviation * loudness
    return jnp.minimum(jnp.maximum(entries, -limit), limit).astype(kind)


def setup_inputs(seed: int = 0) -> dict:
    streams_of = jax.random.split(jax.random.key(seed), 20)
    return {
        "input_field": draw_input_field(jax.random.fold_in(streams_of[19], 71), 0),
        "variable_ids": draw_variable_ids(jax.random.fold_in(streams_of[19], 71), 0),
        "lead_bucket": set_ends(ranked_ids(streams_of[2], (SAMPLES,), BUCKETS, 2), jax.random.fold_in(streams_of[2], 3), 0, BUCKETS - 1).astype(jnp.int32),
        "patch_table": noise(streams_of[3], (VTOT, PATCH, D), PATCH ** -0.5, 3.0),
        "variable_table": draw_variable_table(jax.random.fold_in(streams_of[19], 71), 0),
        "variable_query": draw_variable_query(jax.random.fold_in(streams_of[19], 71), 0),
        "mix_weights": noise(streams_of[6], (D, 3, D), D ** -0.5, 0.1875, ((2, 4),)),
        "mix_output": noise(streams_of[7], (D, D), (D // 4) ** -0.5, 0.375, ((0, 4),)),
        "pos_table": draw_pos_table(jax.random.fold_in(streams_of[19], 71), 0),
        "lead_table": draw_lead_table(jax.random.fold_in(streams_of[19], 71), 0),
        "first_gain": jnp.clip(1.0 + 0.1 * jax.random.normal(streams_of[10], (D,), jnp.float32), 0.5, 1.5),
        "first_bias": noise(streams_of[11], (D,), 0.5, 3.0, (), jnp.float32),
        "attn_weights": noise(streams_of[12], (D, 3, D), D ** -0.5, 0.1875, ((2, 4),)),
        "attn_output": noise(streams_of[13], (D, D), (D // 64) ** -0.5, 1.5, ((0, 4),)),
        "second_gain": jnp.clip(1.0 + 0.1 * jax.random.normal(streams_of[14], (D,), jnp.float32), 0.5, 1.5),
        "second_bias": noise(streams_of[15], (D,), 0.5, 3.0, (), jnp.float32),
        "up_weight": noise(streams_of[16], (D, FF), D ** -0.5, 0.1875, ((1, 4),)),
        "down_weight": noise(streams_of[17], (FF, D), (FF // 4) ** -0.5, 0.1875, ((0, 4),)),
        "cotangent": draw_cotangent(jax.random.fold_in(streams_of[19], 71), 0),
    }


@jax.custom_vjp
def low(v):
    return lax.optimization_barrier(v.astype(jnp.bfloat16)).astype(jnp.float32)

@jax.custom_vjp
def low_back(v):
    return v

def low_keep(v):
    return (low(v), None)

def low_pass(kept, grad):
    return (grad,)

def back_keep(v):
    return (v, None)

def back_low(kept, grad):
    return (low(grad),)
low.defvjp(low_keep, low_pass)
low_back.defvjp(back_keep, back_low)
EPS = 1e-05
HIGH = lax.Precision.HIGHEST

def matmul(left, right):
    return jnp.dot(left, right, precision=HIGH)

def layer_norm(values, gain, offset):
    average = lax.optimization_barrier(jnp.mean(values, axis=-1, keepdims=True))
    centered = values - average
    inv_std = lax.rsqrt(lax.optimization_barrier(jnp.mean(centered * centered, axis=-1, keepdims=True)) + EPS)
    return centered * inv_std * gain + offset

def mix_block(x_block, chosen_patch, chosen_var, query_heads, w_key, w_value, w_out):
    tokens = x_block.shape[1]
    spread_x = x_block.reshape(VARS, PATCH, tokens)
    embedded = jnp.einsum('vpt,vpd->tvd', spread_x, chosen_patch, precision=HIGH) + chosen_var[None]
    embedded = low(embedded).reshape(tokens * VARS, D)
    key_rows = low(low_back(matmul(embedded, w_key))).reshape(tokens, VARS, HEADS, HEAD_DIM)
    value_rows = low(low_back(matmul(embedded, w_value))).reshape(tokens, VARS, HEADS, HEAD_DIM)
    scores = jnp.einsum('tvhe,he->tvh', key_rows, query_heads, precision=HIGH) * HEAD_DIM ** (-0.5)
    weights = jax.nn.softmax(scores, axis=1)
    mixed = jnp.einsum('tvh,tvhe->the', low(weights), value_rows, precision=HIGH)
    mixed = low(mixed.reshape(tokens, D))
    return low_back(matmul(mixed, w_out))

def attend(query_rows, key_rows, value_rows):
    block_rows = min(512, LEN)
    query_blocks = query_rows.reshape(LEN // block_rows, block_rows, HEADS, HEAD_DIM)

    def one_block(query_block):
        scores = low_back(jnp.einsum('qhe,khe->hqk', query_block, key_rows, precision=HIGH) * HEAD_DIM ** (-0.5))
        weights = jax.nn.softmax(scores, axis=-1)
        return jnp.einsum('hqk,khe->qhe', low(weights), value_rows, precision=HIGH)
    return lax.map(jax.checkpoint(one_block), query_blocks).reshape(LEN, D)

def sample_forward(x_sample, bucket, variable_ids, params):
    patch_table, variable_table, variable_query, mix_weights, mix_output, pos_table, lead_table, first_gain, first_bias, attn_weights, attn_output, second_gain, second_bias, up_weight, down_weight = params
    chosen_patch = patch_table[variable_ids]
    chosen_var = variable_table[variable_ids]
    query_heads = low(matmul(low(variable_query)[None, :], mix_weights[:, 0, :])).reshape(HEADS, HEAD_DIM)
    block_tokens = min(256, LEN)
    x_blocks = x_sample.reshape(VARS * PATCH, LEN // block_tokens, block_tokens).transpose(1, 0, 2)

    def mix_one(x_block):
        return mix_block(x_block, chosen_patch, chosen_var, query_heads, mix_weights[:, 1, :], mix_weights[:, 2, :], mix_output)
    mixed_out = lax.map(jax.checkpoint(mix_one), x_blocks).reshape(LEN, D)
    residual_in = mixed_out + pos_table + lead_table[bucket][None, :]
    first_normed = low(layer_norm(residual_in, first_gain, first_bias))
    query_rows = low(low_back(matmul(first_normed, attn_weights[:, 0, :]))).reshape(LEN, HEADS, HEAD_DIM)
    key_rows = low(low_back(matmul(first_normed, attn_weights[:, 1, :]))).reshape(LEN, HEADS, HEAD_DIM)
    value_rows = low(low_back(matmul(first_normed, attn_weights[:, 2, :]))).reshape(LEN, HEADS, HEAD_DIM)
    attended = low(low_back(attend(query_rows, key_rows, value_rows)))
    residual_mid = residual_in + low_back(matmul(attended, attn_output))
    second_normed = low(layer_norm(residual_mid, second_gain, second_bias))
    pre_act = low_back(matmul(second_normed, up_weight))
    hidden = low(jax.nn.gelu(pre_act))
    return residual_mid + low_back(matmul(hidden, down_weight))

def reference(input_field, variable_ids, lead_bucket, patch_table, variable_table, variable_query, mix_weights, mix_output, pos_table, lead_table, first_gain, first_bias, attn_weights, attn_output, second_gain, second_bias, up_weight, down_weight, cotangent):
    params = tuple((item.astype(jnp.float32) for item in (patch_table, variable_table, variable_query, mix_weights, mix_output, pos_table, lead_table, first_gain, first_bias, attn_weights, attn_output, second_gain, second_bias, up_weight, down_weight)))
    field_values = input_field.astype(jnp.float32)

    def forward(field_now, weights_now):

        def one_sample(pair):
            return sample_forward(pair[0], pair[1], variable_ids, weights_now)
        return lax.map(jax.checkpoint(one_sample), (field_now, lead_bucket))
    outputs, pull_back = jax.vjp(forward, field_values, params)
    field_grad, grads = pull_back(cotangent.astype(jnp.float32).reshape(SAMPLES, LEN, D))
    return (outputs.reshape(SAMPLES * LEN, D), field_grad, grads[0], grads[1], grads[2], grads[3], grads[4], grads[5], grads[6], grads[7], grads[8], grads[9], grads[10], grads[11], grads[12], grads[13], grads[14])
```

```python
import functools

import jax
import jax.numpy as jnp
from jax import lax
from jax.experimental import pallas as pl
from jax.experimental.pallas import tpu as pltpu
from jax.sharding import PartitionSpec as P

HEAD_DIM = 64
EPS = 1e-05
SCALE = HEAD_DIM ** (-0.5)
HIGH = lax.Precision.HIGHEST
F32 = jnp.float32
BF16 = jnp.bfloat16
VMEM = pl.BlockSpec(memory_space=pltpu.VMEM)
LIMIT = 48 * 1024 * 1024


def dot(left, right, left_dim=1, right_dim=0, precision=None):
    return lax.dot_general(
        left,
        right,
        (((left_dim,), (right_dim,)), ((), ())),
        precision=precision,
        preferred_element_type=F32,
    )


def call(kernel, outs, *args, flops=0, moved=0):
    cost = pl.CostEstimate(flops=flops, bytes_accessed=moved, transcendentals=0)
    return pl.pallas_call(
        kernel,
        out_shape=[jax.ShapeDtypeStruct(shape, kind) for shape, kind in outs],
        in_specs=[VMEM] * len(args),
        out_specs=[VMEM] * len(outs),
        compiler_params=pltpu.CompilerParams(vmem_limit_bytes=LIMIT),
        cost_estimate=cost,
    )(*args)


def iota(shape, dim):
    return lax.broadcasted_iota(jnp.int32, shape, dim)


def head_lanes(width, head):
    lane = iota((1, width), 1)
    return (lane >= head * HEAD_DIM) & (lane < (head + 1) * HEAD_DIM)


def lanes_of(rows, head):
    return jnp.where(head_lanes(rows.shape[1], head), rows, jnp.zeros_like(rows))


def spread(rows, pixels, top, bottom):
    variables = top.shape[0]
    parts = [top * rows[p * variables : (p + 1) * variables] for p in range(pixels)]
    parts.append(top)
    if bottom:
        parts.append(jnp.zeros((bottom, top.shape[1]), top.dtype))
    return jnp.concatenate(parts, axis=0)


def mix_forward(
    pixels,
    key_ref,
    x_ref,
    table_ref,
    w_ref,
    query_ref,
    xt_ref,
    probs_ref,
    values_ref,
    keys_t_ref,
    score_ref,
    query_col_ref,
    mixed_ref,
):
    channels = x_ref.shape[0]
    variables = channels // pixels
    rows = table_ref.shape[0]
    width = w_ref.shape[2]
    heads = width // HEAD_DIM
    bottom = rows - channels - variables
    pick = (iota((channels, channels), 0) == key_ref[...]).astype(F32).astype(BF16)
    xt = dot(pick, x_ref[...])
    xt_ref[...] = xt.astype(BF16)
    query = dot(query_ref[...], w_ref[0])[0:1].astype(BF16).astype(F32)
    keys = dot(table_ref[...], w_ref[1])
    values = dot(table_ref[...], w_ref[2])
    values_ref[...] = values.astype(BF16)
    keys_t_ref[...] = keys.T
    query_col_ref[...] = jnp.broadcast_to(query, (128, width)).T
    same = (iota((width, 128), 0) // HEAD_DIM == iota((width, 128), 1)).astype(F32)
    score = dot(keys * query, same, precision=HIGH) * SCALE
    score_ref[...] = score
    values_t = values.T.astype(BF16)
    for head in range(heads):
        column = score[:, head : head + 1]
        logits = jnp.broadcast_to(column[channels : channels + variables], (variables, xt.shape[1]))
        for p in range(pixels):
            part = slice(p * variables, (p + 1) * variables)
            logits = logits + column[part] * xt[part]
        weights = jnp.exp(logits - jnp.max(logits, axis=0, keepdims=True))
        probs = weights / jnp.sum(weights, axis=0, keepdims=True)
        probs_ref[head * variables : (head + 1) * variables] = probs
        low = probs.astype(BF16).astype(F32)
        mixing = spread(xt, pixels, low, bottom).astype(BF16)
        part = slice(head * HEAD_DIM, (head + 1) * HEAD_DIM)
        mixed_ref[part] = dot(values_t[part], mixing).astype(BF16)


def mix_backward(
    pixels,
    key_ref,
    xt_ref,
    probs_ref,
    values_ref,
    score_ref,
    w_out_ref,
    grad_ref,
    field_ref,
    mass_ref,
    bias_ref,
):
    channels = xt_ref.shape[0]
    variables = channels // pixels
    rows, width = values_ref.shape
    heads = width // HEAD_DIM
    bottom = rows - channels - variables
    xt = xt_ref[...].astype(F32)
    grad_t = dot(w_out_ref[...], grad_ref[...], 1, 1).astype(BF16)
    values = values_ref[...]
    score = score_ref[...]
    field = jnp.zeros(xt.shape, F32)
    lane = iota((rows, 128), 1)
    sums = jnp.zeros((rows, 128), F32)
    for head in range(heads):
        probs = probs_ref[head * variables : (head + 1) * variables]
        low = probs.astype(BF16).astype(F32)
        back = dot(lanes_of(values, head), grad_t)
        prob_grad = back[channels : channels + variables]
        for p in range(pixels):
            part = slice(p * variables, (p + 1) * variables)
            prob_grad = prob_grad + xt[part] * back[part]
        middle = jnp.sum(probs * prob_grad, axis=0, keepdims=True)
        score_grad = probs * (prob_grad - middle)
        column = score[:, head : head + 1]
        field = field + jnp.concatenate(
            [
                score_grad * column[p * variables : (p + 1) * variables]
                + low * back[p * variables : (p + 1) * variables]
                for p in range(pixels)
            ],
            axis=0,
        )
        total = jnp.sum(
            spread(xt, pixels, score_grad * SCALE, bottom), axis=1, keepdims=True
        )
        sums = jnp.where(lane == head, total, sums)
        mixing = spread(xt, pixels, low, bottom).astype(BF16)
        part = slice(head * HEAD_DIM, (head + 1) * HEAD_DIM)
        mass_ref[part] = dot(grad_t[part], mixing, 1, 1)
    bias_ref[...] = sums.T[0:8]
    pick = (key_ref[...] == iota((channels, channels), 1)).astype(F32).astype(BF16)
    field_ref[...] = dot(pick, field.astype(BF16)).astype(BF16)


def attend_forward(rows_ref, w_ref, q_ref, k_ref, v_ref, out_ref, log_ref):
    rows = rows_ref[...]
    width = w_ref.shape[2]
    query = dot(rows, w_ref[0]).astype(BF16)
    key = dot(rows, w_ref[1]).astype(BF16)
    value = dot(rows, w_ref[2]).astype(BF16)
    q_ref[...] = query
    k_ref[...] = key
    v_ref[...] = value
    scaled = (query.astype(F32) * SCALE).astype(BF16)
    value_t = value.astype(F32).T.astype(BF16)
    parts = []
    for head in range(width // HEAD_DIM):
        scores = dot(lanes_of(key, head), scaled, 1, 1)
        top = jnp.max(scores, axis=0, keepdims=True)
        weights = jnp.exp(scores - top)
        total = jnp.sum(weights, axis=0, keepdims=True)
        log_ref[head : head + 1] = top + jnp.log(total)
        probs = (weights * (1.0 / total)).astype(BF16)
        parts.append(dot(value_t[head * HEAD_DIM : (head + 1) * HEAD_DIM], probs))
    out_ref[...] = jnp.concatenate(parts, axis=0).T.astype(BF16)


def attend_backward(q_ref, k_ref, v_ref, log_ref, grad_ref, w_ref, out_ref):
    query = q_ref[...]
    key = k_ref[...]
    value = v_ref[...]
    width = query.shape[1]
    grad = dot(grad_ref[...], w_ref[...], 1, 1).astype(BF16)
    scaled = (query.astype(F32) * SCALE).astype(BF16)
    key_t = key.astype(F32).T.astype(BF16)
    query_parts = []
    key_grad = jnp.zeros(key.shape, F32)
    value_grad = jnp.zeros(key.shape, F32)
    for head in range(width // HEAD_DIM):
        scores = dot(lanes_of(key, head), scaled, 1, 1)
        probs = jnp.exp(scores - log_ref[head : head + 1])
        prob_grad = dot(lanes_of(value, head), grad, 1, 1)
        middle = jnp.sum(probs * prob_grad, axis=0, keepdims=True)
        score_grad = (probs * (prob_grad - middle)).astype(BF16)
        query_parts.append(dot(key_t[head * HEAD_DIM : (head + 1) * HEAD_DIM], score_grad))
        key_grad = key_grad + dot(score_grad, lanes_of(scaled, head))
        value_grad = value_grad + dot(probs.astype(BF16), lanes_of(grad, head))
    out_ref[0] = (jnp.concatenate(query_parts, axis=0).T * SCALE).astype(BF16)
    out_ref[1] = key_grad.astype(BF16)
    out_ref[2] = value_grad.astype(BF16)


def finish(mass_ref, bias_ref, query_col_ref, keys_t_ref, table_ref, w_ref, query_ref, grad_ref, back_ref):
    width, rows = mass_ref.shape
    heads = width // HEAD_DIM
    mass = mass_ref[...]
    bias = jnp.concatenate(
        [
            jnp.broadcast_to(bias_ref[head : head + 1], (HEAD_DIM, rows))
            for head in range(heads)
        ],
        axis=0,
    )
    key_mass = (bias * query_col_ref[:, 0:1]).astype(BF16)
    mass = mass.astype(BF16)
    total = jnp.sum(keys_t_ref[...] * bias, axis=1, keepdims=True)
    own = table_ref.shape[1]
    total_row = jnp.broadcast_to(total, (width, 128)).T[0:1]
    table_t = table_ref[...].astype(F32).T.astype(BF16)
    grad_ref[0] = query_ref[...] * total_row
    grad_ref[1] = dot(table_t, key_mass, 1, 1)
    grad_ref[2] = dot(table_t, mass, 1, 1)
    back = dot(w_ref[1], key_mass) + dot(w_ref[2], mass)
    query_back = jnp.sum(w_ref[0].astype(F32) * total_row, axis=1, keepdims=True)
    back_ref[...] = jnp.where(iota((own, rows), 1) == rows - 1, query_back, back)


def normalize(values):
    average = jnp.mean(values, axis=-1, keepdims=True)
    centered = values - average
    inv_std = lax.rsqrt(jnp.mean(centered * centered, axis=-1, keepdims=True) + EPS)
    return (centered * inv_std, inv_std)


def norm_back(grad_out, normed, inv_std, gain):
    scaled = grad_out * gain
    first_mean = jnp.mean(scaled, axis=-1, keepdims=True)
    second_mean = jnp.mean(scaled * normed, axis=-1, keepdims=True)
    return inv_std * (scaled - first_mean - normed * second_mean)


def pairs(count, bit):
    return [(i, i ^ bit) for i in range(count)]


def body(
    mesh_dp,
    mesh_mp,
    input_field,
    variable_ids,
    lead_bucket,
    patch_table,
    variable_table,
    variable_query,
    mix_weights,
    mix_output,
    pos_table,
    lead_table,
    first_gain,
    first_bias,
    attn_weights,
    attn_output,
    second_gain,
    second_bias,
    up_weight,
    down_weight,
    cotangent,
):
    length = input_field.shape[2]
    channels = input_field.shape[1]
    variables = variable_ids.shape[0]
    pixels = channels // variables
    model_width = pos_table.shape[1]
    quarter = cotangent.shape[0]
    head_width = mix_weights.shape[2]
    me_mp = lax.axis_index("mp")
    me_dp = lax.axis_index("dp")
    own_width = model_width // mesh_dp
    half = 2 * quarter

    def swap_core(value):
        return lax.ppermute(value, "mp", pairs(mesh_mp, 1))

    def swap_chip(value):
        return lax.ppermute(value, "mp", pairs(mesh_mp, 2))

    def gather(own):
        far = swap_chip(own)
        near = swap_core(jnp.concatenate([own, far], axis=0))
        return jnp.concatenate([own, far, near], axis=0)

    def reduce(left, weights, product):
        near = swap_core(product(left[half:], weights).astype(BF16))
        kept = product(left[:half], weights) + near.astype(F32)
        far = swap_chip(kept[quarter:].astype(BF16))
        return kept[:quarter] + far.astype(F32)

    def own_rows(rows, start):
        return lax.dynamic_slice_in_dim(rows, start, quarter, 0)

    def split_bit(value, axis, bit, step):
        shape = value.shape
        count = shape[axis] // (2 * step)
        view = value.reshape(shape[:axis] + (count, 2, step) + shape[axis + 1 :])

        def part(which):
            picked = lax.dynamic_index_in_dim(view, which, axis + 1, keepdims=False)
            return picked.reshape(shape[:axis] + (count * step,) + shape[axis + 1 :])

        return part(bit), part(1 - bit)

    bits = [1 << i for i in range(mesh_dp.bit_length() - 1)]

    def reduce_samples(keep, send, axis, done, wire=BF16):
        for bit in bits:
            if not (done and bit == 1):
                mine = (me_dp // bit) % 2
                keep, send = split_bit(keep, axis, mine, keep.shape[axis] * bit // mesh_dp)
            got = lax.ppermute(send.astype(wire), "dp", pairs(mesh_dp, bit))
            keep = keep + got.astype(F32)
        return keep

    def step_of(value, axis, bit):
        return value.shape[axis] * bit // mesh_dp

    def product_sum(left, right, axis):
        mine = me_dp % 2
        if axis == 0:
            step = left.shape[1] // mesh_dp
            keep, send = split_bit(left, 1, mine, step)
            return reduce_samples(dot(keep, right, 0, 0), dot(send, right, 0, 0).astype(BF16), 0, True)
        step = right.shape[1] // mesh_dp
        keep, send = split_bit(right, 1, mine, step)
        return reduce_samples(dot(left, keep, 0, 0), dot(left, send, 0, 0).astype(BF16), 1, True)

    w_mix = mix_weights.transpose(1, 0, 2)
    w_attn = attn_weights.transpose(1, 0, 2)
    order = [0, 2, 1, 3]
    field = jnp.concatenate(
        [
            lax.dynamic_slice_in_dim(input_field[0], (me_mp ^ k) * quarter, quarter, 1)
            for k in order
        ],
        axis=1,
    )
    table_rows = channels + variables
    padded = -(-(table_rows + 1) // 128) * 128
    table = jnp.concatenate(
        [
            patch_table.transpose(1, 0, 2).reshape(channels, model_width),
            variable_table,
            jnp.zeros((padded - table_rows, model_width), BF16),
        ],
        axis=0,
    )
    place = (
        jnp.arange(pixels, dtype=jnp.int32)[None, :] * variables + variable_ids[:, None]
    ).reshape(channels)
    query_tile = jnp.broadcast_to(variable_query[None], (16, model_width))
    heads = head_width // HEAD_DIM
    field_t, probs, values, keys_t, score, query_col, mixed_t = call(
        functools.partial(mix_forward, pixels),
        [
            ((channels, length), BF16),
            ((heads * variables, length), F32),
            ((padded, head_width), BF16),
            ((head_width, padded), F32),
            ((padded, 128), F32),
            ((head_width, 128), F32),
            ((head_width, length), BF16),
        ],
        place[None],
        field,
        table,
        w_mix,
        query_tile,
        flops=4 * padded * model_width * head_width,
    )
    cot_full = gather(cotangent)

    def product_t(left, right):
        return dot(left, right, 0, 0)

    near = swap_core(dot(mixed_t[:, half:], mix_output, 0, 0).astype(BF16))
    kept = dot(mixed_t[:, :half], mix_output, 0, 0) + near.astype(F32)
    far = swap_chip(kept[quarter:].astype(BF16))
    summed = kept[:quarter] + far.astype(F32)
    lead_row = lax.dynamic_slice_in_dim(lead_table, lead_bucket[0], 1, 0).astype(F32)
    residual_in = summed + own_rows(pos_table, me_mp * quarter).astype(F32) + lead_row
    normed_one, inv_one = normalize(residual_in)
    first_own = (normed_one * first_gain + first_bias).astype(BF16)
    first_normed = gather(first_own)
    query, key, value, attended, logs = call(
        attend_forward,
        [((length, head_width), BF16)] * 4 + [((8, length), F32)],
        first_normed,
        w_attn,
        flops=6 * length * model_width * head_width + 4 * length * length * head_width,
    )
    residual_mid = residual_in + reduce(attended, attn_output, dot)
    normed_two, inv_two = normalize(residual_mid)
    second_own = (normed_two * second_gain + second_bias).astype(BF16)
    second_normed = gather(second_own)
    grad_hidden = dot(cot_full, down_weight, 1, 1)
    pre_act = dot(second_normed, up_weight)
    hidden_wide, gelu_back = jax.vjp(jax.nn.gelu, pre_act)
    hidden = hidden_wide.astype(BF16)
    grad_pre = gelu_back(grad_hidden)[0].astype(BF16)

    def product_right(left, right):
        return dot(left, right, 1, 1)

    grad_second = reduce(grad_pre, up_weight, product_right)
    grad_mid = cotangent.astype(F32) + norm_back(grad_second, normed_two, inv_two, second_gain)
    mid_full = gather(grad_mid.astype(BF16))
    down_sum = product_sum(hidden, cot_full, 1)
    up_sum = product_sum(second_normed, grad_pre, 0)
    activations = residual_mid + reduce(hidden, down_weight, dot)
    (grad_proj,) = call(
        attend_backward,
        [((3, length, head_width), BF16)],
        query,
        key,
        value,
        logs,
        mid_full,
        attn_output,
        flops=2 * length * model_width * head_width + 20 * length * length * head_width,
    )
    attn_out_sum = product_sum(attended, mid_full, 1)

    def product_three(left, weights):
        return (
            dot(left[0], weights[0], 1, 1)
            + dot(left[1], weights[1], 1, 1)
            + dot(left[2], weights[2], 1, 1)
        )

    near = swap_core(product_three(grad_proj[:, half:], w_attn).astype(BF16))
    kept = product_three(grad_proj[:, :half], w_attn) + near.astype(F32)
    far = swap_chip(kept[quarter:].astype(BF16))
    grad_first = kept[:quarter] + far.astype(F32)
    grad_in = grad_mid + norm_back(grad_first, normed_one, inv_one, first_gain)
    grad_full = gather(grad_in.astype(BF16))

    keep, send = split_bit(first_normed, 1, me_dp % 2, own_width)
    attn_sum = reduce_samples(
        jnp.stack([dot(keep, grad_proj[i], 0, 0) for i in range(3)]),
        jnp.stack([dot(send, grad_proj[i], 0, 0).astype(BF16) for i in range(3)]),
        1,
        True,
    )
    keep, send = split_bit(grad_in, 1, me_dp % 2, own_width)
    pos_sum = reduce_samples(keep, send, 1, True)

    field_part, mass, bias = call(
        functools.partial(mix_backward, pixels),
        [
            ((channels, length), BF16),
            ((head_width, padded), F32),
            ((8, padded), F32),
        ],
        place[:, None],
        field_t,
        probs,
        values,
        score,
        mix_output,
        grad_full,
        flops=2 * length * model_width * head_width,
    )
    keep, send = split_bit(grad_full, 1, me_dp % 2, own_width)
    mix_out_sum = reduce_samples(
        dot(mixed_t, keep), dot(mixed_t, send).astype(BF16), 1, True
    )
    kept = field_part[:, :half].astype(F32) + swap_core(field_part[:, half:]).astype(F32)
    far = swap_chip(kept[:, quarter:].astype(BF16))
    field_grad = (kept[:, :quarter] + far.astype(F32))[None]

    for bit in bits:
        mass = mass + lax.ppermute(mass.astype(BF16), "dp", pairs(mesh_dp, bit)).astype(F32)
        bias = bias + lax.ppermute(bias, "dp", pairs(mesh_dp, bit))
    start = me_dp * own_width
    grad_mix, back = call(
        finish,
        [((3, own_width, head_width), F32), ((own_width, padded), F32)],
        mass,
        bias,
        query_col,
        keys_t,
        lax.dynamic_slice_in_dim(table, start, own_width, 1),
        lax.dynamic_slice_in_dim(w_mix, start, own_width, 1),
        lax.dynamic_slice_in_dim(variable_query, start, own_width, 0)[:, None].astype(F32),
        flops=8 * own_width * padded * head_width,
    )
    final = own_width // mesh_mp
    for bit in (2, 1):
        step = back.shape[0] // 2
        mine = (me_mp // bit) % 2
        keep = lax.dynamic_slice_in_dim(back, mine * step, step, 0)
        send = lax.dynamic_slice_in_dim(back, (1 - mine) * step, step, 0)
        back = keep + lax.ppermute(send, "mp", pairs(mesh_mp, bit))
    patch_total = back[:, :channels].reshape(final, pixels, variables).transpose(2, 1, 0)
    variable_total = back[:, channels:table_rows].T
    query_total = back[:, padded - 1]

    own_sum = jnp.sum(grad_in, axis=0)
    sample = jnp.arange(mesh_dp, dtype=jnp.int32) == me_dp
    small = jnp.concatenate(
        [
            jnp.stack(
                [
                    jnp.sum(grad_first * normed_one, axis=0),
                    jnp.sum(grad_first, axis=0),
                    jnp.sum(grad_second * normed_two, axis=0),
                    jnp.sum(grad_second, axis=0),
                ]
            ),
            jnp.where(sample[:, None], own_sum[None], 0.0),
            jnp.broadcast_to(
                jnp.where(sample, lead_bucket[0].astype(F32) / mesh_mp, 0.0)[:, None],
                (mesh_dp, model_width),
            ),
        ],
        axis=0,
    )
    small = reduce_samples(small, None, 1, False, F32)
    small = small + swap_core(small)
    small = small + swap_chip(small)
    small = lax.dynamic_slice_in_dim(small, me_mp * final, final, 1)
    lead_sums = small[4 : 4 + mesh_dp]
    buckets = small[4 + mesh_dp :, 0].astype(jnp.int32)
    lead_total = jnp.sum(
        jnp.where(
            buckets[:, None, None] == jnp.arange(lead_table.shape[0], dtype=jnp.int32)[None, :, None],
            lead_sums[:, None, :],
            0.0,
        ),
        axis=0,
    )
    return (
        activations,
        field_grad,
        patch_total,
        variable_total,
        query_total,
        grad_mix.transpose(1, 0, 2),
        mix_out_sum,
        pos_sum,
        lead_total,
        small[0],
        small[1],
        attn_sum.transpose(1, 0, 2),
        attn_out_sum,
        small[2],
        small[3],
        up_sum,
        down_sum,
    )


def solution(mesh):
    in_specs = (
        P("dp", None, None),
        P(),
        P("dp"),
        P(),
        P(),
        P(),
        P(None, None, "mp"),
        P("mp", None),
        P(),
        P(),
        P(),
        P(),
        P(None, None, "mp"),
        P("mp", None),
        P(),
        P(),
        P(None, "mp"),
        P("mp", None),
        P(("dp", "mp"), None),
    )
    out_specs = (
        P(("dp", "mp"), None),
        P("dp", None, "mp"),
        P(None, None, ("dp", "mp")),
        P(None, ("dp", "mp")),
        P(("dp", "mp")),
        P("dp", None, "mp"),
        P("mp", "dp"),
        P("mp", "dp"),
        P(None, ("dp", "mp")),
        P(("dp", "mp")),
        P(("dp", "mp")),
        P("dp", None, "mp"),
        P("mp", "dp"),
        P(("dp", "mp")),
        P(("dp", "mp")),
        P("dp", "mp"),
        P("mp", "dp"),
    )
    step = functools.partial(body, mesh.shape["dp"], mesh.shape["mp"])
    return jax.shard_map(step, mesh=mesh, in_specs=in_specs, out_specs=out_specs, check_vma=False)
```

```python
import functools

import jax
import jax.numpy as jnp
from jax import lax
from jax.experimental import pallas as pl
from jax.experimental.pallas import tpu as pltpu
from jax.sharding import PartitionSpec as P

HEAD_DIM = 64
LANES = 128
EPS = 1e-05
SCALE = HEAD_DIM ** (-0.5)
HIGH = lax.Precision.HIGHEST
F32 = jnp.float32
BF16 = jnp.bfloat16
VMEM = pl.BlockSpec(memory_space=pltpu.VMEM)
SMEM = pl.BlockSpec(memory_space=pltpu.SMEM)
ANY = pl.BlockSpec(memory_space=pl.ANY)
HBM = pl.BlockSpec(memory_space=pltpu.HBM)
MIB = 1024 * 1024


def dot(left, right, left_dim=1, right_dim=0, precision=None):
    return lax.dot_general(
        left,
        right,
        (((left_dim,), (right_dim,)), ((), ())),
        precision=precision,
        preferred_element_type=F32,
    )


def call(kernel, outs, args, fetch=(), smem=(), after=(), limit=24, cost=1, scratch=()):
    fetch = [item if isinstance(item, tuple) else (item, item.shape, None) for item in fetch]
    count = len(smem)

    def run(*refs):
        at = count + len(fetch)
        sources, rest = refs[count:at], refs[at:]
        inputs, rest = rest[: len(args)], rest[len(args) + len(after) :]
        if not fetch:
            kernel(*refs[:count], *inputs, *rest)
            return
        *rest, marks = rest
        rest, places = rest[: len(rest) - len(fetch)], rest[len(rest) - len(fetch) :]
        copies = []
        for i, (_, _, pick) in enumerate(fetch):
            source = sources[i] if pick is None else pick(sources[i])
            copies.append(pltpu.make_async_copy(source, places[i], marks.at[i]))
        for copy in copies:
            copy.start()
        for copy in copies:
            copy.wait()
        kernel(*refs[:count], *places, *inputs, *rest)

    places = [pltpu.VMEM(shape, array.dtype) for array, shape, _ in fetch]
    marks = [pltpu.SemaphoreType.DMA((len(fetch),))] if fetch else []
    return pl.pallas_call(
        run,
        out_shape=[jax.ShapeDtypeStruct(shape, kind) for shape, kind in outs],
        in_specs=[SMEM] * count + [HBM] * len(fetch) + [VMEM] * len(args) + [ANY] * len(after),
        out_specs=[VMEM] * len(outs),
        scratch_shapes=list(scratch) + places + marks,
        compiler_params=pltpu.CompilerParams(vmem_limit_bytes=limit * MIB),
        cost_estimate=pl.CostEstimate(
            flops=int(cost * 1e9), bytes_accessed=0, transcendentals=0
        ),
    )(*smem, *(array for array, _, _ in fetch), *args, *after)


def my_bit(bit):
    return (lax.axis_index("dp") // bit) % 2


def my_core():
    return lax.axis_index("mp") % 2


def my_chip():
    return lax.axis_index("mp") // 2


def iota(shape, dim):
    return lax.broadcasted_iota(jnp.int32, shape, dim)


def exact(mask):
    return mask.astype(F32).astype(BF16)


def lanes_of(rows, head):
    lane = iota((1, rows.shape[1]), 1)
    mine = (lane >= head * HEAD_DIM) & (lane < (head + 1) * HEAD_DIM)
    return jnp.where(mine, rows, jnp.zeros_like(rows))


def spread(rows, pixels, top, bottom):
    variables = top.shape[0]
    parts = [top * rows[p * variables : (p + 1) * variables] for p in range(pixels)]
    parts.append(top)
    if bottom:
        parts.append(jnp.zeros((bottom, top.shape[1]), top.dtype))
    return jnp.concatenate(parts, axis=0)


def mix_forward(
    pixels,
    quarter,
    ids_ref,
    x_ref,
    patch_ref,
    variable_ref,
    w_ref,
    w_out_ref,
    query_ref,
    table_ref,
    pick_ref,
    xt_ref,
    probs_ref,
    values_ref,
    keys_t_ref,
    score_ref,
    query_col_ref,
    mixed_ref,
    send_a_ref,
    send_b_ref,
    keep_a_ref,
    keep_b_ref,
):
    channels = x_ref.shape[1]
    variables = channels // pixels
    rows, model_width = table_ref.shape
    width = w_ref.shape[2]
    heads = width // HEAD_DIM
    bottom = rows - channels - variables
    row = iota((channels, channels), 0)
    column = iota((channels, channels), 1)
    major = jnp.zeros((channels, channels), jnp.int32)
    for p in range(pixels):
        inside = (row >= p * variables) & (row < (p + 1) * variables)
        major = jnp.where(inside, (row - p * variables) * pixels + p, major)
    flat = patch_ref[...].reshape(channels, model_width)
    table_ref[0:channels] = dot(exact(column == major), flat).astype(BF16)
    table_ref[channels : channels + variables] = variable_ref[...]
    if bottom:
        table_ref[channels + variables :] = jnp.zeros((bottom, model_width), BF16)
    channel = iota((1, channels), 1)
    place = jnp.zeros((1, channels), jnp.int32)
    for v in range(variables):
        pixel = channel - v * pixels
        inside = (pixel >= 0) & (pixel < pixels)
        place = jnp.where(inside, pixel * variables + ids_ref[v], place)
    pick = (iota((channels, channels), 0) == place).astype(F32)
    pick_ref[...] = pick.T.astype(BF16)
    core = my_core()
    starts = [core, 1 - core, core + 2, 3 - core]
    field = jnp.concatenate(
        [x_ref[0, :, pl.ds(pl.multiple_of(s * quarter, LANES), quarter)] for s in starts], axis=1
    )
    xt = dot(pick.astype(BF16), field)
    xt_ref[...] = xt.astype(BF16)
    query_rows = jnp.broadcast_to(query_ref[...].astype(F32)[None], (16, model_width)).astype(BF16)
    query = dot(query_rows, w_ref[0])[0:1].astype(BF16).astype(F32)
    table = table_ref[...]
    keys = dot(table, w_ref[1])
    values = dot(table, w_ref[2])
    values_ref[...] = values.astype(BF16)
    keys_t_ref[...] = keys.T
    query_col_ref[...] = jnp.broadcast_to(query, (LANES, width)).T
    lane = iota((width, LANES), 1) * HEAD_DIM
    row = iota((width, LANES), 0)
    same = ((row >= lane) & (row < lane + HEAD_DIM)).astype(F32)
    score = dot(keys * query, same, precision=HIGH) * SCALE
    score_ref[...] = score
    values_t = values.T.astype(BF16)
    for head in range(heads):
        column = score[:, head : head + 1]
        logits = jnp.broadcast_to(column[channels : channels + variables], (variables, xt.shape[1]))
        for p in range(pixels):
            part = slice(p * variables, (p + 1) * variables)
            logits = logits + column[part] * xt[part]
        weights = jnp.exp(logits - jnp.max(logits, axis=0, keepdims=True))
        probs = weights / jnp.sum(weights, axis=0, keepdims=True)
        probs_ref[head * variables : (head + 1) * variables] = probs
        low = probs.astype(BF16).astype(F32)
        mixing = spread(xt, pixels, low, bottom).astype(BF16)
        part = slice(head * HEAD_DIM, (head + 1) * HEAD_DIM)
        mixed_ref[part] = dot(values_t[part], mixing).astype(BF16)
    out = dot(mixed_ref[...], w_out_ref[...], 0, 0)
    keep_a_ref[...] = out[0:quarter]
    send_a_ref[...] = out[quarter : 2 * quarter].astype(BF16)
    keep_b_ref[...] = out[2 * quarter : 3 * quarter]
    send_b_ref[...] = out[3 * quarter :].astype(BF16)


def mix_backward(
    pixels,
    pick_ref,
    xt_ref,
    probs_ref,
    values_ref,
    score_ref,
    w_out_ref,
    a0_ref,
    a1_ref,
    b0_ref,
    b1_ref,
    mass_ref,
    mass_low_ref,
    bias_ref,
    field_send_ref,
    field_keep_ref,
):
    channels, length = xt_ref.shape
    variables = channels // pixels
    rows, width = values_ref.shape
    heads = width // HEAD_DIM
    bottom = rows - channels - variables
    quarter = length // 4
    xt = xt_ref[...].astype(F32)
    grad = jnp.concatenate([a0_ref[...], a1_ref[...], b0_ref[...], b1_ref[...]], axis=0)
    grad_t = dot(w_out_ref[...], grad, 1, 1).astype(BF16)
    values = values_ref[...]
    score = score_ref[...]
    field = jnp.zeros(xt.shape, F32)
    lane = iota((rows, LANES), 1)
    sums = jnp.zeros((rows, LANES), F32)
    for head in range(heads):
        probs = probs_ref[head * variables : (head + 1) * variables]
        low = probs.astype(BF16).astype(F32)
        back = dot(lanes_of(values, head), grad_t)
        prob_grad = back[channels : channels + variables]
        for p in range(pixels):
            part = slice(p * variables, (p + 1) * variables)
            prob_grad = prob_grad + xt[part] * back[part]
        middle = jnp.sum(probs * prob_grad, axis=0, keepdims=True)
        score_grad = probs * (prob_grad - middle)
        column = score[:, head : head + 1]
        field = field + jnp.concatenate(
            [
                score_grad * column[p * variables : (p + 1) * variables]
                + low * back[p * variables : (p + 1) * variables]
                for p in range(pixels)
            ],
            axis=0,
        )
        spreading = spread(xt, pixels, score_grad * SCALE, bottom)
        sums = jnp.where(lane == head, jnp.sum(spreading, axis=1, keepdims=True), sums)
        mixing = spread(xt, pixels, low, bottom).astype(BF16)
        part = slice(head * HEAD_DIM, (head + 1) * HEAD_DIM)
        mass_ref[part] = dot(grad_t[part], mixing, 1, 1)
    mass_low_ref[...] = mass_ref[...].astype(BF16)
    bias_ref[...] = sums.T[0:8]
    field = dot(pick_ref[...], field.astype(BF16))
    field_keep_ref[:, 0:quarter] = field[:, 0:quarter]
    field_keep_ref[:, quarter:] = field[:, 2 * quarter : 3 * quarter]
    field_send_ref[:, 0:quarter] = field[:, quarter : 2 * quarter].astype(BF16)
    field_send_ref[:, quarter:] = field[:, 3 * quarter :].astype(BF16)


def norm_forward(*refs):
    *terms, gain_ref, bias_ref, out_ref, low_ref = refs
    total = terms[0][...].astype(F32)
    for term in terms[1:]:
        total = total + term[...].astype(F32)
    out_ref[...] = total
    centered = total - jnp.mean(total, axis=1, keepdims=True)
    inv_std = lax.rsqrt(jnp.mean(centered * centered, axis=1, keepdims=True) + EPS)
    low_ref[...] = (centered * inv_std * gain_ref[...] + bias_ref[...]).astype(BF16)


def norm_backward(with_sum, add_refs, *refs):
    keep_ref, far_ref, rows_ref, gain_ref, above_ref = refs[:5]
    more = refs[5 : 5 + add_refs]
    out_ref, low_ref, sums_ref = refs[5 + add_refs :]
    grad = keep_ref[...] + far_ref[...].astype(F32)
    rows = rows_ref[...]
    centered = rows - jnp.mean(rows, axis=1, keepdims=True)
    inv_std = lax.rsqrt(jnp.mean(centered * centered, axis=1, keepdims=True) + EPS)
    normed = centered * inv_std
    scaled = grad * gain_ref[...]
    first = jnp.mean(scaled, axis=1, keepdims=True)
    second = jnp.mean(scaled * normed, axis=1, keepdims=True)
    out = above_ref[...].astype(F32) + inv_std * (scaled - first - normed * second)
    out_ref[...] = out
    low_ref[...] = out.astype(BF16)
    lines = [
        jnp.sum(grad * normed, axis=0, keepdims=True),
        jnp.sum(grad, axis=0, keepdims=True),
    ]
    lines.append(jnp.sum(out, axis=0, keepdims=True) if with_sum else jnp.zeros_like(lines[0]))
    if add_refs:
        one, two_a, two_b = (ref[...] for ref in more)
        lines = [
            lines[0] + one[0:1],
            lines[1] + one[1:2],
            two_a[0:1] + two_b[0:1],
            two_a[1:2] + two_b[1:2],
            lines[2] + one[2:3],
        ]
    lines.append(jnp.zeros((8 - len(lines), grad.shape[1]), F32))
    sums_ref[...] = jnp.concatenate(lines, axis=0)


def project(own_ref, near_ref, w_ref, out_ref):
    rows = jnp.concatenate([own_ref[...], near_ref[...]], axis=0)
    for i in range(3):
        out_ref[i] = dot(rows, w_ref[i]).astype(BF16)


def attend(query, keys, values_t, logs_ref):
    scaled = (query.astype(F32) * SCALE).astype(BF16)
    parts = []
    for head in range(keys.shape[1] // HEAD_DIM):
        scores = dot(lanes_of(keys, head), scaled, 1, 1)
        top = jnp.max(scores, axis=0, keepdims=True)
        weights = jnp.exp(scores - top)
        total = jnp.sum(weights, axis=0, keepdims=True)
        logs_ref[head : head + 1] = top + jnp.log(total)
        probs = (weights * (1.0 / total)).astype(BF16)
        parts.append(dot(values_t[head * HEAD_DIM : (head + 1) * HEAD_DIM], probs))
    return jnp.concatenate(parts, axis=0).T.astype(BF16)


def split_out(out, keep_ref, send_ref):
    quarter = out.shape[0] // 2
    keep_ref[...] = out[:quarter]
    send_ref[...] = out[quarter:].astype(BF16)


def attend_first(own_ref, near_ref, w_ref, first_ref, w_out_ref, second_ref, out_ref, logs_ref, keep_ref, send_ref):
    project(own_ref, near_ref, w_ref, second_ref)
    keys = jnp.concatenate([first_ref[1], second_ref[1]], axis=0)
    values = jnp.concatenate([first_ref[2], second_ref[2]], axis=0)
    out_ref[...] = attend(first_ref[0], keys, values.astype(F32).T.astype(BF16), logs_ref)
    split_out(dot(out_ref[...], w_out_ref[...]), keep_ref, send_ref)


def attend_second(first_ref, second_ref, w_out_ref, out_ref, logs_ref, keep_ref, send_ref):
    keys = jnp.concatenate([first_ref[1], second_ref[1]], axis=0)
    values = jnp.concatenate([first_ref[2], second_ref[2]], axis=0)
    out_ref[...] = attend(second_ref[0], keys, values.astype(F32).T.astype(BF16), logs_ref)
    split_out(dot(out_ref[...], w_out_ref[...]), keep_ref, send_ref)


def attend_grad(grad, query, keys, values, logs_ref):
    scaled = (query.astype(F32) * SCALE).astype(BF16)
    keys_t = keys.astype(F32).T.astype(BF16)
    query_parts = []
    key_grad = jnp.zeros(keys.shape, F32)
    value_grad = jnp.zeros(keys.shape, F32)
    for head in range(keys.shape[1] // HEAD_DIM):
        scores = dot(lanes_of(keys, head), scaled, 1, 1)
        probs = jnp.exp(scores - logs_ref[head : head + 1])
        prob_grad = dot(lanes_of(values, head), grad, 1, 1)
        middle = jnp.sum(probs * prob_grad, axis=0, keepdims=True)
        score_grad = (probs * (prob_grad - middle)).astype(BF16)
        query_parts.append(dot(keys_t[head * HEAD_DIM : (head + 1) * HEAD_DIM], score_grad))
        key_grad = key_grad + dot(score_grad, lanes_of(scaled, head))
        value_grad = value_grad + dot(probs.astype(BF16), lanes_of(grad, head))
    query_grad = (jnp.concatenate(query_parts, axis=0).T * SCALE).astype(BF16)
    return query_grad, key_grad, value_grad


def attend_back_first(own_ref, near_ref, w_out_ref, first_ref, second_ref, logs_ref, query_ref, key_ref, value_ref):
    rows = jnp.concatenate([own_ref[...], near_ref[...]], axis=0)
    grad = dot(rows, w_out_ref[...], 1, 1).astype(BF16)
    keys = jnp.concatenate([first_ref[1], second_ref[1]], axis=0)
    values = jnp.concatenate([first_ref[2], second_ref[2]], axis=0)
    query_ref[...], key_ref[...], value_ref[...] = attend_grad(
        grad, first_ref[0], keys, values, logs_ref
    )


def project_back(rows_ref, start, count, w_ref):
    total = dot(rows_ref[0, start : start + count], w_ref[0], 1, 1)
    for i in range(1, 3):
        total = total + dot(rows_ref[i, start : start + count], w_ref[i], 1, 1)
    return total


def attend_back_second(
    own_ref,
    near_ref,
    w_out_ref,
    first_ref,
    second_ref,
    logs_ref,
    query_ref,
    key_ref,
    value_ref,
    w_ref,
    out_ref,
    keep_ref,
    send_ref,
):
    rows = jnp.concatenate([own_ref[...], near_ref[...]], axis=0)
    half = rows.shape[0]
    grad = dot(rows, w_out_ref[...], 1, 1).astype(BF16)
    keys = jnp.concatenate([first_ref[1], second_ref[1]], axis=0)
    values = jnp.concatenate([first_ref[2], second_ref[2]], axis=0)
    query_grad, key_grad, value_grad = attend_grad(grad, second_ref[0], keys, values, logs_ref)
    out_ref[0, 0:half] = query_ref[...]
    out_ref[0, half:] = query_grad
    out_ref[1] = (key_ref[...] + key_grad).astype(BF16)
    out_ref[2] = (value_ref[...] + value_grad).astype(BF16)
    split_out(project_back(out_ref, 0, half, w_ref), keep_ref, send_ref)


def attend_back_last(rows_ref, w_ref, keep_ref, send_ref):
    half = rows_ref.shape[1] // 2
    split_out(project_back(rows_ref, half, half, w_ref), keep_ref, send_ref)


def hidden_back(own_ref, near_ref, w_ref, out_ref):
    rows = jnp.concatenate([own_ref[...], near_ref[...]], axis=0)
    out_ref[...] = dot(rows, w_ref[...], 1, 1)


ROOT = 0.7978845608028654
CUBE = 0.044715


def mlp(own_ref, near_ref, w_ref, grad_ref, hidden_ref, out_ref, keep_ref, send_ref):
    rows = jnp.concatenate([own_ref[...], near_ref[...]], axis=0)
    pre = dot(rows, w_ref[...])
    square = pre * pre
    bend = jnp.tanh(ROOT * pre * (1.0 + CUBE * square))
    half = 0.5 * (1.0 + bend)
    hidden_ref[...] = (pre * half).astype(BF16)
    slope = half + (0.5 * ROOT) * pre * (1.0 - bend * bend) * (1.0 + (3.0 * CUBE) * square)
    out_ref[...] = (slope * grad_ref[...]).astype(BF16)
    split_out(dot(out_ref[...], w_ref[...], 1, 1), keep_ref, send_ref)


def mlp_out(first_ref, second_ref, w_ref, keep_a_ref, send_a_ref, keep_b_ref, send_b_ref):
    split_out(dot(first_ref[...], w_ref[...]), keep_a_ref, send_a_ref)
    split_out(dot(second_ref[...], w_ref[...]), keep_b_ref, send_b_ref)


def grad_rows(parts, step, width, which):
    groups = width // (2 * step)
    outs = []
    for group in range(groups):
        start = pl.multiple_of((2 * group + which) * step, LANES)
        line = []
        for left, rights in parts:
            picked = jnp.concatenate([ref[:, pl.ds(start, step)] for ref in left], axis=0)
            line.extend(dot(picked, right, 0, 0) for right in rights)
        outs.append(line)
    return outs, groups


def write_half(ref, parts, step, width, which, dtype):
    outs, groups = grad_rows(parts, step, width, which)
    for group in range(groups):
        column = 0
        for value in outs[group]:
            ref[group * step : (group + 1) * step, column : column + value.shape[1]] = value.astype(dtype)
            column += value.shape[1]


def take_half(out_ref, source, step, which, dtype):
    for group in range(source.shape[0] // (2 * step)):
        start = pl.multiple_of((2 * group + which) * step, 16)
        out_ref[group * step : (group + 1) * step] = source[pl.ds(start, step)].astype(dtype)


def sum_start(load, step, bit, *refs):
    *inputs, out_ref = refs
    parts, width = load(inputs)
    write_half(out_ref, parts, step, width, 1 - my_bit(bit), BF16)


def sum_second(load, step, next_step, bit, next_bit, *refs):
    got_ref, *inputs, keep_ref, send_ref, total = refs
    parts, width = load(inputs)
    write_half(total, parts, step, width, my_bit(bit), F32)
    total[...] = total[...] + got_ref[...].astype(F32)
    take_half(send_ref, total, next_step, 1 - my_bit(next_bit), BF16)
    take_half(keep_ref, total, next_step, my_bit(next_bit), F32)


def sum_next(next_step, next_bit, kept_ref, got_ref, keep_ref, send_ref, total):
    total[...] = kept_ref[...] + got_ref[...].astype(F32)
    take_half(send_ref, total, next_step, 1 - my_bit(next_bit), BF16)
    take_half(keep_ref, total, next_step, my_bit(next_bit), F32)


def load_plain(inputs):
    *left, first, second = inputs
    right = jnp.concatenate([first[...], second[...]], axis=0)
    return [(left, [right])], left[0].shape[1]


def load_attn(inputs):
    left, middle = inputs[0:4], inputs[4:8]
    proj, first, second = inputs[8:]
    attended = jnp.concatenate([first[...], second[...]], axis=0)
    return [(left, [proj[0], proj[1], proj[2]]), (middle, [attended])], left[0].shape[1]


def last_plain(kept_ref, got_ref, out_ref):
    out_ref[...] = kept_ref[...] + got_ref[...].astype(F32)


def last_turned(kept_ref, got_ref, out_ref):
    out_ref[...] = (kept_ref[...] + got_ref[...].astype(F32)).T


def last_attn(kept_ref, got_ref, proj_ref, out_ref):
    total = kept_ref[...] + got_ref[...].astype(F32)
    width = proj_ref.shape[2]
    for i in range(3):
        proj_ref[i] = total[:, i * width : (i + 1) * width]
    out_ref[...] = total[:, 3 * width :].T


def mix_lines(samples, lines, bucket_ref, inputs, rest_ref):
    first_ref, second_ref, own_ref, near_ref = inputs
    quarter, width = first_ref.shape
    rest_ref[0:quarter] = jnp.where(my_chip() == 0, first_ref[...], second_ref[...])
    sample = lax.axis_index("dp")
    sums = own_ref[...] + near_ref[...]
    row = iota((lines, width), 0)
    filled = jnp.concatenate([sums, jnp.zeros((lines - 8, width), F32)], axis=0)
    filled = jnp.where(row < 4, filled, 0.0)
    filled = jnp.where(row == 4 + sample, sums[4:5], filled)
    bucket = bucket_ref[0].astype(F32)
    rest_ref[quarter:] = jnp.where(row == 4 + samples + sample, bucket, filled)


def write_mix(ref, step, which, inputs, rest_ref, dtype):
    left, mixed_ref = inputs[0:4], inputs[4]
    width = left[0].shape[1]
    heads_width = mixed_ref.shape[0]
    for group in range(width // (2 * step)):
        start = pl.multiple_of((2 * group + which) * step, LANES)
        picked = jnp.concatenate([part[:, pl.ds(start, step)] for part in left], axis=0)
        rows = slice(group * step, (group + 1) * step)
        ref[rows, 0:heads_width] = dot(picked, mixed_ref[...], 0, 1).astype(dtype)
        ref[rows, heads_width:] = rest_ref[:, pl.ds(start, step)].T.astype(dtype)


def mix_start(samples, lines, step, bit, bucket_ref, *refs):
    *inputs, out_ref, rest = refs
    mix_lines(samples, lines, bucket_ref, inputs[5:], rest)
    write_mix(out_ref, step, 1 - my_bit(bit), inputs, rest, BF16)


def mix_second(samples, lines, step, next_step, bit, next_bit, bucket_ref, *refs):
    got_ref, *inputs, keep_ref, send_ref, rest, total = refs
    mix_lines(samples, lines, bucket_ref, inputs[5:], rest)
    write_mix(total, step, my_bit(bit), inputs, rest, F32)
    total[...] = total[...] + got_ref[...].astype(F32)
    take_half(send_ref, total, next_step, 1 - my_bit(next_bit), BF16)
    take_half(keep_ref, total, next_step, my_bit(next_bit), F32)


def mix_last(samples, quarter, final, kept_ref, got_ref, out_ref, pos_ref, lead_ref, small_ref):
    total = kept_ref[...] + got_ref[...].astype(F32)
    heads_width = out_ref.shape[0]
    out_ref[...] = total[:, :heads_width].T
    pos_ref[...] = total[:, heads_width : heads_width + quarter].T
    rest = total[:, heads_width + quarter :]
    rows = max(final, 8)
    mine = iota((rows, rest.shape[0]), 1) == iota((rows, rest.shape[0]), 0) + lax.axis_index("mp") * final
    own = dot(mine.astype(F32), rest, precision=HIGH)
    bucket = iota((rows, lead_ref.shape[1]), 1).astype(F32)
    lead = jnp.zeros(bucket.shape, F32)
    for s in range(samples):
        mark = own[:, 4 + samples + s : 5 + samples + s]
        lead = jnp.where(bucket == mark, lead + own[:, 4 + s : 5 + s], lead)
    lead_ref[...] = lead[:final]
    small_ref[...] = own.T[0:8, :final]


def mass_add(mass_ref, got_ref, bias_ref, bias_got_ref, out_ref, low_ref, bias_out_ref):
    total = mass_ref[...] + got_ref[...].astype(F32)
    out_ref[...] = total
    low_ref[...] = total.astype(BF16)
    bias_out_ref[...] = bias_ref[...] + bias_got_ref[...]


def mix_finish(
    mass_ref,
    got_ref,
    bias_ref,
    bias_got_ref,
    query_col_ref,
    keys_t_ref,
    table_ref,
    w_ref,
    query_ref,
    grad_ref,
    keep_ref,
    send_ref,
    scratch,
):
    width, rows = mass_ref.shape
    heads = width // HEAD_DIM
    mass = (mass_ref[...] + got_ref[...].astype(F32)).astype(BF16)
    sums = bias_ref[...] + bias_got_ref[...]
    bias = jnp.concatenate(
        [jnp.broadcast_to(sums[head : head + 1], (HEAD_DIM, rows)) for head in range(heads)], axis=0
    )
    key_mass = (bias * query_col_ref[:, 0:1]).astype(BF16)
    total = jnp.sum(keys_t_ref[...] * bias, axis=1, keepdims=True)
    own = grad_ref.shape[1]
    start = lax.axis_index("dp") * own
    model_width = table_ref.shape[1]
    mine = exact(iota((own, model_width), 1) == iota((own, model_width), 0) + start)
    total_row = jnp.broadcast_to(total, (width, LANES)).T[0:1]
    table_t = dot(mine, table_ref[...], 1, 1).astype(BF16)
    query_rows = jnp.broadcast_to(query_ref[...].astype(F32)[None], (16, model_width)).astype(BF16)
    grad_ref[0] = dot(mine, query_rows, 1, 1)[:, 0:1] * total_row
    grad_ref[1] = dot(table_t, key_mass, 1, 1)
    grad_ref[2] = dot(table_t, mass, 1, 1)
    back = dot(w_ref[1], key_mass) + dot(w_ref[2], mass)
    query_back = jnp.sum(w_ref[0].astype(F32) * total_row, axis=1, keepdims=True)
    scratch[...] = jnp.where(iota((own, rows), 1) == rows - 1, query_back, back)
    keep_part(scratch, keep_ref, send_ref, my_chip())


def keep_part(source, keep_ref, send_ref, which):
    step = keep_ref.shape[0]
    if step % 8:
        first, second = source[0:step], source[step : 2 * step]
        keep_ref[...] = jnp.where(which == 0, first, second)
        send_ref[...] = jnp.where(which == 0, second, first)
    else:
        keep_ref[...] = source[pl.ds(pl.multiple_of(which * step, 8), step)]
        send_ref[...] = source[pl.ds(pl.multiple_of((1 - which) * step, 8), step)]


def tables_next(kept_ref, got_ref, keep_ref, send_ref, scratch):
    scratch[...] = kept_ref[...] + got_ref[...]
    keep_part(scratch, keep_ref, send_ref, my_core())


def pair_sum(keep_ref, got_ref, out_ref, low_ref):
    total = keep_ref[...] + got_ref[...].astype(F32)
    out_ref[...] = total
    low_ref[...] = total.astype(BF16)


def by_chip(own_ref, far_ref, first_ref, second_ref):
    own, far = own_ref[...], far_ref[...]
    first = my_chip() == 0
    first_ref[...] = jnp.where(first, own, far)
    second_ref[...] = jnp.where(first, far, own)


def base_rows(bucket_ref, first_ref, second_ref, lead_ref, out_a_ref, out_b_ref):
    rows = lead_ref.shape[0]
    mark = exact(iota((16, rows), 1) == bucket_ref[0])
    lead = dot(mark, lead_ref[...])[0:1]
    out_a_ref[...] = first_ref[...].astype(F32) + lead
    out_b_ref[...] = second_ref[...].astype(F32) + lead


def field_sum(keep_ref, got_ref, own_ref, send_ref):
    total = keep_ref[...] + got_ref[...].astype(F32)
    quarter = own_ref.shape[1]
    first = my_chip() == 0
    own_ref[...] = jnp.where(first, total[:, :quarter], total[:, quarter:])
    send_ref[...] = jnp.where(first, total[:, quarter:], total[:, :quarter]).astype(BF16)


def field_last(own_ref, far_ref, out_ref):
    out_ref[0] = own_ref[...] + far_ref[...].astype(F32)


def rows_sum(keep_a_ref, got_a_ref, keep_b_ref, got_b_ref, mid_a_ref, mid_b_ref, own_ref, send_ref):
    part_a = keep_a_ref[...] + got_a_ref[...].astype(F32)
    part_b = keep_b_ref[...] + got_b_ref[...].astype(F32)
    first = my_chip() == 0
    own_ref[...] = jnp.where(first, part_a + mid_a_ref[...], part_b + mid_b_ref[...])
    send_ref[...] = jnp.where(first, part_b, part_a).astype(BF16)


def tables_last(pixels, variables, kept_ref, got_ref, patch_ref, variable_ref, query_ref):
    total = kept_ref[...] + got_ref[...]
    for p in range(pixels):
        patch_ref[p] = total[:, p * variables : (p + 1) * variables]
    variable_ref[...] = total[:, pixels * variables : (pixels + 1) * variables]
    query_ref[...] = total.T[total.shape[1] - 8 :]


def pairs(count, bit):
    return [(i, i ^ bit) for i in range(count)]


def body(
    mesh_dp,
    mesh_mp,
    input_field,
    variable_ids,
    lead_bucket,
    patch_table,
    variable_table,
    variable_query,
    mix_weights,
    mix_output,
    pos_table,
    lead_table,
    first_gain,
    first_bias,
    attn_weights,
    attn_output,
    second_gain,
    second_bias,
    up_weight,
    down_weight,
    cotangent,
):
    length = input_field.shape[2]
    channels = input_field.shape[1]
    variables = variable_ids.shape[0]
    pixels = channels // variables
    model_width = pos_table.shape[1]
    quarter = cotangent.shape[0]
    head_width = mix_weights.shape[2]
    hidden_width = up_weight.shape[1]
    heads = head_width // HEAD_DIM
    own_width = model_width // mesh_dp
    half = 2 * quarter
    rows32 = ((quarter, model_width), F32)
    rows16 = ((quarter, model_width), BF16)

    def swap_core(value):
        return lax.ppermute(value, "mp", pairs(mesh_mp, 1))

    def swap_chip(value):
        return lax.ppermute(value, "mp", pairs(mesh_mp, 2))

    def add_core(keep, send):
        kept, low = call(pair_sum, [rows32, rows16], [keep, swap_core(send)], cost=0.3)
        return kept, swap_chip(low)

    def swap_sample(value, bit):
        return lax.ppermute(value, "dp", pairs(mesh_dp, bit))

    all_bits = [1 << i for i in range(mesh_dp.bit_length() - 1)]
    wide = [bit for bit in all_bits if bit * own_width % LANES == 0]

    def order_from(which):
        first = all_bits.index(wide[which % len(wide)])
        return all_bits[first:] + all_bits[:first]

    def steps_of(order):
        left = list(all_bits)
        steps = []
        for bit in order:
            steps.append(own_width << left.index(bit))
            left.remove(bit)
        return steps

    def start_sum(load, inputs, width, order, after=()):
        step = steps_of(order)[0]
        (send,) = call(
            functools.partial(sum_start, load, step, order[0]),
            [((model_width // 2, width), BF16)],
            inputs,
            after=after,
        )
        return send, swap_sample(send, order[0])

    def halves(width, scratch_rows):
        kept = scratch_rows // 2
        return [((kept, width), F32), ((kept, width), BF16)]

    def second_sum(load, inputs, got, width, order, after=()):
        steps = steps_of(order)
        rows = model_width // 2
        keep, send = call(
            functools.partial(sum_second, load, steps[0], steps[1], order[0], order[1]),
            halves(width, rows),
            [got] + inputs,
            after=after,
            scratch=[pltpu.VMEM((rows, width), F32)],
        )
        return keep, swap_sample(send, order[1])

    def rest_sum(keep, got, order):
        steps = steps_of(order)
        for i in range(2, len(order)):
            rows, width = keep.shape
            keep, send = call(
                functools.partial(sum_next, steps[i], order[i]),
                halves(width, rows),
                [keep, got],
                scratch=[pltpu.VMEM((rows, width), F32)],
            )
            got = swap_sample(send, order[i])
        return keep, got

    cot_a0, cot_b0 = call(by_chip, [rows16] * 2, [cotangent, swap_chip(cotangent)], cost=0.3)
    cot_a1 = swap_core(cot_a0)
    cot_b1 = swap_core(cot_b0)

    w_mix = mix_weights.transpose(1, 0, 2)
    w_attn = attn_weights.transpose(1, 0, 2)
    gain_one, bias_one = first_gain[None], first_bias[None]
    gain_two, bias_two = second_gain[None], second_bias[None]
    table_rows = channels + variables
    padded = -(-(table_rows + 1) // LANES) * LANES
    (
        table,
        pick,
        field_t,
        probs,
        values,
        keys_t,
        score,
        query_col,
        mixed_t,
        send_a,
        send_b,
        keep_a,
        keep_b,
    ) = call(
        functools.partial(mix_forward, pixels, quarter),
        [
            ((padded, model_width), BF16),
            ((channels, channels), BF16),
            ((channels, length), BF16),
            ((heads * variables, length), F32),
            ((padded, head_width), BF16),
            ((head_width, padded), F32),
            ((padded, LANES), F32),
            ((head_width, LANES), F32),
            ((head_width, length), BF16),
            rows16,
            rows16,
            rows32,
            rows32,
        ],
        [variable_query],
        fetch=[input_field, patch_table, variable_table, w_mix, mix_output],
        smem=[variable_ids],
    )
    blocks = [
        (pos_table, (quarter, model_width), lambda ref, k=k: ref.at[pl.ds((2 * k + my_core()) * quarter, quarter)])
        for k in range(2)
    ]
    base_a, base_b = call(
        base_rows, [rows32] * 2, [], fetch=blocks + [lead_table], smem=[lead_bucket], cost=0.3
    )
    kept_a, far_a = add_core(keep_a, send_a)
    kept_b, far_b = add_core(keep_b, send_b)

    def norm_rows(terms, gain, bias, after=()):
        return call(norm_forward, [rows32, rows16], terms + [gain, bias], after=after, cost=0.5)

    in_a, one_a0 = norm_rows([kept_a, far_a, base_a], gain_one, bias_one)
    one_a1 = swap_core(one_a0)
    proj_kind = ((3, half, head_width), BF16)
    (proj_a,) = call(project, [proj_kind], [one_a0, one_a1, w_attn])
    (grad_hidden_a,) = call(hidden_back, [((half, hidden_width), F32)], [cot_a0, cot_a1, down_weight])
    (grad_hidden_b,) = call(hidden_back, [((half, hidden_width), F32)], [cot_b0, cot_b1, down_weight])
    in_b, one_b0 = norm_rows(
        [kept_b, far_b, base_b], gain_one, bias_one, after=[grad_hidden_a, grad_hidden_b]
    )
    one_b1 = swap_core(one_b0)
    attend_kinds = [((half, head_width), BF16), ((8, half), F32), rows32, rows16]
    proj_b, attended_a, logs_a, keep_a, send_a = call(
        attend_first,
        [proj_kind] + attend_kinds,
        [one_b0, one_b1, w_attn, proj_a, attn_output],
    )
    attended_b, logs_b, keep_b, send_b = call(
        attend_second, attend_kinds, [proj_a, proj_b, attn_output]
    )
    kept_a, far_a = add_core(keep_a, send_a)
    kept_b, far_b = add_core(keep_b, send_b)
    mid_a, two_a0 = norm_rows([kept_a, far_a, in_a], gain_two, bias_two)
    two_a1 = swap_core(two_a0)
    mlp_kinds = [((half, hidden_width), BF16)] * 2 + [rows32, rows16]
    hidden_a, pre_a, keep_a, send_a = call(mlp, mlp_kinds, [two_a0, two_a1, up_weight, grad_hidden_a])
    kept_a, far_a = add_core(keep_a, send_a)
    mid_b, two_b0 = norm_rows([kept_b, far_b, in_b], gain_two, bias_two)
    two_b1 = swap_core(two_b0)
    hidden_b, pre_b, keep_b, send_b = call(mlp, mlp_kinds, [two_b0, two_b1, up_weight, grad_hidden_b])
    kept_b, far_b = add_core(keep_b, send_b)

    down_order, up_order, attn_order, mix_order = (order_from(i) for i in (1, 0, 0, 0))
    down_in = [cot_a0, cot_a1, cot_b0, cot_b1, hidden_a, hidden_b]
    up_in = [two_a0, two_a1, two_b0, two_b1, pre_a, pre_b]
    down_send, down_got = start_sum(load_plain, down_in, hidden_width, down_order)
    up_send, up_got = start_sum(load_plain, up_in, hidden_width, up_order)

    sums_kind = ((8, model_width), F32)
    back_kinds = [rows32, rows16, sums_kind]
    back_two = functools.partial(norm_backward, False, 0)
    grad_mid_a, mid_a0, sums_two_a = call(
        back_two,
        back_kinds,
        [kept_a, far_a, mid_a, gain_two, cot_a0],
        after=[down_send, up_send],
        cost=0.5,
    )
    mid_a1 = swap_core(mid_a0)
    grad_kinds = [((half, head_width), BF16)] + [((length, head_width), F32)] * 2
    query_grad, key_grad, value_grad = call(
        attend_back_first, grad_kinds, [mid_a0, mid_a1, attn_output, proj_a, proj_b, logs_a]
    )
    grad_mid_b, mid_b0, sums_two_b = call(
        back_two, back_kinds, [kept_b, far_b, mid_b, gain_two, cot_b0], cost=0.5
    )
    mid_b1 = swap_core(mid_b0)
    grad_proj, keep_a, send_a = call(
        attend_back_second,
        [((3, length, head_width), BF16), rows32, rows16],
        [
            mid_b0,
            mid_b1,
            attn_output,
            proj_a,
            proj_b,
            logs_b,
            query_grad,
            key_grad,
            value_grad,
            w_attn,
        ],
    )
    kept_a, far_a = add_core(keep_a, send_a)
    keep_b, send_b = call(attend_back_last, [rows32, rows16], [grad_proj, w_attn])
    kept_b, far_b = add_core(keep_b, send_b)

    attn_in = [one_a0, one_a1, one_b0, one_b1, mid_a0, mid_a1, mid_b0, mid_b1, grad_proj, attended_a, attended_b]
    attn_width = 4 * head_width
    attn_send, attn_got = start_sum(load_attn, attn_in, attn_width, attn_order)
    down_keep, down_got = second_sum(load_plain, down_in, down_got, hidden_width, down_order)
    up_keep, up_got = second_sum(load_plain, up_in, up_got, hidden_width, up_order)

    grad_in_a, in_a0, sums_one_a = call(
        functools.partial(norm_backward, True, 0),
        back_kinds,
        [kept_a, far_a, in_a, gain_one, grad_mid_a],
        after=[attn_send, down_keep, up_keep],
        cost=0.5,
    )
    in_a1 = swap_core(in_a0)
    grad_in_b, in_b0, sums = call(
        functools.partial(norm_backward, True, 3),
        back_kinds,
        [kept_b, far_b, in_b, gain_one, grad_mid_b, sums_one_a, sums_two_a, sums_two_b],
        cost=0.5,
    )
    in_b1 = swap_core(in_b0)
    near_sums = swap_core(sums)
    mass, mass_low, bias, field_send, field_keep = call(
        functools.partial(mix_backward, pixels),
        [
            ((head_width, padded), F32),
            ((head_width, padded), BF16),
            ((8, padded), F32),
            ((channels, half), BF16),
            ((channels, half), F32),
        ],
        [pick, field_t, probs, values, score, mix_output, in_a0, in_a1, in_b0, in_b1],
    )
    mass_kinds = [
        ((head_width, padded), F32),
        ((head_width, padded), BF16),
        ((8, padded), F32),
    ]
    for bit in all_bits[:-1]:
        mass, mass_low, bias = call(
            mass_add,
            mass_kinds,
            [mass, swap_sample(mass_low, bit), bias, swap_sample(bias, bit)],
            cost=0.3,
        )
    mass_got = swap_sample(mass_low, all_bits[-1])
    bias_got = swap_sample(bias, all_bits[-1])

    (own_weights,) = call(
        lambda source, out: out.__setitem__(Ellipsis, source[...]),
        [((3, own_width, head_width), BF16)],
        [],
        fetch=[
            (
                w_mix,
                (3, own_width, head_width),
                lambda ref: ref.at[:, pl.ds(lax.axis_index("dp") * own_width, own_width)],
            )
        ],
        cost=0.1,
    )
    lines = -(-(4 + 2 * mesh_dp) // LANES) * LANES
    mix_in = [in_a0, in_a1, in_b0, in_b1, mixed_t, grad_in_a, grad_in_b, sums, near_sums]
    mix_width = head_width + quarter + lines
    steps = steps_of(mix_order)
    rest = pltpu.VMEM((quarter + lines, model_width), F32)
    (send,) = call(
        functools.partial(mix_start, mesh_dp, lines, steps[0], mix_order[0]),
        [((model_width // 2, mix_width), BF16)],
        mix_in,
        smem=[lead_bucket],
        scratch=[rest],
    )
    got = swap_sample(send, mix_order[0])
    mix_keep, send = call(
        functools.partial(mix_second, mesh_dp, lines, steps[0], steps[1], mix_order[0], mix_order[1]),
        halves(mix_width, model_width // 2),
        [got] + mix_in,
        smem=[lead_bucket],
        scratch=[rest, pltpu.VMEM((model_width // 2, mix_width), F32)],
    )
    mix_keep, mix_got = rest_sum(mix_keep, swap_sample(send, mix_order[1]), mix_order)

    own_field = (channels, quarter)
    field_own, field_far = call(
        field_sum, [(own_field, F32), (own_field, BF16)], [field_keep, swap_core(field_send)], cost=0.3
    )
    (field_grad,) = call(
        field_last, [((1,) + own_field, F32)], [field_own, swap_chip(field_far)], cost=0.3
    )

    attn_keep, attn_got = second_sum(load_attn, attn_in, attn_got, attn_width, attn_order)
    down_keep, down_got = rest_sum(down_keep, down_got, down_order)
    up_keep, up_got = rest_sum(up_keep, up_got, up_order)
    attn_keep, attn_got = rest_sum(attn_keep, attn_got, attn_order)

    keep_a, send_a, keep_b, send_b = call(
        mlp_out, [rows32, rows16] * 2, [hidden_a, hidden_b, down_weight], after=[in_b0]
    )
    rows_own, rows_far = call(
        rows_sum,
        [rows32, rows16],
        [keep_a, swap_core(send_a), keep_b, swap_core(send_b), mid_a, mid_b],
        cost=0.3,
    )
    (activations,) = call(last_plain, [rows32], [rows_own, swap_chip(rows_far)], cost=0.3)

    final = own_width // mesh_mp
    grad_mix, keep, send = call(
        mix_finish,
        [((3, own_width, head_width), F32)] + [((own_width // 2, padded), F32)] * 2,
        [mass, mass_got, bias, bias_got, query_col, keys_t, table, own_weights, variable_query],
        scratch=[pltpu.VMEM((own_width, padded), F32)],
    )
    keep, send = call(
        tables_next,
        [((final, padded), F32)] * 2,
        [keep, swap_chip(send)],
        scratch=[pltpu.VMEM((own_width // 2, padded), F32)],
        cost=0.3,
    )
    patch_total, variable_total, query_total = call(
        functools.partial(tables_last, pixels, variables),
        [((pixels, final, variables), F32), ((final, variables), F32), ((8, final), F32)],
        [keep, swap_core(send)],
    )
    (down_sum,) = call(last_turned, [((hidden_width, own_width), F32)], [down_keep, down_got])
    (up_sum,) = call(last_plain, [((own_width, hidden_width), F32)], [up_keep, up_got])
    attn_sum, attn_out_sum = call(
        last_attn,
        [((3, own_width, head_width), F32), ((head_width, own_width), F32)],
        [attn_keep, attn_got],
    )
    mix_out_sum, pos_sum, lead_total, small = call(
        functools.partial(mix_last, mesh_dp, quarter, final),
        [
            ((head_width, own_width), F32),
            ((quarter, own_width), F32),
            ((final, lead_table.shape[0]), F32),
            ((8, final), F32),
        ],
        [mix_keep, mix_got],
    )
    return (
        activations,
        field_grad,
        patch_total.transpose(2, 0, 1),
        variable_total.T,
        query_total[7],
        grad_mix.transpose(1, 0, 2),
        mix_out_sum,
        pos_sum,
        lead_total.T,
        small[0],
        small[1],
        attn_sum.transpose(1, 0, 2),
        attn_out_sum,
        small[2],
        small[3],
        up_sum,
        down_sum,
    )


def solution(mesh):
    in_specs = (
        P("dp", None, None),
        P(),
        P("dp"),
        P(),
        P(),
        P(),
        P(None, None, "mp"),
        P("mp", None),
        P(),
        P(),
        P(),
        P(),
        P(None, None, "mp"),
        P("mp", None),
        P(),
        P(),
        P(None, "mp"),
        P("mp", None),
        P(("dp", "mp"), None),
    )
    out_specs = (
        P(("dp", "mp"), None),
        P("dp", None, "mp"),
        P(None, None, ("dp", "mp")),
        P(None, ("dp", "mp")),
        P(("dp", "mp")),
        P("dp", None, "mp"),
        P("mp", "dp"),
        P("mp", "dp"),
        P(None, ("dp", "mp")),
        P(("dp", "mp")),
        P(("dp", "mp")),
        P("dp", None, "mp"),
        P("mp", "dp"),
        P(("dp", "mp")),
        P(("dp", "mp")),
        P("dp", "mp"),
        P("mp", "dp"),
    )
    step = functools.partial(body, mesh.shape["dp"], mesh.shape["mp"])
    return jax.shard_map(step, mesh=mesh, in_specs=in_specs, out_specs=out_specs, check_vma=False)
```

```python
import functools
import types

import jax
import jax.numpy as jnp
from jax import lax
from jax.experimental import pallas as pl
from jax.experimental.pallas import tpu as pltpu
from jax.sharding import PartitionSpec as P

HEAD_DIM = 64
LANES = 128
EPS = 1e-05
SCALE = HEAD_DIM ** (-0.5)
HIGH = lax.Precision.HIGHEST
F32 = jnp.float32
BF16 = jnp.bfloat16
VMEM = pl.BlockSpec(memory_space=pltpu.VMEM)
SMEM = pl.BlockSpec(memory_space=pltpu.SMEM)
ANY = pl.BlockSpec(memory_space=pl.ANY)
HBM = pl.BlockSpec(memory_space=pltpu.HBM)
MIB = 1024 * 1024
FIRST_LIMIT = 60
PIECES = 2
AXES = ((0, 1, 2), (1, 2, 0), (0, 1, 2), (0, 1, 2), (1, 0, 2))
ORDER = (
    "mix_a", "mix_b", "first_a", "first_b", "base", "norm_a", "proj", "norm_b", "attend_a", "second_a", "cot",
    "attend_b", "hidden_a", "second_b", "two_a", "mlp_a", "hidden_b", "two_b", "third_a", "mlp_b", "down_1",
    "up_1", "third_b", "mid_a", "back_a", "mid_b", "back_b", "attn_1", "back_c", "fourth_a", "down_2",
    "weights", "fourth_b", "up_2", "in_a", "in_b", "mass_1", "down_3", "mix_1", "field_1", "attn_2", "mass_2",
    "up_3", "mass_3", "rows_1", "down_4", "up_4", "rows_2", "mix_2", "attn_3", "finish", "tables_1", "mix_3",
    "attn_4", "rows_3", "field_2", "tables_2", "mix_4",
)
COSTS = {
    "two_a": 1,
    "two_b": 0.3,
    "mlp_b": 12,
    "mid_a": 1,
    "up_2": 1,
    "in_a": 1,
    "down_3": 2,
    "up_3": 1,
    "tables_1": 1,
}


def dot(left, right, left_dim=1, right_dim=0, precision=None):
    return lax.dot_general(
        left,
        right,
        (((left_dim,), (right_dim,)), ((), ())),
        precision=precision,
        preferred_element_type=F32,
    )


class Rows:
    def __init__(self, refs):
        self.refs = refs
        self.shape = (sum(ref.shape[0] for ref in refs),) + refs[0].shape[1:]

    def __getitem__(self, at):
        return jnp.concatenate([ref[at] for ref in self.refs], axis=0)

    def __setitem__(self, at, value):
        step = self.refs[0].shape[0]
        for i, ref in enumerate(self.refs):
            ref[...] = value[i * step : (i + 1) * step]


def gather_refs(refs, counts):
    refs, grouped = list(refs), []
    for count in counts:
        grouped.append(refs.pop(0) if count is None else Rows([refs.pop(0) for _ in range(count)]))
    return grouped


def flat(items):
    out, counts = [], []
    for item in items:
        pieces = isinstance(item, list)
        out.extend(item if pieces else [item])
        counts.append(len(item) if pieces else None)
    return out, counts


def launch(kernel, outs, args, fetch=(), smem=(), after=(), limit=24, scratch=(), cost=0.1, name=None):
    fetch = [item if isinstance(item, tuple) else (item, item.shape, None) for item in fetch]
    args, arg_counts = flat(args)
    outs, out_counts = flat(outs)
    count = len(smem)

    def run(*refs):
        at = count + len(fetch)
        sources, rest = refs[count:at], refs[at:]
        inputs, rest = gather_refs(rest[: len(args)], arg_counts), rest[len(args) + len(after) :]
        results, rest = gather_refs(rest[: len(outs)], out_counts), rest[len(outs) :]
        if not fetch:
            kernel(*refs[:count], *inputs, *results, *rest)
            return
        *rest, marks = rest
        rest, places = rest[: len(rest) - len(fetch)], rest[len(rest) - len(fetch) :]
        copies = []
        for i, (_, _, pick) in enumerate(fetch):
            source = sources[i] if pick is None else pick(sources[i])
            copies.append(pltpu.make_async_copy(source, places[i], marks.at[i]))
        for copy in copies:
            copy.start()
        for copy in copies:
            copy.wait()
        kernel(*refs[:count], *places, *inputs, *results, *rest)

    places = [pltpu.VMEM(shape, array.dtype) for array, shape, _ in fetch]
    marks = [pltpu.SemaphoreType.DMA((len(fetch),))] if fetch else []
    results = pl.pallas_call(
        run,
        out_shape=[jax.ShapeDtypeStruct(shape, kind) for shape, kind in outs],
        in_specs=[SMEM] * count + [HBM] * len(fetch) + [VMEM] * len(args) + [ANY] * len(after),
        out_specs=[VMEM] * len(outs),
        scratch_shapes=list(scratch) + places + marks,
        name=name,
        compiler_params=pltpu.CompilerParams(vmem_limit_bytes=limit * MIB),
        cost_estimate=pl.CostEstimate(
            flops=int(cost * 1e9), bytes_accessed=0, transcendentals=0
        ),
    )(*smem, *(array for array, _, _ in fetch), *args, *after)
    results, grouped = list(results), []
    for pieces in out_counts:
        grouped.append(results.pop(0) if pieces is None else [results.pop(0) for _ in range(pieces)])
    return grouped


def marked(kernel, *refs):
    *rest, mark_ref = refs
    mark_ref[...] = jnp.zeros_like(mark_ref)
    kernel(*rest)


def my_bit(bit):
    return (lax.axis_index("dp") // bit) % 2


def my_core():
    return lax.axis_index("mp") % 2


def my_chip():
    return lax.axis_index("mp") // 2


def iota(shape, dim):
    return lax.broadcasted_iota(jnp.int32, shape, dim)


def exact(mask):
    return mask.astype(F32).astype(BF16)


def lanes_of(rows, head):
    lane = iota((1, rows.shape[1]), 1)
    mine = (lane >= head * HEAD_DIM) & (lane < (head + 1) * HEAD_DIM)
    return jnp.where(mine, rows, jnp.zeros_like(rows))


def spread(rows, pixels, top, bottom):
    variables = top.shape[0]
    parts = [top * rows[p * variables : (p + 1) * variables] for p in range(pixels)]
    parts.append(top)
    if bottom:
        parts.append(jnp.zeros((bottom, top.shape[1]), top.dtype))
    return jnp.concatenate(parts, axis=0)


def pixel_major(channels, pixels):
    variables = channels // pixels
    row = iota((channels, channels), 0)
    major = jnp.zeros((channels, channels), jnp.int32)
    for p in range(pixels):
        inside = (row >= p * variables) & (row < (p + 1) * variables)
        major = jnp.where(inside, (row - p * variables) * pixels + p, major)
    return exact(iota((channels, channels), 1) == major)


def places(ids_ref, variables, pixels):
    channels = variables * pixels
    channel = iota((1, channels), 1)
    place = jnp.zeros((1, channels), jnp.int32)
    for v in range(variables):
        pixel = channel - v * pixels
        inside = (pixel >= 0) & (pixel < pixels)
        place = jnp.where(inside, pixel * variables + ids_ref[v], place)
    return place


def mix_forward(
    pixels,
    quarter,
    ids_ref,
    x_ref,
    patch_ref,
    variable_ref,
    w_ref,
    query_ref,
    mixed_ref,
    xt_ref,
    probs_ref,
    values_ref,
    keys_t_ref,
    score_ref,
    query_col_ref,
    table_ref,
):
    channels = x_ref.shape[1]
    variables = channels // pixels
    rows, model_width = table_ref.shape
    width = w_ref.shape[2]
    heads = width // HEAD_DIM
    bottom = rows - channels - variables
    flat = patch_ref[...].reshape(channels, model_width)
    table_ref[0:channels] = dot(pixel_major(channels, pixels), flat).astype(BF16)
    table_ref[channels : channels + variables] = variable_ref[...]
    if bottom:
        table_ref[channels + variables :] = jnp.zeros((bottom, model_width), BF16)
    pick = (iota((channels, channels), 0) == places(ids_ref, variables, pixels)).astype(F32)
    core = my_core()
    starts = [core, 1 - core, core + 2, 3 - core]
    field = jnp.concatenate(
        [x_ref[0, :, pl.ds(pl.multiple_of(s * quarter, LANES), quarter)] for s in starts], axis=1
    )
    xt = dot(pick.astype(BF16), field)
    xt_ref[...] = xt.astype(BF16)
    query_rows = jnp.broadcast_to(query_ref[...].astype(F32)[None], (16, model_width)).astype(BF16)
    query = dot(query_rows, w_ref[0])[0:1].astype(BF16).astype(F32)
    table = table_ref[...]
    keys = dot(table, w_ref[1])
    values = dot(table, w_ref[2])
    values_ref[...] = values.astype(BF16)
    keys_t_ref[...] = keys.T
    query_col_ref[...] = jnp.broadcast_to(query, (LANES, width)).T
    lane = iota((width, LANES), 1) * HEAD_DIM
    row = iota((width, LANES), 0)
    same = ((row >= lane) & (row < lane + HEAD_DIM)).astype(F32)
    score = dot(keys * query, same, precision=HIGH) * SCALE
    score_ref[...] = score
    values_t = values.T.astype(BF16)
    for head in range(heads):
        column = score[:, head : head + 1]
        logits = jnp.broadcast_to(column[channels : channels + variables], (variables, xt.shape[1]))
        for p in range(pixels):
            part = slice(p * variables, (p + 1) * variables)
            logits = logits + column[part] * xt[part]
        weights = jnp.exp(logits - jnp.max(logits, axis=0, keepdims=True))
        probs = weights / jnp.sum(weights, axis=0, keepdims=True)
        probs_ref[head * variables : (head + 1) * variables] = probs
        low = probs.astype(BF16).astype(F32)
        mixing = spread(xt, pixels, low, bottom).astype(BF16)
        part = slice(head * HEAD_DIM, (head + 1) * HEAD_DIM)
        mixed_ref[part] = dot(values_t[part], mixing).astype(BF16)


def mix_out(mixed_ref, w_out_ref, send_a_ref, send_b_ref, keep_a_ref, keep_b_ref):
    quarter = keep_a_ref.shape[0]
    out = dot(mixed_ref[...], w_out_ref[...], 0, 0)
    keep_a_ref[...] = out[0:quarter]
    send_a_ref[...] = out[quarter : 2 * quarter].astype(BF16)
    keep_b_ref[...] = out[2 * quarter : 3 * quarter]
    send_b_ref[...] = out[3 * quarter :].astype(BF16)


def pack_mass(mass, bias, packed_ref):
    width = mass.shape[0]
    high = bias.astype(BF16).astype(F32)
    packed_ref[0:width] = mass.astype(BF16)
    packed_ref[width:] = jnp.concatenate([high, bias - high], axis=0).astype(BF16)


def add_mass(mass_ref, bias_ref, got_ref):
    width = mass_ref.shape[0]
    more = got_ref[width:].astype(F32)
    return mass_ref[...] + got_ref[0:width].astype(F32), bias_ref[...] + more[0:8] + more[8:16]


def mix_backward(
    pixels,
    pick_ref,
    xt_ref,
    probs_ref,
    values_ref,
    score_ref,
    w_out_ref,
    a0_ref,
    a1_ref,
    b0_ref,
    b1_ref,
    packed_ref,
    mass_ref,
    bias_ref,
    field_send_ref,
    field_keep_ref,
):
    channels, length = xt_ref.shape
    variables = channels // pixels
    rows, width = values_ref.shape
    heads = width // HEAD_DIM
    bottom = rows - channels - variables
    quarter = length // 4
    xt = xt_ref[...].astype(F32)
    grad = jnp.concatenate([a0_ref[...], a1_ref[...], b0_ref[...], b1_ref[...]], axis=0)
    grad_t = dot(w_out_ref[...], grad, 1, 1).astype(BF16)
    values = values_ref[...]
    score = score_ref[...]
    field = jnp.zeros(xt.shape, F32)
    lane = iota((rows, LANES), 1)
    sums = jnp.zeros((rows, LANES), F32)
    for head in range(heads):
        probs = probs_ref[head * variables : (head + 1) * variables]
        low = probs.astype(BF16).astype(F32)
        back = dot(lanes_of(values, head), grad_t)
        prob_grad = back[channels : channels + variables]
        for p in range(pixels):
            part = slice(p * variables, (p + 1) * variables)
            prob_grad = prob_grad + xt[part] * back[part]
        middle = jnp.sum(probs * prob_grad, axis=0, keepdims=True)
        score_grad = probs * (prob_grad - middle)
        column = score[:, head : head + 1]
        field = field + jnp.concatenate(
            [
                score_grad * column[p * variables : (p + 1) * variables]
                + low * back[p * variables : (p + 1) * variables]
                for p in range(pixels)
            ],
            axis=0,
        )
        spreading = spread(xt, pixels, score_grad * SCALE, bottom)
        sums = jnp.where(lane == head, jnp.sum(spreading, axis=1, keepdims=True), sums)
        mixing = spread(xt, pixels, low, bottom).astype(BF16)
        part = slice(head * HEAD_DIM, (head + 1) * HEAD_DIM)
        mass_ref[part] = dot(grad_t[part], mixing, 1, 1)
    bias_ref[...] = sums.T[0:8]
    pack_mass(mass_ref[...], bias_ref[...], packed_ref)
    field = dot(pick_ref[...], field.astype(BF16))
    field_keep_ref[:, 0:quarter] = field[:, 0:quarter]
    field_keep_ref[:, quarter:] = field[:, 2 * quarter : 3 * quarter]
    field_send_ref[:, 0:quarter] = field[:, quarter : 2 * quarter].astype(BF16)
    field_send_ref[:, quarter:] = field[:, 3 * quarter :].astype(BF16)


def norm_forward(*refs):
    *terms, gain_ref, bias_ref, out_ref, low_ref = refs
    total = terms[0][...].astype(F32)
    for term in terms[1:]:
        total = total + term[...].astype(F32)
    out_ref[...] = total
    centered = total - jnp.mean(total, axis=1, keepdims=True)
    inv_std = lax.rsqrt(jnp.mean(centered * centered, axis=1, keepdims=True) + EPS)
    low_ref[...] = (centered * inv_std * gain_ref[...] + bias_ref[...]).astype(BF16)


def norm_relay(pass_ref, *refs):
    *refs, out_ref = refs
    out_ref[...] = pass_ref[...]
    norm_forward(*refs)


def norm_backward(with_sum, add_refs, *refs):
    keep_ref, far_ref, rows_ref, gain_ref, above_ref = refs[:5]
    more = refs[5 : 5 + add_refs]
    out_ref, low_ref, sums_ref = refs[5 + add_refs :]
    grad = keep_ref[...] + far_ref[...].astype(F32)
    rows = rows_ref[...]
    centered = rows - jnp.mean(rows, axis=1, keepdims=True)
    inv_std = lax.rsqrt(jnp.mean(centered * centered, axis=1, keepdims=True) + EPS)
    normed = centered * inv_std
    scaled = grad * gain_ref[...]
    first = jnp.mean(scaled, axis=1, keepdims=True)
    second = jnp.mean(scaled * normed, axis=1, keepdims=True)
    out = above_ref[...].astype(F32) + inv_std * (scaled - first - normed * second)
    out_ref[...] = out
    low_ref[...] = out.astype(BF16)
    lines = [
        jnp.sum(grad * normed, axis=0, keepdims=True),
        jnp.sum(grad, axis=0, keepdims=True),
    ]
    lines.append(jnp.sum(out, axis=0, keepdims=True) if with_sum else jnp.zeros_like(lines[0]))
    if add_refs:
        one, two_a, two_b = (ref[...] for ref in more)
        lines = [
            lines[0] + one[0:1],
            lines[1] + one[1:2],
            two_a[0:1] + two_b[0:1],
            two_a[1:2] + two_b[1:2],
            lines[2] + one[2:3],
        ]
    lines.append(jnp.zeros((8 - len(lines), grad.shape[1]), F32))
    sums_ref[...] = jnp.concatenate(lines, axis=0)


def project(own_ref, near_ref, w_ref, out_ref):
    rows = jnp.concatenate([own_ref[...], near_ref[...]], axis=0)
    for i in range(3):
        out_ref[i] = dot(rows, w_ref[i]).astype(BF16)


def attend(query, keys, values_t, logs_ref):
    scaled = (query.astype(F32) * SCALE).astype(BF16)
    parts = []
    for head in range(keys.shape[1] // HEAD_DIM):
        scores = dot(lanes_of(keys, head), scaled, 1, 1)
        top = jnp.max(scores, axis=0, keepdims=True)
        weights = jnp.exp(scores - top)
        total = jnp.sum(weights, axis=0, keepdims=True)
        logs_ref[head : head + 1] = top + jnp.log(total)
        probs = (weights * (1.0 / total)).astype(BF16)
        parts.append(dot(values_t[head * HEAD_DIM : (head + 1) * HEAD_DIM], probs))
    return jnp.concatenate(parts, axis=0).T.astype(BF16)


def split_out(out, keep_ref, send_ref):
    quarter = out.shape[0] // 2
    keep_ref[...] = out[:quarter]
    send_ref[...] = out[quarter:].astype(BF16)


def attend_first(own_ref, near_ref, w_ref, first_ref, w_out_ref, second_ref, out_ref, logs_ref, keep_ref, send_ref):
    project(own_ref, near_ref, w_ref, second_ref)
    keys = jnp.concatenate([first_ref[1], second_ref[1]], axis=0)
    values = jnp.concatenate([first_ref[2], second_ref[2]], axis=0)
    out_ref[...] = attend(first_ref[0], keys, values.astype(F32).T.astype(BF16), logs_ref)
    split_out(dot(out_ref[...], w_out_ref[...]), keep_ref, send_ref)


def attend_second(first_ref, second_ref, w_out_ref, out_ref, logs_ref, keep_ref, send_ref):
    keys = jnp.concatenate([first_ref[1], second_ref[1]], axis=0)
    values = jnp.concatenate([first_ref[2], second_ref[2]], axis=0)
    out_ref[...] = attend(second_ref[0], keys, values.astype(F32).T.astype(BF16), logs_ref)
    split_out(dot(out_ref[...], w_out_ref[...]), keep_ref, send_ref)


def attend_grad(grad, query, keys, values, logs_ref):
    scaled = (query.astype(F32) * SCALE).astype(BF16)
    keys_t = keys.astype(F32).T.astype(BF16)
    query_parts = []
    key_grad = jnp.zeros(keys.shape, F32)
    value_grad = jnp.zeros(keys.shape, F32)
    for head in range(keys.shape[1] // HEAD_DIM):
        scores = dot(lanes_of(keys, head), scaled, 1, 1)
        probs = jnp.exp(scores - logs_ref[head : head + 1])
        prob_grad = dot(lanes_of(values, head), grad, 1, 1)
        middle = jnp.sum(probs * prob_grad, axis=0, keepdims=True)
        score_grad = (probs * (prob_grad - middle)).astype(BF16)
        query_parts.append(dot(keys_t[head * HEAD_DIM : (head + 1) * HEAD_DIM], score_grad))
        key_grad = key_grad + dot(score_grad, lanes_of(scaled, head))
        value_grad = value_grad + dot(probs.astype(BF16), lanes_of(grad, head))
    query_grad = (jnp.concatenate(query_parts, axis=0).T * SCALE).astype(BF16)
    return query_grad, key_grad, value_grad


def attend_back_first(own_ref, near_ref, w_out_ref, first_ref, second_ref, logs_ref, query_ref, key_ref, value_ref):
    rows = jnp.concatenate([own_ref[...], near_ref[...]], axis=0)
    grad = dot(rows, w_out_ref[...], 1, 1).astype(BF16)
    keys = jnp.concatenate([first_ref[1], second_ref[1]], axis=0)
    values = jnp.concatenate([first_ref[2], second_ref[2]], axis=0)
    query_ref[...], key_ref[...], value_ref[...] = attend_grad(
        grad, first_ref[0], keys, values, logs_ref
    )


def project_back(rows_ref, start, count, w_ref):
    total = dot(rows_ref[0, start : start + count], w_ref[0], 1, 1)
    for i in range(1, 3):
        total = total + dot(rows_ref[i, start : start + count], w_ref[i], 1, 1)
    return total


def attend_back_second(
    own_ref,
    near_ref,
    w_out_ref,
    first_ref,
    second_ref,
    logs_ref,
    query_ref,
    key_ref,
    value_ref,
    w_ref,
    out_ref,
    keep_ref,
    send_ref,
):
    rows = jnp.concatenate([own_ref[...], near_ref[...]], axis=0)
    half = rows.shape[0]
    grad = dot(rows, w_out_ref[...], 1, 1).astype(BF16)
    keys = jnp.concatenate([first_ref[1], second_ref[1]], axis=0)
    values = jnp.concatenate([first_ref[2], second_ref[2]], axis=0)
    query_grad, key_grad, value_grad = attend_grad(grad, second_ref[0], keys, values, logs_ref)
    out_ref[0, 0:half] = query_ref[...]
    out_ref[0, half:] = query_grad
    out_ref[1] = (key_ref[...] + key_grad).astype(BF16)
    out_ref[2] = (value_ref[...] + value_grad).astype(BF16)
    split_out(project_back(out_ref, 0, half, w_ref), keep_ref, send_ref)


def attend_back_last(rows_ref, w_ref, keep_ref, send_ref):
    half = rows_ref.shape[1] // 2
    split_out(project_back(rows_ref, half, half, w_ref), keep_ref, send_ref)


def hidden_back(own_ref, near_ref, w_ref, out_ref):
    rows = jnp.concatenate([own_ref[...], near_ref[...]], axis=0)
    out_ref[...] = dot(rows, w_ref[...], 1, 1)


ROOT = 0.7978845608028654
CUBE = 0.044715


def mlp(own_ref, near_ref, w_ref, grad_ref, hidden_ref, out_ref, keep_ref, send_ref):
    rows = jnp.concatenate([own_ref[...], near_ref[...]], axis=0)
    pre = dot(rows, w_ref[...])
    square = pre * pre
    bend = jnp.tanh(ROOT * pre * (1.0 + CUBE * square))
    half = 0.5 * (1.0 + bend)
    hidden_ref[...] = (pre * half).astype(BF16)
    slope = half + (0.5 * ROOT) * pre * (1.0 - bend * bend) * (1.0 + (3.0 * CUBE) * square)
    out_ref[...] = (slope * grad_ref[...]).astype(BF16)
    split_out(dot(out_ref[...], w_ref[...], 1, 1), keep_ref, send_ref)


def mlp_out(first_ref, second_ref, w_ref, keep_a_ref, send_a_ref, keep_b_ref, send_b_ref):
    split_out(dot(first_ref[...], w_ref[...]), keep_a_ref, send_a_ref)
    split_out(dot(second_ref[...], w_ref[...]), keep_b_ref, send_b_ref)


def grad_rows(parts, step, width, which):
    groups = width // (2 * step)
    outs = []
    for group in range(groups):
        start = pl.multiple_of((2 * group + which) * step, LANES)
        line = []
        for left, rights in parts:
            picked = jnp.concatenate([ref[:, pl.ds(start, step)] for ref in left], axis=0)
            line.extend(dot(picked, right, 0, 0) for right in rights)
        outs.append(line)
    return outs, groups


def write_half(ref, parts, step, width, which, dtype):
    outs, groups = grad_rows(parts, step, width, which)
    for group in range(groups):
        column = 0
        for value in outs[group]:
            ref[group * step : (group + 1) * step, column : column + value.shape[1]] = value.astype(dtype)
            column += value.shape[1]


def take_half(out_ref, source, step, which, dtype):
    for group in range(source.shape[0] // (2 * step)):
        start = pl.multiple_of((2 * group + which) * step, 16)
        out_ref[group * step : (group + 1) * step] = source[pl.ds(start, step)].astype(dtype)


def sum_start(load, step, bit, *refs):
    *inputs, out_ref = refs
    parts, width = load(inputs)
    write_half(out_ref, parts, step, width, 1 - my_bit(bit), BF16)


def sum_second(load, step, next_step, bit, next_bit, *refs):
    got_ref, *inputs, keep_ref, send_ref, total = refs
    parts, width = load(inputs)
    write_half(total, parts, step, width, my_bit(bit), F32)
    total[...] = total[...] + got_ref[...].astype(F32)
    take_half(send_ref, total, next_step, 1 - my_bit(next_bit), BF16)
    take_half(keep_ref, total, next_step, my_bit(next_bit), F32)


def sum_next(next_step, next_bit, kept_ref, got_ref, keep_ref, send_ref, total):
    total[...] = kept_ref[...] + got_ref[...].astype(F32)
    take_half(send_ref, total, next_step, 1 - my_bit(next_bit), BF16)
    take_half(keep_ref, total, next_step, my_bit(next_bit), F32)


def load_plain(inputs):
    *left, first, second = inputs
    right = jnp.concatenate([first[...], second[...]], axis=0)
    return [(left, [right])], left[0].shape[1]


def load_attn(inputs):
    left, middle = inputs[0:4], inputs[4:8]
    proj, first, second = inputs[8:]
    attended = jnp.concatenate([first[...], second[...]], axis=0)
    return [(left, [proj[0], proj[1], proj[2]]), (middle, [attended])], left[0].shape[1]


def last_plain(kept_ref, got_ref, out_ref):
    out_ref[...] = kept_ref[...] + got_ref[...].astype(F32)


def last_turned(kept_ref, got_ref, out_ref):
    out_ref[...] = (kept_ref[...] + got_ref[...].astype(F32)).T


def last_attn(kept_ref, got_ref, proj_ref, out_ref):
    total = kept_ref[...] + got_ref[...].astype(F32)
    width = proj_ref.shape[2]
    for i in range(3):
        proj_ref[i] = total[:, i * width : (i + 1) * width]
    out_ref[...] = total[:, 3 * width :].T


def mix_lines(samples, lines, bucket_ref, inputs, rest_ref):
    first_ref, second_ref, own_ref, near_ref = inputs
    quarter, width = first_ref.shape
    rest_ref[0:quarter] = jnp.where(my_chip() == 0, first_ref[...], second_ref[...])
    sample = lax.axis_index("dp")
    sums = own_ref[...] + near_ref[...]
    row = iota((lines, width), 0)
    filled = jnp.concatenate([sums, jnp.zeros((lines - 8, width), F32)], axis=0)
    filled = jnp.where(row < 4, filled, 0.0)
    filled = jnp.where(row == 4 + sample, sums[4:5], filled)
    bucket = bucket_ref[0].astype(F32)
    rest_ref[quarter:] = jnp.where(row == 4 + samples + sample, bucket, filled)


def write_mix(ref, step, which, left, mixed_ref, rest_ref, dtype):
    width = left[0].shape[1]
    heads_width = mixed_ref.shape[0]
    for group in range(width // (2 * step)):
        start = pl.multiple_of((2 * group + which) * step, LANES)
        picked = jnp.concatenate([part[:, pl.ds(start, step)] for part in left], axis=0)
        rows = slice(group * step, (group + 1) * step)
        ref[rows, 0:heads_width] = dot(picked, mixed_ref[...], 0, 1).astype(dtype)
        ref[rows, heads_width:] = rest_ref[:, pl.ds(start, step)].T.astype(dtype)


def mix_start(samples, lines, step, bit, bucket_ref, mixed_ref, *refs):
    *inputs, out_ref, rest = refs
    mix_lines(samples, lines, bucket_ref, inputs[4:], rest)
    write_mix(out_ref, step, 1 - my_bit(bit), inputs[:4], mixed_ref, rest, BF16)


def mix_second(samples, lines, step, next_step, bit, next_bit, bucket_ref, mixed_ref, *refs):
    got_ref, *inputs, keep_ref, send_ref, rest, total = refs
    mix_lines(samples, lines, bucket_ref, inputs[4:], rest)
    write_mix(total, step, my_bit(bit), inputs[:4], mixed_ref, rest, F32)
    total[...] = total[...] + got_ref[...].astype(F32)
    take_half(send_ref, total, next_step, 1 - my_bit(next_bit), BF16)
    take_half(keep_ref, total, next_step, my_bit(next_bit), F32)


def mix_last(samples, quarter, final, kept_ref, got_ref, out_ref, pos_ref, lead_ref, small_ref):
    total = kept_ref[...] + got_ref[...].astype(F32)
    heads_width = out_ref.shape[0]
    out_ref[...] = total[:, :heads_width].T
    pos_ref[...] = total[:, heads_width : heads_width + quarter].T
    rest = total[:, heads_width + quarter :]
    rows = max(final, 8)
    mine = iota((rows, rest.shape[0]), 1) == iota((rows, rest.shape[0]), 0) + lax.axis_index("mp") * final
    own = dot(mine.astype(F32), rest, precision=HIGH)
    bucket = iota((rows, lead_ref.shape[1]), 1).astype(F32)
    lead = jnp.zeros(bucket.shape, F32)
    for s in range(samples):
        mark = own[:, 4 + samples + s : 5 + samples + s]
        lead = jnp.where(bucket == mark, lead + own[:, 4 + s : 5 + s], lead)
    lead_ref[...] = lead[:final]
    small_ref[...] = own.T[0:8, :final]


def mass_add(mass_ref, bias_ref, got_ref, packed_ref, mass_out_ref, bias_out_ref):
    mass, bias = add_mass(mass_ref, bias_ref, got_ref)
    mass_out_ref[...] = mass
    bias_out_ref[...] = bias
    pack_mass(mass, bias, packed_ref)


def mix_finish(
    pixels,
    query_col_ref,
    keys_t_ref,
    patch_ref,
    variable_ref,
    mass_ref,
    bias_ref,
    got_ref,
    w_ref,
    query_ref,
    keep_ref,
    send_ref,
    grad_ref,
    scratch,
):
    width, rows = mass_ref.shape
    heads = width // HEAD_DIM
    mass, sums = add_mass(mass_ref, bias_ref, got_ref)
    mass = mass.astype(BF16)
    bias = jnp.concatenate(
        [jnp.broadcast_to(sums[head : head + 1], (HEAD_DIM, rows)) for head in range(heads)], axis=0
    )
    key_mass = (bias * query_col_ref[:, 0:1]).astype(BF16)
    total = jnp.sum(keys_t_ref[...] * bias, axis=1, keepdims=True)
    own = grad_ref.shape[1]
    start = lax.axis_index("dp") * own
    model_width = variable_ref.shape[1]
    channels = patch_ref.shape[0] * pixels
    mine = exact(iota((own, model_width), 1) == iota((own, model_width), 0) + start)
    total_row = jnp.broadcast_to(total, (width, LANES)).T[0:1]
    flat = patch_ref[...].reshape(channels, model_width)
    patch_t = dot(mine, flat, 1, 1).astype(BF16)
    patch_t = dot(patch_t, pixel_major(channels, pixels), 1, 1)
    variable_t = dot(mine, variable_ref[...], 1, 1)
    bottom = rows - channels - variable_ref.shape[0]
    table_t = jnp.concatenate([patch_t, variable_t, jnp.zeros((own, bottom), F32)], axis=1).astype(BF16)
    query_rows = jnp.broadcast_to(query_ref[...].astype(F32)[None], (16, model_width)).astype(BF16)
    grad_ref[0] = dot(mine, query_rows, 1, 1)[:, 0:1] * total_row
    grad_ref[1] = dot(table_t, key_mass, 1, 1)
    grad_ref[2] = dot(table_t, mass, 1, 1)
    back = dot(w_ref[1], key_mass) + dot(w_ref[2], mass)
    query_back = jnp.sum(w_ref[0].astype(F32) * total_row, axis=1, keepdims=True)
    scratch[...] = jnp.where(iota((own, rows), 1) == rows - 1, query_back, back)
    keep_part(scratch, keep_ref, send_ref, my_chip())


def keep_part(source, keep_ref, send_ref, which):
    step = keep_ref.shape[0]
    if step % 8:
        first, second = source[0:step], source[step : 2 * step]
        keep_ref[...] = jnp.where(which == 0, first, second)
        send_ref[...] = jnp.where(which == 0, second, first)
    else:
        keep_ref[...] = source[pl.ds(pl.multiple_of(which * step, 8), step)]
        send_ref[...] = source[pl.ds(pl.multiple_of((1 - which) * step, 8), step)]


def tables_next(kept_ref, got_ref, keep_ref, send_ref, scratch):
    scratch[...] = kept_ref[...] + got_ref[...]
    keep_part(scratch, keep_ref, send_ref, my_core())


def pair_sum(keep_ref, got_ref, out_ref, low_ref):
    total = keep_ref[...] + got_ref[...].astype(F32)
    out_ref[...] = total
    low_ref[...] = total.astype(BF16)


def take_rows(source_ref, out_ref):
    out_ref[...] = source_ref[...]


def take_weights(pixels, ids_ref, source_ref, out_ref, pick_ref):
    out_ref[...] = source_ref[...]
    channels = pick_ref.shape[0]
    pick = iota((channels, channels), 0) == places(ids_ref, channels // pixels, pixels)
    pick_ref[...] = pick.astype(F32).T.astype(BF16)


def by_chip(own_ref, far_ref, first_ref, second_ref):
    own, far = own_ref[...], far_ref[...]
    first = my_chip() == 0
    first_ref[...] = jnp.where(first, own, far)
    second_ref[...] = jnp.where(first, far, own)


def base_rows(bucket_ref, first_ref, second_ref, lead_ref, out_a_ref, out_b_ref):
    rows = lead_ref.shape[0]
    mark = exact(iota((16, rows), 1) == bucket_ref[0])
    lead = dot(mark, lead_ref[...])[0:1]
    out_a_ref[...] = first_ref[...].astype(F32) + lead
    out_b_ref[...] = second_ref[...].astype(F32) + lead


def field_sum(keep_ref, got_ref, own_ref, send_ref):
    total = keep_ref[...] + got_ref[...].astype(F32)
    quarter = own_ref.shape[1]
    first = my_chip() == 0
    own_ref[...] = jnp.where(first, total[:, :quarter], total[:, quarter:])
    send_ref[...] = jnp.where(first, total[:, quarter:], total[:, :quarter]).astype(BF16)


def field_last(own_ref, far_ref, out_ref):
    out_ref[0] = own_ref[...] + far_ref[...].astype(F32)


def rows_sum(keep_a_ref, got_a_ref, keep_b_ref, got_b_ref, mid_a_ref, mid_b_ref, own_ref, send_ref):
    part_a = keep_a_ref[...] + got_a_ref[...].astype(F32)
    part_b = keep_b_ref[...] + got_b_ref[...].astype(F32)
    first = my_chip() == 0
    own_ref[...] = jnp.where(first, part_a + mid_a_ref[...], part_b + mid_b_ref[...])
    send_ref[...] = jnp.where(first, part_b, part_a).astype(BF16)


def tables_last(pixels, variables, kept_ref, got_ref, patch_ref, variable_ref, query_ref):
    total = kept_ref[...] + got_ref[...]
    for p in range(pixels):
        patch_ref[p] = total[:, p * variables : (p + 1) * variables]
    variable_ref[...] = total[:, pixels * variables : (pixels + 1) * variables]
    query_ref[...] = total.T[total.shape[1] - 8 :]


def pairs(count, bit):
    return [(i, i ^ bit) for i in range(count)]


def body(
    mesh_dp,
    mesh_mp,
    input_field,
    variable_ids,
    lead_bucket,
    patch_table,
    variable_table,
    variable_query,
    mix_weights,
    mix_output,
    pos_table,
    lead_table,
    first_gain,
    first_bias,
    attn_weights,
    attn_output,
    second_gain,
    second_bias,
    up_weight,
    down_weight,
    cotangent,
):
    length = input_field.shape[2]
    channels = input_field.shape[1]
    variables = variable_ids.shape[0]
    pixels = channels // variables
    model_width = pos_table.shape[1]
    quarter = cotangent.shape[0]
    head_width = mix_weights.shape[2]
    hidden_width = up_weight.shape[1]
    heads = head_width // HEAD_DIM
    own_width = model_width // mesh_dp
    half = 2 * quarter
    latest, now = [], []
    v = types.SimpleNamespace()

    def call(kernel, outs, args, final=False, **options):
        if final:
            outs = outs + [((8, LANES), F32)]
            kernel = functools.partial(marked, kernel)
        known = flat(args)[0] + list(options.get("fetch", ()))
        after = [last for last in latest if all(last is not arg for arg in known)]
        cost = COSTS.get(now[0], 0.1)
        results = launch(kernel, outs, args, after=after, cost=cost, name=now[0], **options)
        latest[:] = results[-1:] if final else flat(results)[0][:1]
        return results[:-1] if final else results

    rows32 = ((quarter, model_width), F32)
    rows16 = ((quarter, model_width), BF16)
    cut16 = [((quarter // PIECES, model_width), BF16)] * PIECES

    def swap_core(value):
        if isinstance(value, list):
            return [swap_core(piece) for piece in value]
        return lax.ppermute(value, "mp", pairs(mesh_mp, 1))

    def swap_chip(value):
        return lax.ppermute(value, "mp", pairs(mesh_mp, 2))

    def swap_sample(value, bit):
        return lax.ppermute(value, "dp", pairs(mesh_dp, bit))

    def add_near(keep, near):
        kept, low = call(pair_sum, [rows32, rows16], [keep, near])
        return kept, swap_chip(low)

    all_bits = [1 << i for i in range(mesh_dp.bit_length() - 1)]
    wide = [bit for bit in all_bits if bit * own_width % LANES == 0]

    def order_from(axes):
        return [wide[i] for i in axes] + [bit for bit in all_bits if bit not in wide[:3]]

    def steps_of(order):
        left = list(all_bits)
        steps = []
        for bit in order:
            steps.append(own_width << left.index(bit))
            left.remove(bit)
        return steps

    def start_sum(load, inputs, width, order):
        step = steps_of(order)[0]
        (send,) = call(
            functools.partial(sum_start, load, step, order[0]),
            [((model_width // 2, width), BF16)],
            inputs,
        )
        return swap_sample(send, order[0])

    def halves(width, scratch_rows):
        kept = scratch_rows // 2
        return [((kept, width), F32), ((kept, width), BF16)]

    def second_sum(load, inputs, got, width, order):
        steps = steps_of(order)
        rows = model_width // 2
        keep, send = call(
            functools.partial(sum_second, load, steps[0], steps[1], order[0], order[1]),
            halves(width, rows),
            [got] + inputs,
            scratch=[pltpu.VMEM((rows, width), F32)],
        )
        return keep, swap_sample(send, order[1])

    def rest_sum(keep, got, order):
        steps = steps_of(order)
        for i in range(2, len(order)):
            rows, width = keep.shape
            keep, send = call(
                functools.partial(sum_next, steps[i], order[i]),
                halves(width, rows),
                [keep, got],
                scratch=[pltpu.VMEM((rows, width), F32)],
            )
            got = swap_sample(send, order[i])
        return keep, got

    def norm_rows(terms, gain, bias):
        return call(norm_forward, [rows32, cut16], terms + [gain, bias])

    w_mix = mix_weights.transpose(1, 0, 2)
    w_attn = attn_weights.transpose(1, 0, 2)
    gain_one, bias_one = first_gain[None], first_bias[None]
    gain_two, bias_two = second_gain[None], second_bias[None]
    table_rows = channels + variables
    padded = -(-(table_rows + 1) // LANES) * LANES
    lines = -(-(4 + 2 * mesh_dp) // LANES) * LANES
    mix_width = head_width + quarter + lines
    attn_width = 4 * head_width
    final = own_width // mesh_mp
    own_field = (channels, quarter)
    proj_kind = ((3, half, head_width), BF16)
    attend_kinds = [((half, head_width), BF16), ((8, half), F32), rows32, cut16]
    hidden_kind = ((half, hidden_width), F32)
    mlp_kinds = [((half, hidden_width), BF16)] * 2 + [rows32, cut16]
    back_kinds = [rows32, cut16, ((8, model_width), F32)]
    grad_kinds = [((half, head_width), BF16)] + [((length, head_width), F32)] * 2
    mass_kinds = [
        ((head_width + 16, padded), BF16),
        ((head_width, padded), F32),
        ((8, padded), F32),
    ]
    rest_rows = pltpu.VMEM((quarter + lines, model_width), F32)
    down_order, up_order, attn_order, mix_order, mass_bits = map(order_from, AXES)
    mix_steps = steps_of(mix_order)
    back_two = functools.partial(norm_backward, False, 0)

    def mix_a():
        v.mixed_t, v.field_t, v.probs, v.values, v.keys_t, v.score, v.query_col = call(
            functools.partial(mix_forward, pixels, quarter),
            [
                ((head_width, length), BF16),
                ((channels, length), BF16),
                ((heads * variables, length), F32),
                ((padded, head_width), BF16),
                ((head_width, padded), F32),
                ((padded, LANES), F32),
                ((head_width, LANES), F32),
            ],
            [variable_query],
            fetch=[input_field, patch_table, variable_table, w_mix],
            smem=[variable_ids],
            limit=FIRST_LIMIT,
            scratch=[pltpu.VMEM((padded, model_width), BF16)],
        )

    def mix_b():
        send_a, send_b, v.keep_a, v.keep_b = call(
            mix_out, [rows16, rows16, rows32, rows32], [mix_output], fetch=[v.mixed_t]
        )
        v.near_a, v.near_b = swap_core(send_a), swap_core(send_b)

    def first_a():
        v.kept_a, v.far_a = add_near(v.keep_a, v.near_a)

    def first_b():
        v.kept_b, v.far_b = add_near(v.keep_b, v.near_b)

    def second_a():
        first_a()

    def second_b():
        first_b()

    def base():
        blocks = [
            (
                pos_table,
                (quarter, model_width),
                lambda ref, k=k: ref.at[pl.ds((2 * k + my_core()) * quarter, quarter)],
            )
            for k in range(2)
        ]
        v.base_a, v.base_b = call(
            base_rows, [rows32] * 2, [], fetch=blocks + [lead_table], smem=[lead_bucket]
        )

    def norm_a():
        v.in_a, v.one_a0 = norm_rows([v.kept_a, v.far_a, v.base_a], gain_one, bias_one)
        v.one_a1 = swap_core(v.one_a0)

    def proj():
        (v.proj_a,) = call(project, [proj_kind], [v.one_a0, v.one_a1, w_attn])

    def norm_b():
        v.in_b, v.one_b0, v.cot_own = call(
            norm_relay,
            [rows32, cut16, rows16],
            [cotangent, v.kept_b, v.far_b, v.base_b, gain_one, bias_one],
        )
        v.one_b1 = swap_core(v.one_b0)
        v.cot_far = swap_chip(v.cot_own)

    def attend_a():
        v.proj_b, v.attended_a, v.logs_a, v.keep_a, send_a = call(
            attend_first,
            [proj_kind] + attend_kinds,
            [v.one_b0, v.one_b1, w_attn, v.proj_a, attn_output],
        )
        v.near_a = swap_core(send_a)

    def attend_b():
        v.attended_b, v.logs_b, v.keep_b, send_b = call(
            attend_second, attend_kinds, [v.proj_a, v.proj_b, attn_output]
        )
        v.near_b = swap_core(send_b)

    def cot():
        v.cot_a0, v.cot_b0 = call(by_chip, [cut16] * 2, [v.cot_own, v.cot_far])
        v.cot_a1, v.cot_b1 = swap_core(v.cot_a0), swap_core(v.cot_b0)

    def hidden_a():
        (v.grad_hidden_a,) = call(hidden_back, [hidden_kind], [v.cot_a0, v.cot_a1, down_weight])

    def hidden_b():
        (v.grad_hidden_b,) = call(hidden_back, [hidden_kind], [v.cot_b0, v.cot_b1, down_weight])

    def two_a():
        v.mid_a, v.two_a0 = norm_rows([v.kept_a, v.far_a, v.in_a], gain_two, bias_two)
        v.two_a1 = swap_core(v.two_a0)

    def two_b():
        v.mid_b, v.two_b0 = norm_rows([v.kept_b, v.far_b, v.in_b], gain_two, bias_two)
        v.two_b1 = swap_core(v.two_b0)

    def mlp_a():
        v.hidden_a, v.pre_a, v.m_keep_a, send_a = call(
            mlp, mlp_kinds, [v.two_a0, v.two_a1, up_weight, v.grad_hidden_a]
        )
        v.m_near_a = swap_core(send_a)

    def mlp_b():
        v.hidden_b, v.pre_b, v.m_keep_b, send_b = call(
            mlp, mlp_kinds, [v.two_b0, v.two_b1, up_weight, v.grad_hidden_b]
        )
        v.m_near_b = swap_core(send_b)

    def third_a():
        v.m_kept_a, v.m_far_a = add_near(v.m_keep_a, v.m_near_a)

    def third_b():
        v.m_kept_b, v.m_far_b = add_near(v.m_keep_b, v.m_near_b)

    def down_in():
        return [v.cot_a0, v.cot_a1, v.cot_b0, v.cot_b1, v.hidden_a, v.hidden_b]

    def up_in():
        return [v.two_a0, v.two_a1, v.two_b0, v.two_b1, v.pre_a, v.pre_b]

    def attn_in():
        one = [v.one_a0, v.one_a1, v.one_b0, v.one_b1]
        mid = [v.back_a0, v.back_a1, v.back_b0, v.back_b1]
        return one + mid + [v.grad_proj, v.attended_a, v.attended_b]

    def up_1():
        v.up_got = start_sum(load_plain, up_in(), hidden_width, up_order)

    def down_1():
        v.down_got = start_sum(load_plain, down_in(), hidden_width, down_order)

    def attn_1():
        v.attn_got = start_sum(load_attn, attn_in(), attn_width, attn_order)

    def up_2():
        v.up_keep, v.up_got = second_sum(load_plain, up_in(), v.up_got, hidden_width, up_order)

    def down_2():
        v.down_keep, v.down_got = second_sum(
            load_plain, down_in(), v.down_got, hidden_width, down_order
        )

    def attn_2():
        v.attn_keep, v.attn_got = second_sum(
            load_attn, attn_in(), v.attn_got, attn_width, attn_order
        )

    def up_3():
        v.up_keep, v.up_got = rest_sum(v.up_keep, v.up_got, up_order)

    def down_3():
        v.down_keep, v.down_got = rest_sum(v.down_keep, v.down_got, down_order)

    def attn_3():
        v.attn_keep, v.attn_got = rest_sum(v.attn_keep, v.attn_got, attn_order)

    def mid_a():
        v.grad_mid_a, v.back_a0, v.sums_two_a = call(
            back_two, back_kinds, [v.m_kept_a, v.m_far_a, v.mid_a, gain_two, v.cot_a0]
        )
        v.back_a1 = swap_core(v.back_a0)

    def mid_b():
        v.grad_mid_b, v.back_b0, v.sums_two_b = call(
            back_two, back_kinds, [v.m_kept_b, v.m_far_b, v.mid_b, gain_two, v.cot_b0]
        )
        v.back_b1 = swap_core(v.back_b0)

    def back_a():
        v.query_grad, v.key_grad, v.value_grad = call(
            attend_back_first,
            grad_kinds,
            [v.back_a0, v.back_a1, attn_output, v.proj_a, v.proj_b, v.logs_a],
        )

    def back_b():
        v.grad_proj, v.p_keep_a, send_a = call(
            attend_back_second,
            [((3, length, head_width), BF16), rows32, cut16],
            [
                v.back_b0,
                v.back_b1,
                attn_output,
                v.proj_a,
                v.proj_b,
                v.logs_b,
                v.query_grad,
                v.key_grad,
                v.value_grad,
                w_attn,
            ],
        )
        v.p_near_a = swap_core(send_a)

    def back_c():
        v.p_keep_b, send_b = call(attend_back_last, [rows32, cut16], [v.grad_proj, w_attn])
        v.p_near_b = swap_core(send_b)

    def fourth_a():
        v.p_kept_a, v.p_far_a = add_near(v.p_keep_a, v.p_near_a)

    def fourth_b():
        v.p_kept_b, v.p_far_b = add_near(v.p_keep_b, v.p_near_b)

    def in_a():
        v.grad_in_a, v.in_a0, v.sums_one_a = call(
            functools.partial(norm_backward, True, 0),
            back_kinds,
            [v.p_kept_a, v.p_far_a, v.in_a, gain_one, v.grad_mid_a],
        )
        v.in_a1 = swap_core(v.in_a0)

    def in_b():
        v.grad_in_b, v.in_b0, v.sums = call(
            functools.partial(norm_backward, True, 3),
            back_kinds,
            [
                v.p_kept_b,
                v.p_far_b,
                v.in_b,
                gain_one,
                v.grad_mid_b,
                v.sums_one_a,
                v.sums_two_a,
                v.sums_two_b,
            ],
        )
        v.in_b1 = swap_core(v.in_b0)
        v.near_sums = swap_core(v.sums)

    def mass_1():
        packed, v.mass, v.bias, v.field_send, v.field_keep = call(
            functools.partial(mix_backward, pixels),
            mass_kinds + [((channels, half), BF16), ((channels, half), F32)],
            [v.pick, v.field_t, v.probs, v.values, v.score, mix_output, v.in_a0, v.in_a1, v.in_b0, v.in_b1],
        )
        v.mass_got = swap_sample(packed, mass_bits[0])
        v.field_near = swap_core(v.field_send)

    def add_masses(bits):
        for bit in bits:
            packed, v.mass, v.bias = call(mass_add, mass_kinds, [v.mass, v.bias, v.mass_got])
            v.mass_got = swap_sample(packed, bit)

    def mass_2():
        add_masses(mass_bits[1:2])

    def mass_3():
        add_masses(mass_bits[2:])

    def mix_in():
        rows = [v.in_a0, v.in_a1, v.in_b0, v.in_b1]
        return rows + [v.grad_in_a, v.grad_in_b, v.sums, v.near_sums]

    def mix_1():
        (send,) = call(
            functools.partial(mix_start, mesh_dp, lines, mix_steps[0], mix_order[0]),
            [((model_width // 2, mix_width), BF16)],
            [v.mixed_t] + mix_in(),
            smem=[lead_bucket],
            scratch=[rest_rows],
        )
        v.mix_got = swap_sample(send, mix_order[0])

    def mix_2():
        v.mix_keep, send = call(
            functools.partial(
                mix_second, mesh_dp, lines, mix_steps[0], mix_steps[1], mix_order[0], mix_order[1]
            ),
            halves(mix_width, model_width // 2),
            [v.mixed_t, v.mix_got] + mix_in(),
            smem=[lead_bucket],
            scratch=[rest_rows, pltpu.VMEM((model_width // 2, mix_width), F32)],
        )
        v.mix_got = swap_sample(send, mix_order[1])

    def mix_3():
        v.mix_keep, v.mix_got = rest_sum(v.mix_keep, v.mix_got, mix_order)

    def field_1():
        v.field_own, far = call(
            field_sum, [(own_field, F32), (own_field, BF16)], [v.field_keep, v.field_near]
        )
        v.field_got = swap_chip(far)

    def field_2():
        (v.field_grad,) = call(
            field_last, [((1,) + own_field, F32)], [v.field_own, v.field_got], final=True
        )

    def rows_1():
        v.r_keep_a, send_a, v.r_keep_b, send_b = call(
            mlp_out, [rows32, cut16] * 2, [v.hidden_a, v.hidden_b, down_weight]
        )
        v.r_near_a, v.r_near_b = swap_core(send_a), swap_core(send_b)

    def rows_2():
        v.rows_own, far = call(
            rows_sum,
            [rows32, rows16],
            [v.r_keep_a, v.r_near_a, v.r_keep_b, v.r_near_b, v.mid_a, v.mid_b],
        )
        v.rows_got = swap_chip(far)

    def rows_3():
        (v.activations,) = call(last_plain, [rows32], [v.rows_own, v.rows_got], final=True)

    def weights():
        v.own_weights, v.pick = call(
            functools.partial(take_weights, pixels),
            [((3, own_width, head_width), BF16), ((channels, channels), BF16)],
            [],
            smem=[variable_ids],
            fetch=[
                (
                    w_mix,
                    (3, own_width, head_width),
                    lambda ref: ref.at[:, pl.ds(lax.axis_index("dp") * own_width, own_width)],
                )
            ],
        )

    def finish():
        v.t_keep, send, v.grad_mix = call(
            functools.partial(mix_finish, pixels),
            [((own_width // 2, padded), F32)] * 2 + [((3, own_width, head_width), F32)],
            [
                v.query_col,
                v.keys_t,
                patch_table,
                variable_table,
                v.mass,
                v.bias,
                v.mass_got,
                v.own_weights,
                variable_query,
            ],
            scratch=[pltpu.VMEM((own_width, padded), F32)],
        )
        v.t_far = swap_chip(send)

    def tables_1():
        v.t_keep, send = call(
            tables_next,
            [((final, padded), F32)] * 2,
            [v.t_keep, v.t_far],
            scratch=[pltpu.VMEM((own_width // 2, padded), F32)],
        )
        v.t_near = swap_core(send)

    def tables_2():
        v.patch_total, v.variable_total, v.query_total = call(
            functools.partial(tables_last, pixels, variables),
            [((pixels, final, variables), F32), ((final, variables), F32), ((8, final), F32)],
            [v.t_keep, v.t_near],
            final=True,
        )

    def down_4():
        (v.down_sum,) = call(
            last_turned, [((hidden_width, own_width), F32)], [v.down_keep, v.down_got], final=True
        )

    def up_4():
        (v.up_sum,) = call(
            last_plain, [((own_width, hidden_width), F32)], [v.up_keep, v.up_got], final=True
        )

    def mix_4():
        v.mix_out_sum, v.pos_sum, v.lead_total, v.small = call(
            functools.partial(mix_last, mesh_dp, quarter, final),
            [
                ((head_width, own_width), F32),
                ((quarter, own_width), F32),
                ((final, lead_table.shape[0]), F32),
                ((8, final), F32),
            ],
            [v.mix_keep, v.mix_got],
            final=True,
        )

    def attn_4():
        v.attn_sum, v.attn_out_sum = call(
            last_attn,
            [((3, own_width, head_width), F32), ((head_width, own_width), F32)],
            [v.attn_keep, v.attn_got],
            final=True,
        )

    steps = dict(locals())
    for name in ORDER:
        now[:] = [name]
        steps[name]()
    return (
        v.activations,
        v.field_grad,
        v.patch_total.transpose(2, 0, 1),
        v.variable_total.T,
        v.query_total[7],
        v.grad_mix.transpose(1, 0, 2),
        v.mix_out_sum,
        v.pos_sum,
        v.lead_total.T,
        v.small[0],
        v.small[1],
        v.attn_sum.transpose(1, 0, 2),
        v.attn_out_sum,
        v.small[2],
        v.small[3],
        v.up_sum,
        v.down_sum,
    )


def solution(mesh):
    in_specs = (
        P("dp", None, None),
        P(),
        P("dp"),
        P(),
        P(),
        P(),
        P(None, None, "mp"),
        P("mp", None),
        P(),
        P(),
        P(),
        P(),
        P(None, None, "mp"),
        P("mp", None),
        P(),
        P(),
        P(None, "mp"),
        P("mp", None),
        P(("dp", "mp"), None),
    )
    out_specs = (
        P(("dp", "mp"), None),
        P("dp", None, "mp"),
        P(None, None, ("dp", "mp")),
        P(None, ("dp", "mp")),
        P(("dp", "mp")),
        P("dp", None, "mp"),
        P("mp", "dp"),
        P("mp", "dp"),
        P(None, ("dp", "mp")),
        P(("dp", "mp")),
        P(("dp", "mp")),
        P("dp", None, "mp"),
        P("mp", "dp"),
        P(("dp", "mp")),
        P(("dp", "mp")),
        P("dp", "mp"),
        P("mp", "dp"),
    )
    step = functools.partial(body, mesh.shape["dp"], mesh.shape["mp"])
    return jax.shard_map(step, mesh=mesh, in_specs=in_specs, out_specs=out_specs, check_vma=False)
```

```python
import functools
import types

import jax
import jax.numpy as jnp
from jax import lax
from jax.experimental import pallas as pl
from jax.experimental.pallas import tpu as pltpu
from jax.sharding import PartitionSpec as P

HEAD_DIM = 64
LANES = 128
EPS = 1e-05
SCALE = HEAD_DIM ** (-0.5)
HIGH = lax.Precision.HIGHEST
F32 = jnp.float32
BF16 = jnp.bfloat16
VMEM = pl.BlockSpec(memory_space=pltpu.VMEM)
SMEM = pl.BlockSpec(memory_space=pltpu.SMEM)
ANY = pl.BlockSpec(memory_space=pl.ANY)
HBM = pl.BlockSpec(memory_space=pltpu.HBM)
MIB = 1024 * 1024
FIRST_LIMIT = 60
PIECES = 2
AXES = ((0, 1, 2), (1, 2, 0), (0, 1, 2), (0, 1, 2), (1, 0, 2))
ORDER = (
    "mix_a", "mix_b", "first_a", "first_b", "base", "norm_a", "proj", "norm_b", "attend_a", "second_a", "cot",
    "attend_b", "hidden_a", "second_b", "two_a", "mlp_a", "two_b", "hidden_b", "third_a", "mlp_b", "down_1",
    "up_1", "third_b", "mid_a", "back_a", "mid_b", "back_b", "attn_1", "back_c", "fourth_a", "down_2",
    "weights", "fourth_b", "up_2", "in_a", "in_b", "mix_1", "mass_1", "down_3", "attn_2", "mass_2", "up_3",
    "field_1", "mass_3", "rows_1", "down_4", "up_4", "rows_2", "mix_2", "attn_3", "finish", "tables_1",
    "mix_3", "attn_4", "rows_3", "field_2", "tables_2", "mix_4",
)
COSTS = {
    "two_a": 1,
    "two_b": 0.3,
    "mlp_b": 12,
    "mid_a": 1,
    "up_2": 1,
    "in_a": 0.5,
    "down_3": 2,
    "up_3": 1,
    "tables_1": 1,
    "weights": 5,
}


def dot(left, right, left_dim=1, right_dim=0, precision=None):
    return lax.dot_general(
        left,
        right,
        (((left_dim,), (right_dim,)), ((), ())),
        precision=precision,
        preferred_element_type=F32,
    )


class Rows:
    def __init__(self, refs):
        self.refs = refs
        self.shape = (sum(ref.shape[0] for ref in refs),) + refs[0].shape[1:]

    def __getitem__(self, at):
        return jnp.concatenate([ref[at] for ref in self.refs], axis=0)

    def __setitem__(self, at, value):
        step = self.refs[0].shape[0]
        for i, ref in enumerate(self.refs):
            ref[...] = value[i * step : (i + 1) * step]


def gather_refs(refs, counts):
    refs, grouped = list(refs), []
    for count in counts:
        grouped.append(refs.pop(0) if count is None else Rows([refs.pop(0) for _ in range(count)]))
    return grouped


def flat(items):
    out, counts = [], []
    for item in items:
        pieces = isinstance(item, list)
        out.extend(item if pieces else [item])
        counts.append(len(item) if pieces else None)
    return out, counts


def launch(kernel, outs, args, fetch=(), smem=(), after=(), limit=24, scratch=(), cost=0.1, name=None, lazy=False):
    fetch = [item if isinstance(item, tuple) else (item, item.shape, None) for item in fetch]
    args, arg_counts = flat(args)
    outs, out_counts = flat(outs)
    count = len(smem)

    def run(*refs):
        at = count + len(fetch)
        sources, rest = refs[count:at], refs[at:]
        inputs, rest = gather_refs(rest[: len(args)], arg_counts), rest[len(args) + len(after) :]
        results, rest = gather_refs(rest[: len(outs)], out_counts), rest[len(outs) :]
        if not fetch:
            kernel(*refs[:count], *inputs, *results, *rest)
            return
        *rest, marks = rest
        rest, places = rest[: len(rest) - len(fetch)], rest[len(rest) - len(fetch) :]
        copies = []
        for i, (_, _, pick) in enumerate(fetch):
            source = sources[i] if pick is None else pick(sources[i])
            copies.append(pltpu.make_async_copy(source, places[i], marks.at[i]))
        for copy in copies:
            copy.start()
        if lazy:
            kernel([copy.wait for copy in copies], *refs[:count], *places, *inputs, *results, *rest)
            return
        for copy in copies:
            copy.wait()
        kernel(*refs[:count], *places, *inputs, *results, *rest)

    places = [
        (pltpu.SMEM if array.dtype == jnp.int32 else pltpu.VMEM)(shape, array.dtype)
        for array, shape, _ in fetch
    ]
    marks = [pltpu.SemaphoreType.DMA((len(fetch),))] if fetch else []
    results = pl.pallas_call(
        run,
        out_shape=[jax.ShapeDtypeStruct(shape, kind) for shape, kind in outs],
        in_specs=[SMEM] * count + [HBM] * len(fetch) + [VMEM] * len(args) + [ANY] * len(after),
        out_specs=[VMEM] * len(outs),
        scratch_shapes=list(scratch) + places + marks,
        name=name,
        compiler_params=pltpu.CompilerParams(vmem_limit_bytes=limit * MIB),
        cost_estimate=pl.CostEstimate(
            flops=int(cost * 1e9), bytes_accessed=0, transcendentals=0
        ),
    )(*smem, *(array for array, _, _ in fetch), *args, *after)
    results, grouped = list(results), []
    for pieces in out_counts:
        grouped.append(results.pop(0) if pieces is None else [results.pop(0) for _ in range(pieces)])
    return grouped


def marked(kernel, *refs):
    *rest, mark_ref = refs
    mark_ref[...] = jnp.zeros_like(mark_ref)
    kernel(*rest)


def my_bit(bit):
    return (lax.axis_index("dp") // bit) % 2


def my_core():
    return lax.axis_index("mp") % 2


def my_chip():
    return lax.axis_index("mp") // 2


def iota(shape, dim):
    return lax.broadcasted_iota(jnp.int32, shape, dim)


def exact(mask):
    return mask.astype(F32).astype(BF16)


def lanes_of(rows, head):
    lane = iota((1, rows.shape[1]), 1)
    mine = (lane >= head * HEAD_DIM) & (lane < (head + 1) * HEAD_DIM)
    return jnp.where(mine, rows, jnp.zeros_like(rows))


def spread(rows, pixels, top, bottom):
    variables = top.shape[0]
    parts = [top * rows[p * variables : (p + 1) * variables] for p in range(pixels)]
    parts.append(top)
    if bottom:
        parts.append(jnp.zeros((bottom, top.shape[1]), top.dtype))
    return jnp.concatenate(parts, axis=0)


def pixel_major(channels, pixels):
    variables = channels // pixels
    row = iota((channels, channels), 0)
    major = jnp.zeros((channels, channels), jnp.int32)
    for p in range(pixels):
        inside = (row >= p * variables) & (row < (p + 1) * variables)
        major = jnp.where(inside, (row - p * variables) * pixels + p, major)
    return exact(iota((channels, channels), 1) == major)


def places(ids_ref, variables, pixels):
    channels = variables * pixels
    channel = iota((1, channels), 1)
    place = jnp.zeros((1, channels), jnp.int32)
    for v in range(variables):
        pixel = channel - v * pixels
        inside = (pixel >= 0) & (pixel < pixels)
        place = jnp.where(inside, pixel * variables + ids_ref[v], place)
    return place


def mix_forward(
    pixels,
    quarter,
    waits,
    ids_ref,
    x_ref,
    patch_ref,
    variable_ref,
    w_ref,
    query_ref,
    mixed_ref,
    xt_ref,
    probs_ref,
    values_ref,
    keys_t_ref,
    score_ref,
    query_col_ref,
    table_ref,
):
    channels = x_ref.shape[1]
    variables = channels // pixels
    rows, model_width = table_ref.shape
    width = w_ref.shape[2]
    heads = width // HEAD_DIM
    bottom = rows - channels - variables
    wait_ids, wait_field, wait_patch, wait_variable, wait_weights, wait_query = waits
    wait_patch()
    flat = patch_ref[...].reshape(channels, model_width)
    table_ref[0:channels] = dot(pixel_major(channels, pixels), flat).astype(BF16)
    wait_variable()
    table_ref[channels : channels + variables] = variable_ref[...]
    if bottom:
        table_ref[channels + variables :] = jnp.zeros((bottom, model_width), BF16)
    wait_ids()
    pick = (iota((channels, channels), 0) == places(ids_ref, variables, pixels)).astype(F32)
    wait_field()
    core = my_core()
    starts = [core, 1 - core, core + 2, 3 - core]
    field = jnp.concatenate(
        [x_ref[0, :, pl.ds(pl.multiple_of(s * quarter, LANES), quarter)] for s in starts], axis=1
    )
    xt = dot(pick.astype(BF16), field)
    xt_ref[...] = xt.astype(BF16)
    wait_weights()
    wait_query()
    query_rows = jnp.broadcast_to(query_ref[...].astype(F32)[None], (16, model_width)).astype(BF16)
    query = dot(query_rows, w_ref[0])[0:1].astype(BF16).astype(F32)
    table = table_ref[...]
    keys = dot(table, w_ref[1])
    values = dot(table, w_ref[2])
    values_ref[...] = values.astype(BF16)
    keys_t_ref[...] = keys.T
    query_col_ref[...] = jnp.broadcast_to(query, (LANES, width)).T
    lane = iota((width, LANES), 1) * HEAD_DIM
    row = iota((width, LANES), 0)
    same = ((row >= lane) & (row < lane + HEAD_DIM)).astype(F32)
    score = dot(keys * query, same, precision=HIGH) * SCALE
    score_ref[...] = score
    values_t = values.T.astype(BF16)
    for head in range(heads):
        column = score[:, head : head + 1]
        logits = jnp.broadcast_to(column[channels : channels + variables], (variables, xt.shape[1]))
        for p in range(pixels):
            part = slice(p * variables, (p + 1) * variables)
            logits = logits + column[part] * xt[part]
        weights = jnp.exp(logits - jnp.max(logits, axis=0, keepdims=True))
        probs = weights / jnp.sum(weights, axis=0, keepdims=True)
        probs_ref[head * variables : (head + 1) * variables] = probs
        low = probs.astype(BF16).astype(F32)
        mixing = spread(xt, pixels, low, bottom).astype(BF16)
        part = slice(head * HEAD_DIM, (head + 1) * HEAD_DIM)
        mixed_ref[part] = dot(values_t[part], mixing).astype(BF16)


def mix_out(mixed_ref, w_out_ref, send_a_ref, send_b_ref, keep_a_ref, keep_b_ref):
    quarter = keep_a_ref.shape[0]
    out = dot(mixed_ref[...], w_out_ref[...], 0, 0)
    keep_a_ref[...] = out[0:quarter]
    send_a_ref[...] = out[quarter : 2 * quarter].astype(BF16)
    keep_b_ref[...] = out[2 * quarter : 3 * quarter]
    send_b_ref[...] = out[3 * quarter :].astype(BF16)


def pack_mass(mass, bias, packed_ref):
    width = mass.shape[0]
    high = bias.astype(BF16).astype(F32)
    packed_ref[0:width] = mass.astype(BF16)
    packed_ref[width:] = jnp.concatenate([high, bias - high], axis=0).astype(BF16)


def add_mass(mass_ref, bias_ref, got_ref):
    width = mass_ref.shape[0]
    more = got_ref[width:].astype(F32)
    return mass_ref[...] + got_ref[0:width].astype(F32), bias_ref[...] + more[0:8] + more[8:16]


def mix_backward(
    pixels,
    pick_ref,
    xt_ref,
    probs_ref,
    values_ref,
    score_ref,
    w_out_ref,
    a0_ref,
    a1_ref,
    b0_ref,
    b1_ref,
    packed_ref,
    mass_ref,
    bias_ref,
    field_send_ref,
    field_keep_ref,
):
    channels, length = xt_ref.shape
    variables = channels // pixels
    rows, width = values_ref.shape
    heads = width // HEAD_DIM
    bottom = rows - channels - variables
    quarter = length // 4
    xt = xt_ref[...].astype(F32)
    grad = jnp.concatenate([a0_ref[...], a1_ref[...], b0_ref[...], b1_ref[...]], axis=0)
    grad_t = dot(w_out_ref[...], grad, 1, 1).astype(BF16)
    values = values_ref[...]
    score = score_ref[...]
    field = jnp.zeros(xt.shape, F32)
    lane = iota((rows, LANES), 1)
    sums = jnp.zeros((rows, LANES), F32)
    for head in range(heads):
        probs = probs_ref[head * variables : (head + 1) * variables]
        low = probs.astype(BF16).astype(F32)
        back = dot(lanes_of(values, head), grad_t)
        prob_grad = back[channels : channels + variables]
        for p in range(pixels):
            part = slice(p * variables, (p + 1) * variables)
            prob_grad = prob_grad + xt[part] * back[part]
        middle = jnp.sum(probs * prob_grad, axis=0, keepdims=True)
        score_grad = probs * (prob_grad - middle)
        column = score[:, head : head + 1]
        field = field + jnp.concatenate(
            [
                score_grad * column[p * variables : (p + 1) * variables]
                + low * back[p * variables : (p + 1) * variables]
                for p in range(pixels)
            ],
            axis=0,
        )
        spreading = spread(xt, pixels, score_grad * SCALE, bottom)
        sums = jnp.where(lane == head, jnp.sum(spreading, axis=1, keepdims=True), sums)
        mixing = spread(xt, pixels, low, bottom).astype(BF16)
        part = slice(head * HEAD_DIM, (head + 1) * HEAD_DIM)
        mass_ref[part] = dot(grad_t[part], mixing, 1, 1)
    bias_ref[...] = sums.T[0:8]
    pack_mass(mass_ref[...], bias_ref[...], packed_ref)
    field = dot(pick_ref[...], field.astype(BF16))
    field_keep_ref[:, 0:quarter] = field[:, 0:quarter]
    field_keep_ref[:, quarter:] = field[:, 2 * quarter : 3 * quarter]
    field_send_ref[:, 0:quarter] = field[:, quarter : 2 * quarter].astype(BF16)
    field_send_ref[:, quarter:] = field[:, 3 * quarter :].astype(BF16)


def norm_forward(*refs):
    *terms, gain_ref, bias_ref, out_ref, low_ref = refs
    total = terms[0][...].astype(F32)
    for term in terms[1:]:
        total = total + term[...].astype(F32)
    out_ref[...] = total
    centered = total - jnp.mean(total, axis=1, keepdims=True)
    inv_std = lax.rsqrt(jnp.mean(centered * centered, axis=1, keepdims=True) + EPS)
    low_ref[...] = (centered * inv_std * gain_ref[...] + bias_ref[...]).astype(BF16)


def norm_relay(pass_ref, *refs):
    *refs, out_ref = refs
    out_ref[...] = pass_ref[...]
    norm_forward(*refs)


def norm_backward(with_sum, add_refs, *refs):
    keep_ref, far_ref, rows_ref, gain_ref, above_ref = refs[:5]
    more = refs[5 : 5 + add_refs]
    out_ref, low_ref, sums_ref = refs[5 + add_refs :]
    grad = keep_ref[...] + far_ref[...].astype(F32)
    rows = rows_ref[...]
    centered = rows - jnp.mean(rows, axis=1, keepdims=True)
    inv_std = lax.rsqrt(jnp.mean(centered * centered, axis=1, keepdims=True) + EPS)
    normed = centered * inv_std
    scaled = grad * gain_ref[...]
    first = jnp.mean(scaled, axis=1, keepdims=True)
    second = jnp.mean(scaled * normed, axis=1, keepdims=True)
    out = above_ref[...].astype(F32) + inv_std * (scaled - first - normed * second)
    out_ref[...] = out
    low_ref[...] = out.astype(BF16)
    lines = [
        jnp.sum(grad * normed, axis=0, keepdims=True),
        jnp.sum(grad, axis=0, keepdims=True),
    ]
    lines.append(jnp.sum(out, axis=0, keepdims=True) if with_sum else jnp.zeros_like(lines[0]))
    if add_refs:
        one, two_a, two_b = (ref[...] for ref in more)
        lines = [
            lines[0] + one[0:1],
            lines[1] + one[1:2],
            two_a[0:1] + two_b[0:1],
            two_a[1:2] + two_b[1:2],
            lines[2] + one[2:3],
        ]
    lines.append(jnp.zeros((8 - len(lines), grad.shape[1]), F32))
    sums_ref[...] = jnp.concatenate(lines, axis=0)


def project(own_ref, near_ref, w_ref, out_ref):
    rows = jnp.concatenate([own_ref[...], near_ref[...]], axis=0)
    for i in range(3):
        out_ref[i] = dot(rows, w_ref[i]).astype(BF16)


def attend(query, keys, values_t, logs_ref):
    scaled = (query.astype(F32) * SCALE).astype(BF16)
    parts = []
    for head in range(keys.shape[1] // HEAD_DIM):
        scores = dot(lanes_of(keys, head), scaled, 1, 1)
        top = jnp.max(scores, axis=0, keepdims=True)
        weights = jnp.exp(scores - top)
        total = jnp.sum(weights, axis=0, keepdims=True)
        logs_ref[head : head + 1] = top + jnp.log(total)
        probs = (weights * (1.0 / total)).astype(BF16)
        parts.append(dot(values_t[head * HEAD_DIM : (head + 1) * HEAD_DIM], probs))
    return jnp.concatenate(parts, axis=0).T.astype(BF16)


def split_out(out, keep_ref, send_ref):
    quarter = out.shape[0] // 2
    keep_ref[...] = out[:quarter]
    send_ref[...] = out[quarter:].astype(BF16)


def attend_first(own_ref, near_ref, w_ref, first_ref, w_out_ref, second_ref, out_ref, logs_ref, keep_ref, send_ref):
    project(own_ref, near_ref, w_ref, second_ref)
    keys = jnp.concatenate([first_ref[1], second_ref[1]], axis=0)
    values = jnp.concatenate([first_ref[2], second_ref[2]], axis=0)
    out_ref[...] = attend(first_ref[0], keys, values.astype(F32).T.astype(BF16), logs_ref)
    split_out(dot(out_ref[...], w_out_ref[...]), keep_ref, send_ref)


def attend_second(first_ref, second_ref, w_out_ref, out_ref, logs_ref, keep_ref, send_ref):
    keys = jnp.concatenate([first_ref[1], second_ref[1]], axis=0)
    values = jnp.concatenate([first_ref[2], second_ref[2]], axis=0)
    out_ref[...] = attend(second_ref[0], keys, values.astype(F32).T.astype(BF16), logs_ref)
    split_out(dot(out_ref[...], w_out_ref[...]), keep_ref, send_ref)


def attend_grad(grad, query, keys, values, logs_ref):
    scaled = (query.astype(F32) * SCALE).astype(BF16)
    keys_t = keys.astype(F32).T.astype(BF16)
    query_parts = []
    key_grad = jnp.zeros(keys.shape, F32)
    value_grad = jnp.zeros(keys.shape, F32)
    for head in range(keys.shape[1] // HEAD_DIM):
        scores = dot(lanes_of(keys, head), scaled, 1, 1)
        probs = jnp.exp(scores - logs_ref[head : head + 1])
        prob_grad = dot(lanes_of(values, head), grad, 1, 1)
        middle = jnp.sum(probs * prob_grad, axis=0, keepdims=True)
        score_grad = (probs * (prob_grad - middle)).astype(BF16)
        query_parts.append(dot(keys_t[head * HEAD_DIM : (head + 1) * HEAD_DIM], score_grad))
        key_grad = key_grad + dot(score_grad, lanes_of(scaled, head))
        value_grad = value_grad + dot(probs.astype(BF16), lanes_of(grad, head))
    query_grad = (jnp.concatenate(query_parts, axis=0).T * SCALE).astype(BF16)
    return query_grad, key_grad, value_grad


def attend_back_first(own_ref, near_ref, w_out_ref, first_ref, second_ref, logs_ref, query_ref, key_ref, value_ref):
    rows = jnp.concatenate([own_ref[...], near_ref[...]], axis=0)
    grad = dot(rows, w_out_ref[...], 1, 1).astype(BF16)
    keys = jnp.concatenate([first_ref[1], second_ref[1]], axis=0)
    values = jnp.concatenate([first_ref[2], second_ref[2]], axis=0)
    query_ref[...], key_ref[...], value_ref[...] = attend_grad(
        grad, first_ref[0], keys, values, logs_ref
    )


def project_back(rows_ref, start, count, w_ref):
    total = dot(rows_ref[0, start : start + count], w_ref[0], 1, 1)
    for i in range(1, 3):
        total = total + dot(rows_ref[i, start : start + count], w_ref[i], 1, 1)
    return total


def attend_back_second(
    own_ref,
    near_ref,
    w_out_ref,
    first_ref,
    second_ref,
    logs_ref,
    query_ref,
    key_ref,
    value_ref,
    w_ref,
    out_ref,
    keep_ref,
    send_ref,
):
    rows = jnp.concatenate([own_ref[...], near_ref[...]], axis=0)
    half = rows.shape[0]
    grad = dot(rows, w_out_ref[...], 1, 1).astype(BF16)
    keys = jnp.concatenate([first_ref[1], second_ref[1]], axis=0)
    values = jnp.concatenate([first_ref[2], second_ref[2]], axis=0)
    query_grad, key_grad, value_grad = attend_grad(grad, second_ref[0], keys, values, logs_ref)
    out_ref[0, 0:half] = query_ref[...]
    out_ref[0, half:] = query_grad
    out_ref[1] = (key_ref[...] + key_grad).astype(BF16)
    out_ref[2] = (value_ref[...] + value_grad).astype(BF16)
    split_out(project_back(out_ref, 0, half, w_ref), keep_ref, send_ref)


def attend_back_last(rows_ref, w_ref, keep_ref, send_ref):
    half = rows_ref.shape[1] // 2
    split_out(project_back(rows_ref, half, half, w_ref), keep_ref, send_ref)


def hidden_back(own_ref, near_ref, w_ref, out_ref):
    rows = jnp.concatenate([own_ref[...], near_ref[...]], axis=0)
    out_ref[...] = dot(rows, w_ref[...], 1, 1)


ROOT = 0.7978845608028654
CUBE = 0.044715


def mlp(own_ref, near_ref, w_ref, grad_ref, hidden_ref, out_ref, keep_ref, send_ref):
    rows = jnp.concatenate([own_ref[...], near_ref[...]], axis=0)
    pre = dot(rows, w_ref[...])
    square = pre * pre
    bend = jnp.tanh(ROOT * pre * (1.0 + CUBE * square))
    half = 0.5 * (1.0 + bend)
    hidden_ref[...] = (pre * half).astype(BF16)
    slope = half + (0.5 * ROOT) * pre * (1.0 - bend * bend) * (1.0 + (3.0 * CUBE) * square)
    out_ref[...] = (slope * grad_ref[...]).astype(BF16)
    split_out(dot(out_ref[...], w_ref[...], 1, 1), keep_ref, send_ref)


def mlp_out(first_ref, second_ref, w_ref, keep_a_ref, send_a_ref, keep_b_ref, send_b_ref):
    split_out(dot(first_ref[...], w_ref[...]), keep_a_ref, send_a_ref)
    split_out(dot(second_ref[...], w_ref[...]), keep_b_ref, send_b_ref)


def grad_rows(parts, step, width, which):
    groups = width // (2 * step)
    outs = []
    for group in range(groups):
        start = pl.multiple_of((2 * group + which) * step, LANES)
        line = []
        for left, rights in parts:
            picked = jnp.concatenate([ref[:, pl.ds(start, step)] for ref in left], axis=0)
            line.extend(dot(picked, right, 0, 0) for right in rights)
        outs.append(line)
    return outs, groups


def write_half(ref, parts, step, width, which, dtype):
    outs, groups = grad_rows(parts, step, width, which)
    for group in range(groups):
        column = 0
        for value in outs[group]:
            ref[group * step : (group + 1) * step, column : column + value.shape[1]] = value.astype(dtype)
            column += value.shape[1]


def take_half(out_ref, source, step, which, dtype):
    for group in range(source.shape[0] // (2 * step)):
        start = pl.multiple_of((2 * group + which) * step, 16)
        out_ref[group * step : (group + 1) * step] = source[pl.ds(start, step)].astype(dtype)


def sum_start(load, step, bit, *refs):
    *inputs, out_ref = refs
    parts, width = load(inputs)
    write_half(out_ref, parts, step, width, 1 - my_bit(bit), BF16)


def sum_second(load, step, next_step, bit, next_bit, *refs):
    got_ref, *inputs, keep_ref, send_ref, total = refs
    parts, width = load(inputs)
    write_half(total, parts, step, width, my_bit(bit), F32)
    total[...] = total[...] + got_ref[...].astype(F32)
    take_half(send_ref, total, next_step, 1 - my_bit(next_bit), BF16)
    take_half(keep_ref, total, next_step, my_bit(next_bit), F32)


def sum_next(next_step, next_bit, kept_ref, got_ref, keep_ref, send_ref, total):
    total[...] = kept_ref[...] + got_ref[...].astype(F32)
    take_half(send_ref, total, next_step, 1 - my_bit(next_bit), BF16)
    take_half(keep_ref, total, next_step, my_bit(next_bit), F32)


def load_plain(inputs):
    *left, first, second = inputs
    right = jnp.concatenate([first[...], second[...]], axis=0)
    return [(left, [right])], left[0].shape[1]


def load_attn(inputs):
    left, middle = inputs[0:4], inputs[4:8]
    proj, first, second = inputs[8:]
    attended = jnp.concatenate([first[...], second[...]], axis=0)
    return [(left, [proj[0], proj[1], proj[2]]), (middle, [attended])], left[0].shape[1]


def last_plain(kept_ref, got_ref, out_ref):
    out_ref[...] = kept_ref[...] + got_ref[...].astype(F32)


def last_turned(kept_ref, got_ref, out_ref):
    out_ref[...] = (kept_ref[...] + got_ref[...].astype(F32)).T


def last_attn(kept_ref, got_ref, proj_ref, out_ref):
    total = kept_ref[...] + got_ref[...].astype(F32)
    width = proj_ref.shape[2]
    for i in range(3):
        proj_ref[i] = total[:, i * width : (i + 1) * width]
    out_ref[...] = total[:, 3 * width :].T


def mix_lines(samples, lines, bucket_ref, inputs, rest_ref):
    first_ref, second_ref, own_ref, near_ref = inputs
    quarter, width = first_ref.shape
    rest_ref[0:quarter] = jnp.where(my_chip() == 0, first_ref[...], second_ref[...])
    sample = lax.axis_index("dp")
    sums = own_ref[...] + near_ref[...]
    row = iota((lines, width), 0)
    filled = jnp.concatenate([sums, jnp.zeros((lines - 8, width), F32)], axis=0)
    filled = jnp.where(row < 4, filled, 0.0)
    filled = jnp.where(row == 4 + sample, sums[4:5], filled)
    bucket = bucket_ref[0].astype(F32)
    rest_ref[quarter:] = jnp.where(row == 4 + samples + sample, bucket, filled)


def write_mix(ref, step, which, left, mixed_ref, rest_ref, dtype):
    width = left[0].shape[1]
    heads_width = mixed_ref.shape[0]
    for group in range(width // (2 * step)):
        start = pl.multiple_of((2 * group + which) * step, LANES)
        picked = jnp.concatenate([part[:, pl.ds(start, step)] for part in left], axis=0)
        rows = slice(group * step, (group + 1) * step)
        ref[rows, 0:heads_width] = dot(picked, mixed_ref[...], 0, 1).astype(dtype)
        ref[rows, heads_width:] = rest_ref[:, pl.ds(start, step)].T.astype(dtype)


def mix_start(samples, lines, step, bit, bucket_ref, mixed_ref, *refs):
    *inputs, out_ref, rest = refs
    mix_lines(samples, lines, bucket_ref, inputs[4:], rest)
    write_mix(out_ref, step, 1 - my_bit(bit), inputs[:4], mixed_ref, rest, BF16)


def mix_second(samples, lines, step, next_step, bit, next_bit, bucket_ref, mixed_ref, *refs):
    got_ref, *inputs, keep_ref, send_ref, rest, total = refs
    mix_lines(samples, lines, bucket_ref, inputs[4:], rest)
    write_mix(total, step, my_bit(bit), inputs[:4], mixed_ref, rest, F32)
    total[...] = total[...] + got_ref[...].astype(F32)
    take_half(send_ref, total, next_step, 1 - my_bit(next_bit), BF16)
    take_half(keep_ref, total, next_step, my_bit(next_bit), F32)


def mix_last(samples, quarter, final, kept_ref, got_ref, out_ref, pos_ref, lead_ref, small_ref):
    total = kept_ref[...] + got_ref[...].astype(F32)
    heads_width = out_ref.shape[0]
    out_ref[...] = total[:, :heads_width].T
    pos_ref[...] = total[:, heads_width : heads_width + quarter].T
    rest = total[:, heads_width + quarter :]
    rows = max(final, 8)
    mine = iota((rows, rest.shape[0]), 1) == iota((rows, rest.shape[0]), 0) + lax.axis_index("mp") * final
    own = dot(mine.astype(F32), rest, precision=HIGH)
    bucket = iota((rows, lead_ref.shape[1]), 1).astype(F32)
    lead = jnp.zeros(bucket.shape, F32)
    for s in range(samples):
        mark = own[:, 4 + samples + s : 5 + samples + s]
        lead = jnp.where(bucket == mark, lead + own[:, 4 + s : 5 + s], lead)
    lead_ref[...] = lead[:final]
    small_ref[...] = own.T[0:8, :final]


def mass_add(mass_ref, bias_ref, got_ref, packed_ref, mass_out_ref, bias_out_ref):
    mass, bias = add_mass(mass_ref, bias_ref, got_ref)
    mass_out_ref[...] = mass
    bias_out_ref[...] = bias
    pack_mass(mass, bias, packed_ref)


def mix_finish(
    pixels,
    query_col_ref,
    keys_t_ref,
    patch_ref,
    variable_ref,
    mass_ref,
    bias_ref,
    got_ref,
    w_ref,
    query_ref,
    keep_ref,
    send_ref,
    grad_ref,
    scratch,
):
    width, rows = mass_ref.shape
    heads = width // HEAD_DIM
    mass, sums = add_mass(mass_ref, bias_ref, got_ref)
    mass = mass.astype(BF16)
    bias = jnp.concatenate(
        [jnp.broadcast_to(sums[head : head + 1], (HEAD_DIM, rows)) for head in range(heads)], axis=0
    )
    key_mass = (bias * query_col_ref[:, 0:1]).astype(BF16)
    total = jnp.sum(keys_t_ref[...] * bias, axis=1, keepdims=True)
    own = grad_ref.shape[1]
    start = lax.axis_index("dp") * own
    model_width = variable_ref.shape[1]
    channels = patch_ref.shape[0] * pixels
    mine = exact(iota((own, model_width), 1) == iota((own, model_width), 0) + start)
    total_row = jnp.broadcast_to(total, (width, LANES)).T[0:1]
    flat = patch_ref[...].reshape(channels, model_width)
    patch_t = dot(mine, flat, 1, 1).astype(BF16)
    patch_t = dot(patch_t, pixel_major(channels, pixels), 1, 1)
    variable_t = dot(mine, variable_ref[...], 1, 1)
    bottom = rows - channels - variable_ref.shape[0]
    table_t = jnp.concatenate([patch_t, variable_t, jnp.zeros((own, bottom), F32)], axis=1).astype(BF16)
    query_rows = jnp.broadcast_to(query_ref[...].astype(F32)[None], (16, model_width)).astype(BF16)
    grad_ref[0] = dot(mine, query_rows, 1, 1)[:, 0:1] * total_row
    grad_ref[1] = dot(table_t, key_mass, 1, 1)
    grad_ref[2] = dot(table_t, mass, 1, 1)
    back = dot(w_ref[1], key_mass) + dot(w_ref[2], mass)
    query_back = jnp.sum(w_ref[0].astype(F32) * total_row, axis=1, keepdims=True)
    scratch[...] = jnp.where(iota((own, rows), 1) == rows - 1, query_back, back)
    keep_part(scratch, keep_ref, send_ref, my_chip())


def keep_part(source, keep_ref, send_ref, which):
    step = keep_ref.shape[0]
    if step % 8:
        first, second = source[0:step], source[step : 2 * step]
        keep_ref[...] = jnp.where(which == 0, first, second)
        send_ref[...] = jnp.where(which == 0, second, first)
    else:
        keep_ref[...] = source[pl.ds(pl.multiple_of(which * step, 8), step)]
        send_ref[...] = source[pl.ds(pl.multiple_of((1 - which) * step, 8), step)]


def tables_next(kept_ref, got_ref, keep_ref, send_ref, scratch):
    scratch[...] = kept_ref[...] + got_ref[...]
    keep_part(scratch, keep_ref, send_ref, my_core())


def pair_sum(keep_ref, got_ref, out_ref, low_ref):
    total = keep_ref[...] + got_ref[...].astype(F32)
    out_ref[...] = total
    low_ref[...] = total.astype(BF16)


def take_rows(source_ref, out_ref):
    out_ref[...] = source_ref[...]


def take_weights(pixels, ids_ref, source_ref, out_ref, pick_ref):
    out_ref[...] = source_ref[...]
    channels = pick_ref.shape[0]
    pick = iota((channels, channels), 0) == places(ids_ref, channels // pixels, pixels)
    pick_ref[...] = pick.astype(F32).T.astype(BF16)


def by_chip(own_ref, far_ref, first_ref, second_ref):
    own, far = own_ref[...], far_ref[...]
    first = my_chip() == 0
    first_ref[...] = jnp.where(first, own, far)
    second_ref[...] = jnp.where(first, far, own)


def base_rows(bucket_ref, first_ref, second_ref, lead_ref, out_a_ref, out_b_ref):
    rows = lead_ref.shape[0]
    mark = exact(iota((16, rows), 1) == bucket_ref[0])
    lead = dot(mark, lead_ref[...])[0:1]
    out_a_ref[...] = first_ref[...].astype(F32) + lead
    out_b_ref[...] = second_ref[...].astype(F32) + lead


def field_sum(keep_ref, got_ref, own_ref, send_ref):
    total = keep_ref[...] + got_ref[...].astype(F32)
    quarter = own_ref.shape[1]
    first = my_chip() == 0
    own_ref[...] = jnp.where(first, total[:, :quarter], total[:, quarter:])
    send_ref[...] = jnp.where(first, total[:, quarter:], total[:, :quarter]).astype(BF16)


def field_last(own_ref, far_ref, out_ref):
    out_ref[0] = own_ref[...] + far_ref[...].astype(F32)


def rows_sum(keep_a_ref, got_a_ref, keep_b_ref, got_b_ref, mid_a_ref, mid_b_ref, own_ref, send_ref):
    part_a = keep_a_ref[...] + got_a_ref[...].astype(F32)
    part_b = keep_b_ref[...] + got_b_ref[...].astype(F32)
    first = my_chip() == 0
    own_ref[...] = jnp.where(first, part_a + mid_a_ref[...], part_b + mid_b_ref[...])
    send_ref[...] = jnp.where(first, part_b, part_a).astype(BF16)


def tables_last(pixels, variables, kept_ref, got_ref, patch_ref, variable_ref, query_ref):
    total = kept_ref[...] + got_ref[...]
    for p in range(pixels):
        patch_ref[p] = total[:, p * variables : (p + 1) * variables]
    variable_ref[...] = total[:, pixels * variables : (pixels + 1) * variables]
    query_ref[...] = total.T[total.shape[1] - 8 :]


def pairs(count, bit):
    return [(i, i ^ bit) for i in range(count)]


def body(
    mesh_dp,
    mesh_mp,
    input_field,
    variable_ids,
    lead_bucket,
    patch_table,
    variable_table,
    variable_query,
    mix_weights,
    mix_output,
    pos_table,
    lead_table,
    first_gain,
    first_bias,
    attn_weights,
    attn_output,
    second_gain,
    second_bias,
    up_weight,
    down_weight,
    cotangent,
):
    length = input_field.shape[2]
    channels = input_field.shape[1]
    variables = variable_ids.shape[0]
    pixels = channels // variables
    model_width = pos_table.shape[1]
    quarter = cotangent.shape[0]
    head_width = mix_weights.shape[2]
    hidden_width = up_weight.shape[1]
    heads = head_width // HEAD_DIM
    own_width = model_width // mesh_dp
    half = 2 * quarter
    latest, now = [], []
    v = types.SimpleNamespace()

    def call(kernel, outs, args, final=False, **options):
        if final:
            outs = outs + [((8, LANES), F32)]
            kernel = functools.partial(marked, kernel)
        known = flat(args)[0] + list(options.get("fetch", ()))
        after = [last for last in latest if all(last is not arg for arg in known)]
        cost = COSTS.get(now[0], 0.1)
        results = launch(kernel, outs, args, after=after, cost=cost, name=now[0], **options)
        latest[:] = results[-1:] if final else flat(results)[0][:1]
        return results[:-1] if final else results

    rows32 = ((quarter, model_width), F32)
    rows16 = ((quarter, model_width), BF16)
    cut16 = [((quarter // PIECES, model_width), BF16)] * PIECES

    def swap_core(value):
        if isinstance(value, list):
            return [swap_core(piece) for piece in value]
        return lax.ppermute(value, "mp", pairs(mesh_mp, 1))

    def swap_chip(value):
        return lax.ppermute(value, "mp", pairs(mesh_mp, 2))

    def swap_sample(value, bit):
        return lax.ppermute(value, "dp", pairs(mesh_dp, bit))

    def add_near(keep, near):
        kept, low = call(pair_sum, [rows32, rows16], [keep, near])
        return kept, swap_chip(low)

    all_bits = [1 << i for i in range(mesh_dp.bit_length() - 1)]
    wide = [bit for bit in all_bits if bit * own_width % LANES == 0]

    def order_from(axes):
        return [wide[i] for i in axes] + [bit for bit in all_bits if bit not in wide[:3]]

    def steps_of(order):
        left = list(all_bits)
        steps = []
        for bit in order:
            steps.append(own_width << left.index(bit))
            left.remove(bit)
        return steps

    def start_sum(load, inputs, width, order):
        step = steps_of(order)[0]
        (send,) = call(
            functools.partial(sum_start, load, step, order[0]),
            [((model_width // 2, width), BF16)],
            inputs,
        )
        return swap_sample(send, order[0])

    def halves(width, scratch_rows):
        kept = scratch_rows // 2
        return [((kept, width), F32), ((kept, width), BF16)]

    def second_sum(load, inputs, got, width, order):
        steps = steps_of(order)
        rows = model_width // 2
        keep, send = call(
            functools.partial(sum_second, load, steps[0], steps[1], order[0], order[1]),
            halves(width, rows),
            [got] + inputs,
            scratch=[pltpu.VMEM((rows, width), F32)],
        )
        return keep, swap_sample(send, order[1])

    def rest_sum(keep, got, order):
        steps = steps_of(order)
        for i in range(2, len(order)):
            rows, width = keep.shape
            keep, send = call(
                functools.partial(sum_next, steps[i], order[i]),
                halves(width, rows),
                [keep, got],
                scratch=[pltpu.VMEM((rows, width), F32)],
            )
            got = swap_sample(send, order[i])
        return keep, got

    def norm_rows(terms, gain, bias):
        return call(norm_forward, [rows32, cut16], terms + [gain, bias])

    w_mix = mix_weights.transpose(1, 0, 2)
    w_attn = attn_weights.transpose(1, 0, 2)
    gain_one, bias_one = first_gain[None], first_bias[None]
    gain_two, bias_two = second_gain[None], second_bias[None]
    table_rows = channels + variables
    padded = -(-(table_rows + 1) // LANES) * LANES
    lines = -(-(4 + 2 * mesh_dp) // LANES) * LANES
    mix_width = head_width + quarter + lines
    attn_width = 4 * head_width
    final = own_width // mesh_mp
    own_field = (channels, quarter)
    proj_kind = ((3, half, head_width), BF16)
    attend_kinds = [((half, head_width), BF16), ((8, half), F32), rows32, cut16]
    hidden_kind = ((half, hidden_width), F32)
    mlp_kinds = [((half, hidden_width), BF16)] * 2 + [rows32, cut16]
    back_kinds = [rows32, cut16, ((8, model_width), F32)]
    grad_kinds = [((half, head_width), BF16)] + [((length, head_width), F32)] * 2
    mass_kinds = [
        ((head_width + 16, padded), BF16),
        ((head_width, padded), F32),
        ((8, padded), F32),
    ]
    rest_rows = pltpu.VMEM((quarter + lines, model_width), F32)
    down_order, up_order, attn_order, mix_order, mass_bits = map(order_from, AXES)
    mix_steps = steps_of(mix_order)
    back_two = functools.partial(norm_backward, False, 0)

    def mix_a():
        v.mixed_t, v.field_t, v.probs, v.values, v.keys_t, v.score, v.query_col = call(
            functools.partial(mix_forward, pixels, quarter),
            [
                ((head_width, length), BF16),
                ((channels, length), BF16),
                ((heads * variables, length), F32),
                ((padded, head_width), BF16),
                ((head_width, padded), F32),
                ((padded, LANES), F32),
                ((head_width, LANES), F32),
            ],
            [],
            fetch=[variable_ids, input_field, patch_table, variable_table, w_mix, variable_query],
            limit=FIRST_LIMIT,
            lazy=True,
            scratch=[pltpu.VMEM((padded, model_width), BF16)],
        )

    def mix_b():
        send_a, send_b, v.keep_a, v.keep_b = call(
            mix_out, [rows16, rows16, rows32, rows32], [mix_output], fetch=[v.mixed_t]
        )
        v.near_a, v.near_b = swap_core(send_a), swap_core(send_b)

    def first_a():
        v.kept_a, v.far_a = add_near(v.keep_a, v.near_a)

    def first_b():
        v.kept_b, v.far_b = add_near(v.keep_b, v.near_b)

    def second_a():
        first_a()

    def second_b():
        first_b()

    def base():
        blocks = [
            (
                pos_table,
                (quarter, model_width),
                lambda ref, k=k: ref.at[pl.ds((2 * k + my_core()) * quarter, quarter)],
            )
            for k in range(2)
        ]
        v.base_a, v.base_b = call(
            base_rows, [rows32] * 2, [], fetch=blocks + [lead_table], smem=[lead_bucket]
        )

    def norm_a():
        v.in_a, v.one_a0 = norm_rows([v.kept_a, v.far_a, v.base_a], gain_one, bias_one)
        v.one_a1 = swap_core(v.one_a0)

    def proj():
        (v.proj_a,) = call(project, [proj_kind], [v.one_a0, v.one_a1, w_attn])

    def norm_b():
        v.in_b, v.one_b0, v.cot_own = call(
            norm_relay,
            [rows32, cut16, rows16],
            [cotangent, v.kept_b, v.far_b, v.base_b, gain_one, bias_one],
        )
        v.one_b1 = swap_core(v.one_b0)
        v.cot_far = swap_chip(v.cot_own)

    def attend_a():
        v.proj_b, v.attended_a, v.logs_a, v.keep_a, send_a = call(
            attend_first,
            [proj_kind] + attend_kinds,
            [v.one_b0, v.one_b1, w_attn, v.proj_a, attn_output],
        )
        v.near_a = swap_core(send_a)

    def attend_b():
        v.attended_b, v.logs_b, v.keep_b, send_b = call(
            attend_second, attend_kinds, [v.proj_a, v.proj_b, attn_output]
        )
        v.near_b = swap_core(send_b)

    def cot():
        v.cot_a0, v.cot_b0 = call(by_chip, [cut16] * 2, [v.cot_own, v.cot_far])
        v.cot_a1, v.cot_b1 = swap_core(v.cot_a0), swap_core(v.cot_b0)

    def hidden_a():
        (v.grad_hidden_a,) = call(hidden_back, [hidden_kind], [v.cot_a0, v.cot_a1, down_weight])

    def hidden_b():
        (v.grad_hidden_b,) = call(hidden_back, [hidden_kind], [v.cot_b0, v.cot_b1, down_weight])

    def two_a():
        v.mid_a, v.two_a0 = norm_rows([v.kept_a, v.far_a, v.in_a], gain_two, bias_two)
        v.two_a1 = swap_core(v.two_a0)

    def two_b():
        v.mid_b, v.two_b0 = norm_rows([v.kept_b, v.far_b, v.in_b], gain_two, bias_two)
        v.two_b1 = swap_core(v.two_b0)

    def mlp_a():
        v.hidden_a, v.pre_a, v.m_keep_a, send_a = call(
            mlp, mlp_kinds, [v.two_a0, v.two_a1, up_weight, v.grad_hidden_a]
        )
        v.m_near_a = swap_core(send_a)

    def mlp_b():
        v.hidden_b, v.pre_b, v.m_keep_b, send_b = call(
            mlp, mlp_kinds, [v.two_b0, v.two_b1, up_weight, v.grad_hidden_b]
        )
        v.m_near_b = swap_core(send_b)

    def third_a():
        v.m_kept_a, v.m_far_a = add_near(v.m_keep_a, v.m_near_a)

    def third_b():
        v.m_kept_b, v.m_far_b = add_near(v.m_keep_b, v.m_near_b)

    def down_in():
        return [v.cot_a0, v.cot_a1, v.cot_b0, v.cot_b1, v.hidden_a, v.hidden_b]

    def up_in():
        return [v.two_a0, v.two_a1, v.two_b0, v.two_b1, v.pre_a, v.pre_b]

    def attn_in():
        one = [v.one_a0, v.one_a1, v.one_b0, v.one_b1]
        mid = [v.back_a0, v.back_a1, v.back_b0, v.back_b1]
        return one + mid + [v.grad_proj, v.attended_a, v.attended_b]

    def up_1():
        v.up_got = start_sum(load_plain, up_in(), hidden_width, up_order)

    def down_1():
        v.down_got = start_sum(load_plain, down_in(), hidden_width, down_order)

    def attn_1():
        v.attn_got = start_sum(load_attn, attn_in(), attn_width, attn_order)

    def up_2():
        v.up_keep, v.up_got = second_sum(load_plain, up_in(), v.up_got, hidden_width, up_order)

    def down_2():
        v.down_keep, v.down_got = second_sum(
            load_plain, down_in(), v.down_got, hidden_width, down_order
        )

    def attn_2():
        v.attn_keep, v.attn_got = second_sum(
            load_attn, attn_in(), v.attn_got, attn_width, attn_order
        )

    def up_3():
        v.up_keep, v.up_got = rest_sum(v.up_keep, v.up_got, up_order)

    def down_3():
        v.down_keep, v.down_got = rest_sum(v.down_keep, v.down_got, down_order)

    def attn_3():
        v.attn_keep, v.attn_got = rest_sum(v.attn_keep, v.attn_got, attn_order)

    def mid_a():
        v.grad_mid_a, v.back_a0, v.sums_two_a = call(
            back_two, back_kinds, [v.m_kept_a, v.m_far_a, v.mid_a, gain_two, v.cot_a0]
        )
        v.back_a1 = swap_core(v.back_a0)

    def mid_b():
        v.grad_mid_b, v.back_b0, v.sums_two_b = call(
            back_two, back_kinds, [v.m_kept_b, v.m_far_b, v.mid_b, gain_two, v.cot_b0]
        )
        v.back_b1 = swap_core(v.back_b0)

    def back_a():
        v.query_grad, v.key_grad, v.value_grad = call(
            attend_back_first,
            grad_kinds,
            [v.back_a0, v.back_a1, attn_output, v.proj_a, v.proj_b, v.logs_a],
        )

    def back_b():
        v.grad_proj, v.p_keep_a, send_a = call(
            attend_back_second,
            [((3, length, head_width), BF16), rows32, cut16],
            [
                v.back_b0,
                v.back_b1,
                attn_output,
                v.proj_a,
                v.proj_b,
                v.logs_b,
                v.query_grad,
                v.key_grad,
                v.value_grad,
                w_attn,
            ],
        )
        v.p_near_a = swap_core(send_a)

    def back_c():
        v.p_keep_b, send_b = call(attend_back_last, [rows32, cut16], [v.grad_proj, w_attn])
        v.p_near_b = swap_core(send_b)

    def fourth_a():
        v.p_kept_a, v.p_far_a = add_near(v.p_keep_a, v.p_near_a)

    def fourth_b():
        v.p_kept_b, v.p_far_b = add_near(v.p_keep_b, v.p_near_b)

    def in_a():
        v.grad_in_a, v.in_a0, v.sums_one_a = call(
            functools.partial(norm_backward, True, 0),
            back_kinds,
            [v.p_kept_a, v.p_far_a, v.in_a, gain_one, v.grad_mid_a],
        )
        v.in_a1 = swap_core(v.in_a0)

    def in_b():
        v.grad_in_b, v.in_b0, v.sums = call(
            functools.partial(norm_backward, True, 3),
            back_kinds,
            [
                v.p_kept_b,
                v.p_far_b,
                v.in_b,
                gain_one,
                v.grad_mid_b,
                v.sums_one_a,
                v.sums_two_a,
                v.sums_two_b,
            ],
        )
        v.in_b1 = swap_core(v.in_b0)
        v.near_sums = swap_core(v.sums)

    def mass_1():
        packed, v.mass, v.bias, v.field_send, v.field_keep = call(
            functools.partial(mix_backward, pixels),
            mass_kinds + [((channels, half), BF16), ((channels, half), F32)],
            [v.pick, v.field_t, v.probs, v.values, v.score, mix_output, v.in_a0, v.in_a1, v.in_b0, v.in_b1],
        )
        v.mass_got = swap_sample(packed, mass_bits[0])
        v.field_near = swap_core(v.field_send)

    def add_masses(bits):
        for bit in bits:
            packed, v.mass, v.bias = call(mass_add, mass_kinds, [v.mass, v.bias, v.mass_got])
            v.mass_got = swap_sample(packed, bit)

    def mass_2():
        add_masses(mass_bits[1:2])

    def mass_3():
        add_masses(mass_bits[2:])

    def mix_in():
        rows = [v.in_a0, v.in_a1, v.in_b0, v.in_b1]
        return rows + [v.grad_in_a, v.grad_in_b, v.sums, v.near_sums]

    def mix_1():
        (send,) = call(
            functools.partial(mix_start, mesh_dp, lines, mix_steps[0], mix_order[0]),
            [((model_width // 2, mix_width), BF16)],
            [v.mixed_t] + mix_in(),
            smem=[lead_bucket],
            scratch=[rest_rows],
        )
        v.mix_got = swap_sample(send, mix_order[0])

    def mix_2():
        v.mix_keep, send = call(
            functools.partial(
                mix_second, mesh_dp, lines, mix_steps[0], mix_steps[1], mix_order[0], mix_order[1]
            ),
            halves(mix_width, model_width // 2),
            [v.mixed_t, v.mix_got] + mix_in(),
            smem=[lead_bucket],
            scratch=[rest_rows, pltpu.VMEM((model_width // 2, mix_width), F32)],
        )
        v.mix_got = swap_sample(send, mix_order[1])

    def mix_3():
        v.mix_keep, v.mix_got = rest_sum(v.mix_keep, v.mix_got, mix_order)

    def field_1():
        v.field_own, far = call(
            field_sum, [(own_field, F32), (own_field, BF16)], [v.field_keep, v.field_near]
        )
        v.field_got = swap_chip(far)

    def field_2():
        (v.field_grad,) = call(
            field_last, [((1,) + own_field, F32)], [v.field_own, v.field_got], final=True
        )

    def rows_1():
        v.r_keep_a, send_a, v.r_keep_b, send_b = call(
            mlp_out, [rows32, cut16] * 2, [v.hidden_a, v.hidden_b, down_weight]
        )
        v.r_near_a, v.r_near_b = swap_core(send_a), swap_core(send_b)

    def rows_2():
        v.rows_own, far = call(
            rows_sum,
            [rows32, rows16],
            [v.r_keep_a, v.r_near_a, v.r_keep_b, v.r_near_b, v.mid_a, v.mid_b],
        )
        v.rows_got = swap_chip(far)

    def rows_3():
        (v.activations,) = call(last_plain, [rows32], [v.rows_own, v.rows_got], final=True)

    def weights():
        v.own_weights, v.pick = call(
            functools.partial(take_weights, pixels),
            [((3, own_width, head_width), BF16), ((channels, channels), BF16)],
            [],
            smem=[variable_ids],
            fetch=[
                (
                    w_mix,
                    (3, own_width, head_width),
                    lambda ref: ref.at[:, pl.ds(lax.axis_index("dp") * own_width, own_width)],
                )
            ],
        )

    def finish():
        v.t_keep, send, v.grad_mix = call(
            functools.partial(mix_finish, pixels),
            [((own_width // 2, padded), F32)] * 2 + [((3, own_width, head_width), F32)],
            [
                v.query_col,
                v.keys_t,
                patch_table,
                variable_table,
                v.mass,
                v.bias,
                v.mass_got,
                v.own_weights,
                variable_query,
            ],
            scratch=[pltpu.VMEM((own_width, padded), F32)],
        )
        v.t_far = swap_chip(send)

    def tables_1():
        v.t_keep, send = call(
            tables_next,
            [((final, padded), F32)] * 2,
            [v.t_keep, v.t_far],
            scratch=[pltpu.VMEM((own_width // 2, padded), F32)],
        )
        v.t_near = swap_core(send)

    def tables_2():
        v.patch_total, v.variable_total, v.query_total = call(
            functools.partial(tables_last, pixels, variables),
            [((pixels, final, variables), F32), ((final, variables), F32), ((8, final), F32)],
            [v.t_keep, v.t_near],
            final=True,
        )

    def down_4():
        (v.down_sum,) = call(
            last_turned, [((hidden_width, own_width), F32)], [v.down_keep, v.down_got], final=True
        )

    def up_4():
        (v.up_sum,) = call(
            last_plain, [((own_width, hidden_width), F32)], [v.up_keep, v.up_got], final=True
        )

    def mix_4():
        v.mix_out_sum, v.pos_sum, v.lead_total, v.small = call(
            functools.partial(mix_last, mesh_dp, quarter, final),
            [
                ((head_width, own_width), F32),
                ((quarter, own_width), F32),
                ((final, lead_table.shape[0]), F32),
                ((8, final), F32),
            ],
            [v.mix_keep, v.mix_got],
            final=True,
        )

    def attn_4():
        v.attn_sum, v.attn_out_sum = call(
            last_attn,
            [((3, own_width, head_width), F32), ((head_width, own_width), F32)],
            [v.attn_keep, v.attn_got],
            final=True,
        )

    steps = dict(locals())
    for name in ORDER:
        now[:] = [name]
        steps[name]()
    return (
        v.activations,
        v.field_grad,
        v.patch_total.transpose(2, 0, 1),
        v.variable_total.T,
        v.query_total[7],
        v.grad_mix.transpose(1, 0, 2),
        v.mix_out_sum,
        v.pos_sum,
        v.lead_total.T,
        v.small[0],
        v.small[1],
        v.attn_sum.transpose(1, 0, 2),
        v.attn_out_sum,
        v.small[2],
        v.small[3],
        v.up_sum,
        v.down_sum,
    )


def solution(mesh):
    in_specs = (
        P("dp", None, None),
        P(),
        P("dp"),
        P(),
        P(),
        P(),
        P(None, None, "mp"),
        P("mp", None),
        P(),
        P(),
        P(),
        P(),
        P(None, None, "mp"),
        P("mp", None),
        P(),
        P(),
        P(None, "mp"),
        P("mp", None),
        P(("dp", "mp"), None),
    )
    out_specs = (
        P(("dp", "mp"), None),
        P("dp", None, "mp"),
        P(None, None, ("dp", "mp")),
        P(None, ("dp", "mp")),
        P(("dp", "mp")),
        P("dp", None, "mp"),
        P("mp", "dp"),
        P("mp", "dp"),
        P(None, ("dp", "mp")),
        P(("dp", "mp")),
        P(("dp", "mp")),
        P("dp", None, "mp"),
        P("mp", "dp"),
        P(("dp", "mp")),
        P(("dp", "mp")),
        P("dp", "mp"),
        P("mp", "dp"),
    )
    step = functools.partial(body, mesh.shape["dp"], mesh.shape["mp"])
    return jax.shard_map(step, mesh=mesh, in_specs=in_specs, out_specs=out_specs, check_vma=False)
```

```python
import functools
import types

import jax
import jax.numpy as jnp
from jax import lax
from jax.experimental import pallas as pl
from jax.experimental.pallas import tpu as pltpu
from jax.sharding import PartitionSpec as P

HEAD_DIM = 64
LANES = 128
EPS = 1e-05
SCALE = HEAD_DIM ** (-0.5)
HIGH = lax.Precision.HIGHEST
F32 = jnp.float32
BF16 = jnp.bfloat16
VMEM = pl.BlockSpec(memory_space=pltpu.VMEM)
SMEM = pl.BlockSpec(memory_space=pltpu.SMEM)
ANY = pl.BlockSpec(memory_space=pl.ANY)
HBM = pl.BlockSpec(memory_space=pltpu.HBM)
MIB = 1024 * 1024
FIRST_LIMIT = 60
PIECES = 2
AXES = ((0, 1, 2), (1, 2, 0), (0, 1, 2), (0, 1, 2), (1, 0, 2))
ORDER = (
    "mix_a", "mix_b", "first_a", "first_b", "base", "norm_a", "proj", "norm_b", "attend_a", "second_a", "cot",
    "attend_b", "hidden_a", "second_b", "two_a", "hidden_b", "mlp_a", "third_a", "two_b", "mlp_b", "down_1",
    "up_1", "mid_a", "third_b", "back_a", "mid_b", "back_b", "attn_1", "fourth_a", "back_c", "fourth_b",
    "down_2", "up_2", "weights", "in_a", "in_b", "mass_1", "mix_1", "down_3", "attn_2", "up_3", "mass_2",
    "mass_3", "rows_1", "down_4", "rows_2", "mix_2", "field_1", "attn_3", "finish", "tables_1", "mix_3",
    "rows_3", "field_2", "up_4", "attn_4", "tables_2", "mix_4",
)
COSTS = {
    "norm_a": 12,
    "second_a": 0.5,
    "second_b": 1,
    "cot": 1,
    "hidden_b": 3,
    "weights": 1,
    "two_a": 6.4,
    "mlp_a": 0.4,
    "third_a": 1,
    "mlp_b": 1,
    "back_a": 1.6,
    "back_c": 0.5,
    "fourth_a": 0.5,
    "attn_1": 0.5,
    "up_2": 2,
    "mass_2": 0.5,
    "field_2": 0.4,
    "up_3": 0.5,
    "tables_1": 1,
    "tables_2": 0.5,
}


def dot(left, right, left_dim=1, right_dim=0, precision=None):
    return lax.dot_general(
        left,
        right,
        (((left_dim,), (right_dim,)), ((), ())),
        precision=precision,
        preferred_element_type=F32,
    )


class Rows:
    def __init__(self, refs):
        self.refs = refs
        self.shape = (sum(ref.shape[0] for ref in refs),) + refs[0].shape[1:]

    def __getitem__(self, at):
        return jnp.concatenate([ref[at] for ref in self.refs], axis=0)

    def __setitem__(self, at, value):
        step = self.refs[0].shape[0]
        for i, ref in enumerate(self.refs):
            ref[...] = value[i * step : (i + 1) * step]


def gather_refs(refs, counts):
    refs, grouped = list(refs), []
    for count in counts:
        grouped.append(refs.pop(0) if count is None else Rows([refs.pop(0) for _ in range(count)]))
    return grouped


def flat(items):
    out, counts = [], []
    for item in items:
        pieces = isinstance(item, list)
        out.extend(item if pieces else [item])
        counts.append(len(item) if pieces else None)
    return out, counts


def launch(kernel, outs, args, fetch=(), smem=(), after=(), limit=24, scratch=(), cost=0.1, name=None, lazy=False):
    fetch = [item if isinstance(item, tuple) else (item, item.shape, None) for item in fetch]
    args, arg_counts = flat(args)
    outs, out_counts = flat(outs)
    count = len(smem)

    def run(*refs):
        at = count + len(fetch)
        sources, rest = refs[count:at], refs[at:]
        inputs, rest = gather_refs(rest[: len(args)], arg_counts), rest[len(args) + len(after) :]
        results, rest = gather_refs(rest[: len(outs)], out_counts), rest[len(outs) :]
        if not fetch:
            kernel(*refs[:count], *inputs, *results, *rest)
            return
        *rest, marks = rest
        rest, places = rest[: len(rest) - len(fetch)], rest[len(rest) - len(fetch) :]
        copies = []
        for i, (_, _, pick) in enumerate(fetch):
            source = sources[i] if pick is None else pick(sources[i])
            copies.append(pltpu.make_async_copy(source, places[i], marks.at[i]))
        for copy in copies:
            copy.start()
        if lazy:
            kernel([copy.wait for copy in copies], *refs[:count], *places, *inputs, *results, *rest)
            return
        for copy in copies:
            copy.wait()
        kernel(*refs[:count], *places, *inputs, *results, *rest)

    places = [
        (pltpu.SMEM if array.dtype == jnp.int32 else pltpu.VMEM)(shape, array.dtype)
        for array, shape, _ in fetch
    ]
    marks = [pltpu.SemaphoreType.DMA((len(fetch),))] if fetch else []
    results = pl.pallas_call(
        run,
        out_shape=[jax.ShapeDtypeStruct(shape, kind) for shape, kind in outs],
        in_specs=[SMEM] * count + [HBM] * len(fetch) + [VMEM] * len(args) + [ANY] * len(after),
        out_specs=[VMEM] * len(outs),
        scratch_shapes=list(scratch) + places + marks,
        name=name,
        compiler_params=pltpu.CompilerParams(vmem_limit_bytes=limit * MIB),
        cost_estimate=pl.CostEstimate(
            flops=int(cost * 1e9), bytes_accessed=0, transcendentals=0
        ),
    )(*smem, *(array for array, _, _ in fetch), *args, *after)
    results, grouped = list(results), []
    for pieces in out_counts:
        grouped.append(results.pop(0) if pieces is None else [results.pop(0) for _ in range(pieces)])
    return grouped


def marked(kernel, *refs):
    *rest, mark_ref = refs
    mark_ref[...] = jnp.zeros_like(mark_ref)
    kernel(*rest)


def my_bit(bit):
    return (lax.axis_index("dp") // bit) % 2


def my_core():
    return lax.axis_index("mp") % 2


def my_chip():
    return lax.axis_index("mp") // 2


def iota(shape, dim):
    return lax.broadcasted_iota(jnp.int32, shape, dim)


def exact(mask):
    return mask.astype(F32).astype(BF16)


def lanes_of(rows, head):
    lane = iota((1, rows.shape[1]), 1)
    mine = (lane >= head * HEAD_DIM) & (lane < (head + 1) * HEAD_DIM)
    return jnp.where(mine, rows, jnp.zeros_like(rows))


def spread(rows, pixels, top, bottom):
    variables = top.shape[0]
    parts = [top * rows[p * variables : (p + 1) * variables] for p in range(pixels)]
    parts.append(top)
    if bottom:
        parts.append(jnp.zeros((bottom, top.shape[1]), top.dtype))
    return jnp.concatenate(parts, axis=0)


def pixel_major(channels, pixels):
    variables = channels // pixels
    row = iota((channels, channels), 0)
    major = jnp.zeros((channels, channels), jnp.int32)
    for p in range(pixels):
        inside = (row >= p * variables) & (row < (p + 1) * variables)
        major = jnp.where(inside, (row - p * variables) * pixels + p, major)
    return exact(iota((channels, channels), 1) == major)


def places(ids_ref, variables, pixels):
    channels = variables * pixels
    channel = iota((1, channels), 1)
    place = jnp.zeros((1, channels), jnp.int32)
    for v in range(variables):
        pixel = channel - v * pixels
        inside = (pixel >= 0) & (pixel < pixels)
        place = jnp.where(inside, pixel * variables + ids_ref[v], place)
    return place


def mix_forward(
    pixels,
    quarter,
    waits,
    ids_ref,
    x_ref,
    patch_ref,
    variable_ref,
    w_ref,
    query_ref,
    mixed_ref,
    xt_ref,
    probs_ref,
    values_ref,
    keys_t_ref,
    score_ref,
    query_col_ref,
    table_ref,
):
    channels = x_ref.shape[1]
    variables = channels // pixels
    rows, model_width = table_ref.shape
    width = w_ref.shape[2]
    heads = width // HEAD_DIM
    bottom = rows - channels - variables
    wait_ids, wait_field, wait_patch, wait_variable, wait_weights, wait_query = waits
    wait_patch()
    flat = patch_ref[...].reshape(channels, model_width)
    table_ref[0:channels] = dot(pixel_major(channels, pixels), flat).astype(BF16)
    wait_variable()
    table_ref[channels : channels + variables] = variable_ref[...]
    if bottom:
        table_ref[channels + variables :] = jnp.zeros((bottom, model_width), BF16)
    wait_ids()
    pick = (iota((channels, channels), 0) == places(ids_ref, variables, pixels)).astype(F32)
    wait_field()
    core = my_core()
    starts = [core, 1 - core, core + 2, 3 - core]
    field = jnp.concatenate(
        [x_ref[0, :, pl.ds(pl.multiple_of(s * quarter, LANES), quarter)] for s in starts], axis=1
    )
    xt = dot(pick.astype(BF16), field)
    xt_ref[...] = xt.astype(BF16)
    wait_weights()
    wait_query()
    query_rows = jnp.broadcast_to(query_ref[...].astype(F32)[None], (16, model_width)).astype(BF16)
    query = dot(query_rows, w_ref[0])[0:1].astype(BF16).astype(F32)
    table = table_ref[...]
    keys = dot(table, w_ref[1])
    values = dot(table, w_ref[2])
    values_ref[...] = values.astype(BF16)
    keys_t_ref[...] = keys.T
    query_col_ref[...] = jnp.broadcast_to(query, (LANES, width)).T
    lane = iota((width, LANES), 1) * HEAD_DIM
    row = iota((width, LANES), 0)
    same = ((row >= lane) & (row < lane + HEAD_DIM)).astype(F32)
    score = dot(keys * query, same, precision=HIGH) * SCALE
    score_ref[...] = score
    values_t = values.T.astype(BF16)
    for head in range(heads):
        column = score[:, head : head + 1]
        logits = jnp.broadcast_to(column[channels : channels + variables], (variables, xt.shape[1]))
        for p in range(pixels):
            part = slice(p * variables, (p + 1) * variables)
            logits = logits + column[part] * xt[part]
        weights = jnp.exp(logits - jnp.max(logits, axis=0, keepdims=True))
        probs = weights / jnp.sum(weights, axis=0, keepdims=True)
        probs_ref[head * variables : (head + 1) * variables] = probs
        low = probs.astype(BF16).astype(F32)
        mixing = spread(xt, pixels, low, bottom).astype(BF16)
        part = slice(head * HEAD_DIM, (head + 1) * HEAD_DIM)
        mixed_ref[part] = dot(values_t[part], mixing).astype(BF16)


def mix_out(mixed_ref, w_out_ref, send_a_ref, send_b_ref, keep_a_ref, keep_b_ref):
    quarter = keep_a_ref.shape[0]
    out = dot(mixed_ref[...], w_out_ref[...], 0, 0)
    keep_a_ref[...] = out[0:quarter]
    send_a_ref[...] = out[quarter : 2 * quarter].astype(BF16)
    keep_b_ref[...] = out[2 * quarter : 3 * quarter]
    send_b_ref[...] = out[3 * quarter :].astype(BF16)


def pack_mass(mass, bias, packed_ref):
    width = mass.shape[0]
    high = bias.astype(BF16).astype(F32)
    packed_ref[0:width] = mass.astype(BF16)
    packed_ref[width:] = jnp.concatenate([high, bias - high], axis=0).astype(BF16)


def add_mass(mass_ref, bias_ref, got_ref):
    width = mass_ref.shape[0]
    more = got_ref[width:].astype(F32)
    return mass_ref[...] + got_ref[0:width].astype(F32), bias_ref[...] + more[0:8] + more[8:16]


def mix_backward(
    pixels,
    pick_ref,
    xt_ref,
    probs_ref,
    values_ref,
    score_ref,
    w_out_ref,
    a0_ref,
    a1_ref,
    b0_ref,
    b1_ref,
    packed_ref,
    mass_ref,
    bias_ref,
    field_send_ref,
    field_keep_ref,
):
    channels, length = xt_ref.shape
    variables = channels // pixels
    rows, width = values_ref.shape
    heads = width // HEAD_DIM
    bottom = rows - channels - variables
    quarter = length // 4
    xt = xt_ref[...].astype(F32)
    grad = jnp.concatenate([a0_ref[...], a1_ref[...], b0_ref[...], b1_ref[...]], axis=0)
    grad_t = dot(w_out_ref[...], grad, 1, 1).astype(BF16)
    values = values_ref[...]
    score = score_ref[...]
    field = jnp.zeros(xt.shape, F32)
    lane = iota((rows, LANES), 1)
    sums = jnp.zeros((rows, LANES), F32)
    for head in range(heads):
        probs = probs_ref[head * variables : (head + 1) * variables]
        low = probs.astype(BF16).astype(F32)
        back = dot(lanes_of(values, head), grad_t)
        prob_grad = back[channels : channels + variables]
        for p in range(pixels):
            part = slice(p * variables, (p + 1) * variables)
            prob_grad = prob_grad + xt[part] * back[part]
        middle = jnp.sum(probs * prob_grad, axis=0, keepdims=True)
        score_grad = probs * (prob_grad - middle)
        column = score[:, head : head + 1]
        field = field + jnp.concatenate(
            [
                score_grad * column[p * variables : (p + 1) * variables]
                + low * back[p * variables : (p + 1) * variables]
                for p in range(pixels)
            ],
            axis=0,
        )
        spreading = spread(xt, pixels, score_grad * SCALE, bottom)
        sums = jnp.where(lane == head, jnp.sum(spreading, axis=1, keepdims=True), sums)
        mixing = spread(xt, pixels, low, bottom).astype(BF16)
        part = slice(head * HEAD_DIM, (head + 1) * HEAD_DIM)
        mass_ref[part] = dot(grad_t[part], mixing, 1, 1)
    bias_ref[...] = sums.T[0:8]
    pack_mass(mass_ref[...], bias_ref[...], packed_ref)
    field = dot(pick_ref[...], field.astype(BF16))
    field_keep_ref[:, 0:quarter] = field[:, 0:quarter]
    field_keep_ref[:, quarter:] = field[:, 2 * quarter : 3 * quarter]
    field_send_ref[:, 0:quarter] = field[:, quarter : 2 * quarter].astype(BF16)
    field_send_ref[:, quarter:] = field[:, 3 * quarter :].astype(BF16)


def norm_forward(*refs):
    *terms, gain_ref, bias_ref, out_ref, low_ref = refs
    total = terms[0][...].astype(F32)
    for term in terms[1:]:
        total = total + term[...].astype(F32)
    out_ref[...] = total
    centered = total - jnp.mean(total, axis=1, keepdims=True)
    inv_std = lax.rsqrt(jnp.mean(centered * centered, axis=1, keepdims=True) + EPS)
    low_ref[...] = (centered * inv_std * gain_ref[...] + bias_ref[...]).astype(BF16)


def norm_relay(pass_ref, *refs):
    *refs, out_ref = refs
    out_ref[...] = pass_ref[...]
    norm_forward(*refs)


def norm_backward(with_sum, add_refs, *refs):
    keep_ref, far_ref, rows_ref, gain_ref, above_ref = refs[:5]
    more = refs[5 : 5 + add_refs]
    out_ref, low_ref, sums_ref = refs[5 + add_refs :]
    grad = keep_ref[...] + far_ref[...].astype(F32)
    rows = rows_ref[...]
    centered = rows - jnp.mean(rows, axis=1, keepdims=True)
    inv_std = lax.rsqrt(jnp.mean(centered * centered, axis=1, keepdims=True) + EPS)
    normed = centered * inv_std
    scaled = grad * gain_ref[...]
    first = jnp.mean(scaled, axis=1, keepdims=True)
    second = jnp.mean(scaled * normed, axis=1, keepdims=True)
    out = above_ref[...].astype(F32) + inv_std * (scaled - first - normed * second)
    out_ref[...] = out
    low_ref[...] = out.astype(BF16)
    lines = [
        jnp.sum(grad * normed, axis=0, keepdims=True),
        jnp.sum(grad, axis=0, keepdims=True),
    ]
    lines.append(jnp.sum(out, axis=0, keepdims=True) if with_sum else jnp.zeros_like(lines[0]))
    if add_refs:
        one, two_a, two_b = (ref[...] for ref in more)
        lines = [
            lines[0] + one[0:1],
            lines[1] + one[1:2],
            two_a[0:1] + two_b[0:1],
            two_a[1:2] + two_b[1:2],
            lines[2] + one[2:3],
        ]
    lines.append(jnp.zeros((8 - len(lines), grad.shape[1]), F32))
    sums_ref[...] = jnp.concatenate(lines, axis=0)


def project(own_ref, near_ref, w_ref, out_ref):
    rows = jnp.concatenate([own_ref[...], near_ref[...]], axis=0)
    for i in range(3):
        out_ref[i] = dot(rows, w_ref[i]).astype(BF16)


def attend(query, keys, values_t, logs_ref):
    scaled = (query.astype(F32) * SCALE).astype(BF16)
    parts = []
    for head in range(keys.shape[1] // HEAD_DIM):
        scores = dot(keys, lanes_of(scaled, head), 1, 1)
        top = jnp.max(scores, axis=0, keepdims=True)
        weights = jnp.exp(scores - top)
        total = jnp.sum(weights, axis=0, keepdims=True)
        logs_ref[head : head + 1] = top + jnp.log(total)
        part = dot(values_t[head * HEAD_DIM : (head + 1) * HEAD_DIM], weights.astype(BF16))
        parts.append(part * (1.0 / total))
    return jnp.concatenate(parts, axis=0).T.astype(BF16)


def split_out(out, keep_ref, send_ref):
    quarter = out.shape[0] // 2
    keep_ref[...] = out[:quarter]
    send_ref[...] = out[quarter:].astype(BF16)


def attend_first(own_ref, near_ref, w_ref, first_ref, w_out_ref, second_ref, out_ref, logs_ref, keep_ref, send_ref):
    project(own_ref, near_ref, w_ref, second_ref)
    keys = jnp.concatenate([first_ref[1], second_ref[1]], axis=0)
    values = jnp.concatenate([first_ref[2], second_ref[2]], axis=0)
    out_ref[...] = attend(first_ref[0], keys, values.T, logs_ref)
    split_out(dot(out_ref[...], w_out_ref[...]), keep_ref, send_ref)


def attend_second(first_ref, second_ref, w_out_ref, out_ref, logs_ref, keep_ref, send_ref):
    keys = jnp.concatenate([first_ref[1], second_ref[1]], axis=0)
    values = jnp.concatenate([first_ref[2], second_ref[2]], axis=0)
    out_ref[...] = attend(second_ref[0], keys, values.T, logs_ref)
    split_out(dot(out_ref[...], w_out_ref[...]), keep_ref, send_ref)


def attend_grad(grad, query, keys, values, logs_ref):
    scaled = (query.astype(F32) * SCALE).astype(BF16)
    keys_t = keys.T
    query_parts = []
    key_grad = jnp.zeros(keys.shape, F32)
    value_grad = jnp.zeros(keys.shape, F32)
    for head in range(keys.shape[1] // HEAD_DIM):
        head_query, head_grad = lanes_of(scaled, head), lanes_of(grad, head)
        scores = dot(keys, head_query, 1, 1)
        probs = jnp.exp(scores - logs_ref[head : head + 1])
        prob_grad = dot(values, head_grad, 1, 1)
        middle = jnp.sum(probs * prob_grad, axis=0, keepdims=True)
        score_grad = (probs * (prob_grad - middle)).astype(BF16)
        query_parts.append(dot(keys_t[head * HEAD_DIM : (head + 1) * HEAD_DIM], score_grad))
        key_grad = key_grad + dot(score_grad, head_query)
        value_grad = value_grad + dot(probs.astype(BF16), head_grad)
    query_grad = (jnp.concatenate(query_parts, axis=0).T * SCALE).astype(BF16)
    return query_grad, key_grad, value_grad


def attend_back_first(own_ref, near_ref, w_out_ref, first_ref, second_ref, logs_ref, query_ref, key_ref, value_ref):
    rows = jnp.concatenate([own_ref[...], near_ref[...]], axis=0)
    grad = dot(rows, w_out_ref[...], 1, 1).astype(BF16)
    keys = jnp.concatenate([first_ref[1], second_ref[1]], axis=0)
    values = jnp.concatenate([first_ref[2], second_ref[2]], axis=0)
    query_ref[...], key_ref[...], value_ref[...] = attend_grad(
        grad, first_ref[0], keys, values, logs_ref
    )


def project_back(rows_ref, start, count, w_ref):
    total = dot(rows_ref[0, start : start + count], w_ref[0], 1, 1)
    for i in range(1, 3):
        total = total + dot(rows_ref[i, start : start + count], w_ref[i], 1, 1)
    return total


def attend_back_second(
    own_ref,
    near_ref,
    w_out_ref,
    first_ref,
    second_ref,
    logs_ref,
    query_ref,
    key_ref,
    value_ref,
    w_ref,
    out_ref,
    keep_ref,
    send_ref,
):
    rows = jnp.concatenate([own_ref[...], near_ref[...]], axis=0)
    half = rows.shape[0]
    grad = dot(rows, w_out_ref[...], 1, 1).astype(BF16)
    keys = jnp.concatenate([first_ref[1], second_ref[1]], axis=0)
    values = jnp.concatenate([first_ref[2], second_ref[2]], axis=0)
    query_grad, key_grad, value_grad = attend_grad(grad, second_ref[0], keys, values, logs_ref)
    out_ref[0, 0:half] = query_ref[...]
    out_ref[0, half:] = query_grad
    out_ref[1] = (key_ref[...] + key_grad).astype(BF16)
    out_ref[2] = (value_ref[...] + value_grad).astype(BF16)
    split_out(project_back(out_ref, 0, half, w_ref), keep_ref, send_ref)


def attend_back_last(rows_ref, w_ref, keep_ref, send_ref):
    half = rows_ref.shape[1] // 2
    split_out(project_back(rows_ref, half, half, w_ref), keep_ref, send_ref)


def hidden_back(own_ref, near_ref, w_ref, out_ref):
    rows = jnp.concatenate([own_ref[...], near_ref[...]], axis=0)
    out_ref[...] = dot(rows, w_ref[...], 1, 1)


ROOT = 0.7978845608028654
CUBE = 0.044715


def mlp(own_ref, near_ref, w_ref, grad_ref, hidden_ref, out_ref, keep_ref, send_ref):
    rows = jnp.concatenate([own_ref[...], near_ref[...]], axis=0)
    pre = dot(rows, w_ref[...])
    square = pre * pre
    bend = jnp.tanh(ROOT * pre * (1.0 + CUBE * square))
    half = 0.5 * (1.0 + bend)
    hidden_ref[...] = (pre * half).astype(BF16)
    slope = half + (0.5 * ROOT) * pre * (1.0 - bend * bend) * (1.0 + (3.0 * CUBE) * square)
    out_ref[...] = (slope * grad_ref[...]).astype(BF16)
    split_out(dot(out_ref[...], w_ref[...], 1, 1), keep_ref, send_ref)


def mlp_out(first_ref, second_ref, w_ref, keep_a_ref, send_a_ref, keep_b_ref, send_b_ref):
    split_out(dot(first_ref[...], w_ref[...]), keep_a_ref, send_a_ref)
    split_out(dot(second_ref[...], w_ref[...]), keep_b_ref, send_b_ref)


def grad_rows(parts, step, width, which):
    groups = width // (2 * step)
    outs = []
    for group in range(groups):
        start = pl.multiple_of((2 * group + which) * step, LANES)
        line = []
        for left, rights in parts:
            picked = jnp.concatenate([ref[:, pl.ds(start, step)] for ref in left], axis=0)
            line.extend(dot(picked, right, 0, 0) for right in rights)
        outs.append(line)
    return outs, groups


def write_half(ref, parts, step, width, which, dtype):
    outs, groups = grad_rows(parts, step, width, which)
    for group in range(groups):
        column = 0
        for value in outs[group]:
            ref[group * step : (group + 1) * step, column : column + value.shape[1]] = value.astype(dtype)
            column += value.shape[1]


def take_half(out_ref, source, step, which, dtype):
    for group in range(source.shape[0] // (2 * step)):
        start = pl.multiple_of((2 * group + which) * step, 16)
        out_ref[group * step : (group + 1) * step] = source[pl.ds(start, step)].astype(dtype)


def sum_start(load, step, bit, *refs):
    *inputs, out_ref = refs
    parts, width = load(inputs)
    write_half(out_ref, parts, step, width, 1 - my_bit(bit), BF16)


def sum_second(load, step, next_step, bit, next_bit, *refs):
    got_ref, *inputs, keep_ref, send_ref, total = refs
    parts, width = load(inputs)
    write_half(total, parts, step, width, my_bit(bit), F32)
    total[...] = total[...] + got_ref[...].astype(F32)
    take_half(send_ref, total, next_step, 1 - my_bit(next_bit), BF16)
    take_half(keep_ref, total, next_step, my_bit(next_bit), F32)


def sum_next(next_step, next_bit, kept_ref, got_ref, keep_ref, send_ref, total):
    total[...] = kept_ref[...] + got_ref[...].astype(F32)
    take_half(send_ref, total, next_step, 1 - my_bit(next_bit), BF16)
    take_half(keep_ref, total, next_step, my_bit(next_bit), F32)


def load_plain(inputs):
    *left, first, second = inputs
    right = jnp.concatenate([first[...], second[...]], axis=0)
    return [(left, [right])], left[0].shape[1]


def load_attn(inputs):
    left, middle = inputs[0:4], inputs[4:8]
    proj, first, second = inputs[8:]
    attended = jnp.concatenate([first[...], second[...]], axis=0)
    return [(left, [proj[0], proj[1], proj[2]]), (middle, [attended])], left[0].shape[1]


def last_plain(kept_ref, got_ref, out_ref):
    out_ref[...] = kept_ref[...] + got_ref[...].astype(F32)


def last_turned(kept_ref, got_ref, out_ref):
    out_ref[...] = (kept_ref[...] + got_ref[...].astype(F32)).T


def last_attn(kept_ref, got_ref, proj_ref, out_ref):
    total = kept_ref[...] + got_ref[...].astype(F32)
    width = proj_ref.shape[2]
    for i in range(3):
        proj_ref[i] = total[:, i * width : (i + 1) * width]
    out_ref[...] = total[:, 3 * width :].T


def mix_lines(samples, lines, bucket_ref, inputs, rest_ref):
    first_ref, second_ref, own_ref, near_ref = inputs
    quarter, width = first_ref.shape
    rest_ref[0:quarter] = jnp.where(my_chip() == 0, first_ref[...], second_ref[...])
    sample = lax.axis_index("dp")
    sums = own_ref[...] + near_ref[...]
    row = iota((lines, width), 0)
    filled = jnp.concatenate([sums, jnp.zeros((lines - 8, width), F32)], axis=0)
    filled = jnp.where(row < 4, filled, 0.0)
    filled = jnp.where(row == 4 + sample, sums[4:5], filled)
    bucket = bucket_ref[0].astype(F32)
    rest_ref[quarter:] = jnp.where(row == 4 + samples + sample, bucket, filled)


def write_mix(ref, step, which, left, mixed_ref, rest_ref, dtype):
    width = left[0].shape[1]
    heads_width = mixed_ref.shape[0]
    for group in range(width // (2 * step)):
        start = pl.multiple_of((2 * group + which) * step, LANES)
        picked = jnp.concatenate([part[:, pl.ds(start, step)] for part in left], axis=0)
        rows = slice(group * step, (group + 1) * step)
        ref[rows, 0:heads_width] = dot(picked, mixed_ref[...], 0, 1).astype(dtype)
        ref[rows, heads_width:] = rest_ref[:, pl.ds(start, step)].T.astype(dtype)


def mix_start(samples, lines, step, bit, bucket_ref, mixed_ref, *refs):
    *inputs, out_ref, rest = refs
    mix_lines(samples, lines, bucket_ref, inputs[4:], rest)
    write_mix(out_ref, step, 1 - my_bit(bit), inputs[:4], mixed_ref, rest, BF16)


def mix_second(samples, lines, step, next_step, bit, next_bit, bucket_ref, mixed_ref, *refs):
    got_ref, *inputs, keep_ref, send_ref, rest, total = refs
    mix_lines(samples, lines, bucket_ref, inputs[4:], rest)
    write_mix(total, step, my_bit(bit), inputs[:4], mixed_ref, rest, F32)
    total[...] = total[...] + got_ref[...].astype(F32)
    take_half(send_ref, total, next_step, 1 - my_bit(next_bit), BF16)
    take_half(keep_ref, total, next_step, my_bit(next_bit), F32)


def mix_last(samples, quarter, final, kept_ref, got_ref, out_ref, pos_ref, lead_ref, small_ref):
    total = kept_ref[...] + got_ref[...].astype(F32)
    heads_width = out_ref.shape[0]
    out_ref[...] = total[:, :heads_width].T
    pos_ref[...] = total[:, heads_width : heads_width + quarter].T
    rest = total[:, heads_width + quarter :]
    rows = max(final, 8)
    mine = iota((rows, rest.shape[0]), 1) == iota((rows, rest.shape[0]), 0) + lax.axis_index("mp") * final
    own = dot(mine.astype(F32), rest, precision=HIGH)
    bucket = iota((rows, lead_ref.shape[1]), 1).astype(F32)
    lead = jnp.zeros(bucket.shape, F32)
    for s in range(samples):
        mark = own[:, 4 + samples + s : 5 + samples + s]
        lead = jnp.where(bucket == mark, lead + own[:, 4 + s : 5 + s], lead)
    lead_ref[...] = lead[:final]
    small_ref[...] = own.T[0:8, :final]


def mass_add(mass_ref, bias_ref, got_ref, packed_ref, mass_out_ref, bias_out_ref):
    mass, bias = add_mass(mass_ref, bias_ref, got_ref)
    mass_out_ref[...] = mass
    bias_out_ref[...] = bias
    pack_mass(mass, bias, packed_ref)


def mix_finish(
    pixels,
    query_col_ref,
    keys_t_ref,
    patch_ref,
    variable_ref,
    mass_ref,
    bias_ref,
    got_ref,
    w_ref,
    query_ref,
    keep_ref,
    send_ref,
    grad_ref,
    scratch,
):
    width, rows = mass_ref.shape
    heads = width // HEAD_DIM
    mass, sums = add_mass(mass_ref, bias_ref, got_ref)
    mass = mass.astype(BF16)
    bias = jnp.concatenate(
        [jnp.broadcast_to(sums[head : head + 1], (HEAD_DIM, rows)) for head in range(heads)], axis=0
    )
    key_mass = (bias * query_col_ref[:, 0:1]).astype(BF16)
    total = jnp.sum(keys_t_ref[...] * bias, axis=1, keepdims=True)
    own = grad_ref.shape[1]
    start = lax.axis_index("dp") * own
    model_width = variable_ref.shape[1]
    channels = patch_ref.shape[0] * pixels
    mine = exact(iota((own, model_width), 1) == iota((own, model_width), 0) + start)
    total_row = jnp.broadcast_to(total, (width, LANES)).T[0:1]
    flat = patch_ref[...].reshape(channels, model_width)
    patch_t = dot(mine, flat, 1, 1).astype(BF16)
    patch_t = dot(patch_t, pixel_major(channels, pixels), 1, 1)
    variable_t = dot(mine, variable_ref[...], 1, 1)
    bottom = rows - channels - variable_ref.shape[0]
    table_t = jnp.concatenate([patch_t, variable_t, jnp.zeros((own, bottom), F32)], axis=1).astype(BF16)
    query_rows = jnp.broadcast_to(query_ref[...].astype(F32)[None], (16, model_width)).astype(BF16)
    grad_ref[0] = dot(mine, query_rows, 1, 1)[:, 0:1] * total_row
    grad_ref[1] = dot(table_t, key_mass, 1, 1)
    grad_ref[2] = dot(table_t, mass, 1, 1)
    back = dot(w_ref[1], key_mass) + dot(w_ref[2], mass)
    query_back = jnp.sum(w_ref[0].astype(F32) * total_row, axis=1, keepdims=True)
    scratch[...] = jnp.where(iota((own, rows), 1) == rows - 1, query_back, back)
    keep_part(scratch, keep_ref, send_ref, my_chip())


def keep_part(source, keep_ref, send_ref, which):
    step = keep_ref.shape[0]
    if step % 8:
        first, second = source[0:step], source[step : 2 * step]
        keep_ref[...] = jnp.where(which == 0, first, second)
        send_ref[...] = jnp.where(which == 0, second, first)
    else:
        keep_ref[...] = source[pl.ds(pl.multiple_of(which * step, 8), step)]
        send_ref[...] = source[pl.ds(pl.multiple_of((1 - which) * step, 8), step)]


def tables_next(kept_ref, got_ref, keep_ref, send_ref, scratch):
    scratch[...] = kept_ref[...] + got_ref[...]
    keep_part(scratch, keep_ref, send_ref, my_core())


def pair_sum(keep_ref, got_ref, out_ref, low_ref):
    total = keep_ref[...] + got_ref[...].astype(F32)
    out_ref[...] = total
    low_ref[...] = total.astype(BF16)


def take_rows(source_ref, out_ref):
    out_ref[...] = source_ref[...]


def take_weights(pixels, ids_ref, source_ref, out_ref, pick_ref):
    out_ref[...] = source_ref[...]
    channels = pick_ref.shape[0]
    pick = iota((channels, channels), 0) == places(ids_ref, channels // pixels, pixels)
    pick_ref[...] = pick.astype(F32).T.astype(BF16)


def by_chip(own_ref, far_ref, first_ref, second_ref):
    own, far = own_ref[...], far_ref[...]
    first = my_chip() == 0
    first_ref[...] = jnp.where(first, own, far)
    second_ref[...] = jnp.where(first, far, own)


def base_rows(bucket_ref, first_ref, second_ref, lead_ref, out_a_ref, out_b_ref):
    rows = lead_ref.shape[0]
    mark = exact(iota((16, rows), 1) == bucket_ref[0])
    lead = dot(mark, lead_ref[...])[0:1]
    out_a_ref[...] = first_ref[...].astype(F32) + lead
    out_b_ref[...] = second_ref[...].astype(F32) + lead


def field_sum(keep_ref, got_ref, own_ref, send_ref):
    total = keep_ref[...] + got_ref[...].astype(F32)
    quarter = own_ref.shape[1]
    first = my_chip() == 0
    own_ref[...] = jnp.where(first, total[:, :quarter], total[:, quarter:])
    send_ref[...] = jnp.where(first, total[:, quarter:], total[:, :quarter]).astype(BF16)


def field_last(own_ref, far_ref, out_ref):
    out_ref[0] = own_ref[...] + far_ref[...].astype(F32)


def rows_sum(keep_a_ref, got_a_ref, keep_b_ref, got_b_ref, mid_a_ref, mid_b_ref, own_ref, send_ref):
    part_a = keep_a_ref[...] + got_a_ref[...].astype(F32)
    part_b = keep_b_ref[...] + got_b_ref[...].astype(F32)
    first = my_chip() == 0
    own_ref[...] = jnp.where(first, part_a + mid_a_ref[...], part_b + mid_b_ref[...])
    send_ref[...] = jnp.where(first, part_b, part_a).astype(BF16)


def tables_last(pixels, variables, kept_ref, got_ref, patch_ref, variable_ref, query_ref):
    total = kept_ref[...] + got_ref[...]
    for p in range(pixels):
        patch_ref[p] = total[:, p * variables : (p + 1) * variables]
    variable_ref[...] = total[:, pixels * variables : (pixels + 1) * variables]
    query_ref[...] = total.T[total.shape[1] - 8 :]


def pairs(count, bit):
    return [(i, i ^ bit) for i in range(count)]


def body(
    mesh_dp,
    mesh_mp,
    input_field,
    variable_ids,
    lead_bucket,
    patch_table,
    variable_table,
    variable_query,
    mix_weights,
    mix_output,
    pos_table,
    lead_table,
    first_gain,
    first_bias,
    attn_weights,
    attn_output,
    second_gain,
    second_bias,
    up_weight,
    down_weight,
    cotangent,
):
    length = input_field.shape[2]
    channels = input_field.shape[1]
    variables = variable_ids.shape[0]
    pixels = channels // variables
    model_width = pos_table.shape[1]
    quarter = cotangent.shape[0]
    head_width = mix_weights.shape[2]
    hidden_width = up_weight.shape[1]
    heads = head_width // HEAD_DIM
    own_width = model_width // mesh_dp
    half = 2 * quarter
    latest, now = [], []
    v = types.SimpleNamespace()

    def call(kernel, outs, args, final=False, **options):
        if final:
            outs = outs + [((8, LANES), F32)]
            kernel = functools.partial(marked, kernel)
        known = flat(args)[0] + list(options.get("fetch", ()))
        after = [last for last in latest if all(last is not arg for arg in known)]
        cost = COSTS.get(now[0], 0.1)
        results = launch(kernel, outs, args, after=after, cost=cost, name=now[0], **options)
        latest[:] = results[-1:] if final else flat(results)[0][:1]
        return results[:-1] if final else results

    rows32 = ((quarter, model_width), F32)
    rows16 = ((quarter, model_width), BF16)
    cut16 = [((quarter // PIECES, model_width), BF16)] * PIECES

    def swap_core(value):
        if isinstance(value, list):
            return [swap_core(piece) for piece in value]
        return lax.ppermute(value, "mp", pairs(mesh_mp, 1))

    def swap_chip(value):
        return lax.ppermute(value, "mp", pairs(mesh_mp, 2))

    def swap_sample(value, bit):
        return lax.ppermute(value, "dp", pairs(mesh_dp, bit))

    def add_near(keep, near):
        kept, low = call(pair_sum, [rows32, rows16], [keep, near])
        return kept, swap_chip(low)

    all_bits = [1 << i for i in range(mesh_dp.bit_length() - 1)]
    wide = [bit for bit in all_bits if bit * own_width % LANES == 0]

    def order_from(axes):
        return [wide[i] for i in axes] + [bit for bit in all_bits if bit not in wide[:3]]

    def steps_of(order):
        left = list(all_bits)
        steps = []
        for bit in order:
            steps.append(own_width << left.index(bit))
            left.remove(bit)
        return steps

    def start_sum(load, inputs, width, order):
        step = steps_of(order)[0]
        (send,) = call(
            functools.partial(sum_start, load, step, order[0]),
            [((model_width // 2, width), BF16)],
            inputs,
        )
        return swap_sample(send, order[0])

    def halves(width, scratch_rows):
        kept = scratch_rows // 2
        return [((kept, width), F32), ((kept, width), BF16)]

    def second_sum(load, inputs, got, width, order):
        steps = steps_of(order)
        rows = model_width // 2
        keep, send = call(
            functools.partial(sum_second, load, steps[0], steps[1], order[0], order[1]),
            halves(width, rows),
            [got] + inputs,
            scratch=[pltpu.VMEM((rows, width), F32)],
        )
        return keep, swap_sample(send, order[1])

    def rest_sum(keep, got, order):
        steps = steps_of(order)
        for i in range(2, len(order)):
            rows, width = keep.shape
            keep, send = call(
                functools.partial(sum_next, steps[i], order[i]),
                halves(width, rows),
                [keep, got],
                scratch=[pltpu.VMEM((rows, width), F32)],
            )
            got = swap_sample(send, order[i])
        return keep, got

    def norm_rows(terms, gain, bias):
        return call(norm_forward, [rows32, cut16], terms + [gain, bias])

    w_mix = mix_weights.transpose(1, 0, 2)
    w_attn = attn_weights.transpose(1, 0, 2)
    gain_one, bias_one = first_gain[None], first_bias[None]
    gain_two, bias_two = second_gain[None], second_bias[None]
    table_rows = channels + variables
    padded = -(-(table_rows + 1) // LANES) * LANES
    lines = -(-(4 + 2 * mesh_dp) // LANES) * LANES
    mix_width = head_width + quarter + lines
    attn_width = 4 * head_width
    final = own_width // mesh_mp
    own_field = (channels, quarter)
    proj_kind = ((3, half, head_width), BF16)
    attend_kinds = [((half, head_width), BF16), ((8, half), F32), rows32, cut16]
    hidden_kind = ((half, hidden_width), F32)
    mlp_kinds = [((half, hidden_width), BF16)] * 2 + [rows32, cut16]
    back_kinds = [rows32, cut16, ((8, model_width), F32)]
    grad_kinds = [((half, head_width), BF16)] + [((length, head_width), F32)] * 2
    mass_kinds = [
        ((head_width + 16, padded), BF16),
        ((head_width, padded), F32),
        ((8, padded), F32),
    ]
    rest_rows = pltpu.VMEM((quarter + lines, model_width), F32)
    down_order, up_order, attn_order, mix_order, mass_bits = map(order_from, AXES)
    mix_steps = steps_of(mix_order)
    back_two = functools.partial(norm_backward, False, 0)

    def mix_a():
        v.mixed_t, v.field_t, v.probs, v.values, v.keys_t, v.score, v.query_col = call(
            functools.partial(mix_forward, pixels, quarter),
            [
                ((head_width, length), BF16),
                ((channels, length), BF16),
                ((heads * variables, length), F32),
                ((padded, head_width), BF16),
                ((head_width, padded), F32),
                ((padded, LANES), F32),
                ((head_width, LANES), F32),
            ],
            [],
            fetch=[variable_ids, input_field, patch_table, variable_table, w_mix, variable_query],
            limit=FIRST_LIMIT,
            lazy=True,
            scratch=[pltpu.VMEM((padded, model_width), BF16)],
        )

    def mix_b():
        send_a, send_b, v.keep_a, v.keep_b = call(
            mix_out, [rows16, rows16, rows32, rows32], [mix_output], fetch=[v.mixed_t]
        )
        v.near_a, v.near_b = swap_core(send_a), swap_core(send_b)

    def first_a():
        v.kept_a, v.far_a = add_near(v.keep_a, v.near_a)

    def first_b():
        v.kept_b, v.far_b = add_near(v.keep_b, v.near_b)

    def second_a():
        first_a()

    def second_b():
        first_b()

    def base():
        blocks = [
            (
                pos_table,
                (quarter, model_width),
                lambda ref, k=k: ref.at[pl.ds((2 * k + my_core()) * quarter, quarter)],
            )
            for k in range(2)
        ]
        v.base_a, v.base_b = call(
            base_rows, [rows32] * 2, [], fetch=blocks + [lead_table], smem=[lead_bucket]
        )

    def norm_a():
        v.in_a, v.one_a0 = norm_rows([v.kept_a, v.far_a, v.base_a], gain_one, bias_one)
        v.one_a1 = swap_core(v.one_a0)

    def proj():
        (v.proj_a,) = call(project, [proj_kind], [v.one_a0, v.one_a1, w_attn])

    def norm_b():
        v.in_b, v.one_b0, v.cot_own = call(
            norm_relay,
            [rows32, cut16, rows16],
            [cotangent, v.kept_b, v.far_b, v.base_b, gain_one, bias_one],
        )
        v.one_b1 = swap_core(v.one_b0)
        v.cot_far = swap_chip(v.cot_own)

    def attend_a():
        v.proj_b, v.attended_a, v.logs_a, v.keep_a, send_a = call(
            attend_first,
            [proj_kind] + attend_kinds,
            [v.one_b0, v.one_b1, w_attn, v.proj_a, attn_output],
        )
        v.near_a = swap_core(send_a)

    def attend_b():
        v.attended_b, v.logs_b, v.keep_b, send_b = call(
            attend_second, attend_kinds, [v.proj_a, v.proj_b, attn_output]
        )
        v.near_b = swap_core(send_b)

    def cot():
        v.cot_a0, v.cot_b0 = call(by_chip, [cut16] * 2, [v.cot_own, v.cot_far])
        v.cot_a1, v.cot_b1 = swap_core(v.cot_a0), swap_core(v.cot_b0)

    def hidden_a():
        (v.grad_hidden_a,) = call(hidden_back, [hidden_kind], [v.cot_a0, v.cot_a1, down_weight])

    def hidden_b():
        (v.grad_hidden_b,) = call(hidden_back, [hidden_kind], [v.cot_b0, v.cot_b1, down_weight])

    def two_a():
        v.mid_a, v.two_a0 = norm_rows([v.kept_a, v.far_a, v.in_a], gain_two, bias_two)
        v.two_a1 = swap_core(v.two_a0)

    def two_b():
        v.mid_b, v.two_b0 = norm_rows([v.kept_b, v.far_b, v.in_b], gain_two, bias_two)
        v.two_b1 = swap_core(v.two_b0)

    def mlp_a():
        v.hidden_a, v.pre_a, v.m_keep_a, send_a = call(
            mlp, mlp_kinds, [v.two_a0, v.two_a1, up_weight, v.grad_hidden_a]
        )
        v.m_near_a = swap_core(send_a)

    def mlp_b():
        v.hidden_b, v.pre_b, v.m_keep_b, send_b = call(
            mlp, mlp_kinds, [v.two_b0, v.two_b1, up_weight, v.grad_hidden_b]
        )
        v.m_near_b = swap_core(send_b)

    def third_a():
        v.m_kept_a, v.m_far_a = add_near(v.m_keep_a, v.m_near_a)

    def third_b():
        v.m_kept_b, v.m_far_b = add_near(v.m_keep_b, v.m_near_b)

    def down_in():
        return [v.cot_a0, v.cot_a1, v.cot_b0, v.cot_b1, v.hidden_a, v.hidden_b]

    def up_in():
        return [v.two_a0, v.two_a1, v.two_b0, v.two_b1, v.pre_a, v.pre_b]

    def attn_in():
        one = [v.one_a0, v.one_a1, v.one_b0, v.one_b1]
        mid = [v.back_a0, v.back_a1, v.back_b0, v.back_b1]
        return one + mid + [v.grad_proj, v.attended_a, v.attended_b]

    def up_1():
        v.up_got = start_sum(load_plain, up_in(), hidden_width, up_order)

    def down_1():
        v.down_got = start_sum(load_plain, down_in(), hidden_width, down_order)

    def attn_1():
        v.attn_got = start_sum(load_attn, attn_in(), attn_width, attn_order)

    def up_2():
        v.up_keep, v.up_got = second_sum(load_plain, up_in(), v.up_got, hidden_width, up_order)

    def down_2():
        v.down_keep, v.down_got = second_sum(
            load_plain, down_in(), v.down_got, hidden_width, down_order
        )

    def attn_2():
        v.attn_keep, v.attn_got = second_sum(
            load_attn, attn_in(), v.attn_got, attn_width, attn_order
        )

    def up_3():
        v.up_keep, v.up_got = rest_sum(v.up_keep, v.up_got, up_order)

    def down_3():
        v.down_keep, v.down_got = rest_sum(v.down_keep, v.down_got, down_order)

    def attn_3():
        v.attn_keep, v.attn_got = rest_sum(v.attn_keep, v.attn_got, attn_order)

    def mid_a():
        v.grad_mid_a, v.back_a0, v.sums_two_a = call(
            back_two, back_kinds, [v.m_kept_a, v.m_far_a, v.mid_a, gain_two, v.cot_a0]
        )
        v.back_a1 = swap_core(v.back_a0)

    def mid_b():
        v.grad_mid_b, v.back_b0, v.sums_two_b = call(
            back_two, back_kinds, [v.m_kept_b, v.m_far_b, v.mid_b, gain_two, v.cot_b0]
        )
        v.back_b1 = swap_core(v.back_b0)

    def back_a():
        v.query_grad, v.key_grad, v.value_grad = call(
            attend_back_first,
            grad_kinds,
            [v.back_a0, v.back_a1, attn_output, v.proj_a, v.proj_b, v.logs_a],
        )

    def back_b():
        v.grad_proj, v.p_keep_a, send_a = call(
            attend_back_second,
            [((3, length, head_width), BF16), rows32, cut16],
            [
                v.back_b0,
                v.back_b1,
                attn_output,
                v.proj_a,
                v.proj_b,
                v.logs_b,
                v.query_grad,
                v.key_grad,
                v.value_grad,
                w_attn,
            ],
        )
        v.p_near_a = swap_core(send_a)

    def back_c():
        v.p_keep_b, send_b = call(attend_back_last, [rows32, cut16], [v.grad_proj, w_attn])
        v.p_near_b = swap_core(send_b)

    def fourth_a():
        v.p_kept_a, v.p_far_a = add_near(v.p_keep_a, v.p_near_a)

    def fourth_b():
        v.p_kept_b, v.p_far_b = add_near(v.p_keep_b, v.p_near_b)

    def in_a():
        v.grad_in_a, v.in_a0, v.sums_one_a = call(
            functools.partial(norm_backward, True, 0),
            back_kinds,
            [v.p_kept_a, v.p_far_a, v.in_a, gain_one, v.grad_mid_a],
        )
        v.in_a1 = swap_core(v.in_a0)

    def in_b():
        v.grad_in_b, v.in_b0, v.sums = call(
            functools.partial(norm_backward, True, 3),
            back_kinds,
            [
                v.p_kept_b,
                v.p_far_b,
                v.in_b,
                gain_one,
                v.grad_mid_b,
                v.sums_one_a,
                v.sums_two_a,
                v.sums_two_b,
            ],
        )
        v.in_b1 = swap_core(v.in_b0)
        v.near_sums = swap_core(v.sums)

    def mass_1():
        packed, v.mass, v.bias, v.field_send, v.field_keep = call(
            functools.partial(mix_backward, pixels),
            mass_kinds + [((channels, half), BF16), ((channels, half), F32)],
            [v.pick, v.field_t, v.probs, v.values, v.score, mix_output, v.in_a0, v.in_a1, v.in_b0, v.in_b1],
        )
        v.mass_got = swap_sample(packed, mass_bits[0])
        v.field_near = swap_core(v.field_send)

    def add_masses(bits):
        for bit in bits:
            packed, v.mass, v.bias = call(mass_add, mass_kinds, [v.mass, v.bias, v.mass_got])
            v.mass_got = swap_sample(packed, bit)

    def mass_2():
        add_masses(mass_bits[1:2])

    def mass_3():
        add_masses(mass_bits[2:])

    def mix_in():
        rows = [v.in_a0, v.in_a1, v.in_b0, v.in_b1]
        return rows + [v.grad_in_a, v.grad_in_b, v.sums, v.near_sums]

    def mix_1():
        (send,) = call(
            functools.partial(mix_start, mesh_dp, lines, mix_steps[0], mix_order[0]),
            [((model_width // 2, mix_width), BF16)],
            [v.mixed_t] + mix_in(),
            smem=[lead_bucket],
            scratch=[rest_rows],
        )
        v.mix_got = swap_sample(send, mix_order[0])

    def mix_2():
        v.mix_keep, send = call(
            functools.partial(
                mix_second, mesh_dp, lines, mix_steps[0], mix_steps[1], mix_order[0], mix_order[1]
            ),
            halves(mix_width, model_width // 2),
            [v.mixed_t, v.mix_got] + mix_in(),
            smem=[lead_bucket],
            scratch=[rest_rows, pltpu.VMEM((model_width // 2, mix_width), F32)],
        )
        v.mix_got = swap_sample(send, mix_order[1])

    def mix_3():
        v.mix_keep, v.mix_got = rest_sum(v.mix_keep, v.mix_got, mix_order)

    def field_1():
        v.field_own, far = call(
            field_sum, [(own_field, F32), (own_field, BF16)], [v.field_keep, v.field_near]
        )
        v.field_got = swap_chip(far)

    def field_2():
        (v.field_grad,) = call(
            field_last, [((1,) + own_field, F32)], [v.field_own, v.field_got], final=True
        )

    def rows_1():
        v.r_keep_a, send_a, v.r_keep_b, send_b = call(
            mlp_out, [rows32, cut16] * 2, [v.hidden_a, v.hidden_b, down_weight]
        )
        v.r_near_a, v.r_near_b = swap_core(send_a), swap_core(send_b)

    def rows_2():
        v.rows_own, far = call(
            rows_sum,
            [rows32, rows16],
            [v.r_keep_a, v.r_near_a, v.r_keep_b, v.r_near_b, v.mid_a, v.mid_b],
        )
        v.rows_got = swap_chip(far)

    def rows_3():
        (v.activations,) = call(last_plain, [rows32], [v.rows_own, v.rows_got], final=True)

    def weights():
        v.own_weights, v.pick = call(
            functools.partial(take_weights, pixels),
            [((3, own_width, head_width), BF16), ((channels, channels), BF16)],
            [],
            smem=[variable_ids],
            fetch=[
                (
                    w_mix,
                    (3, own_width, head_width),
                    lambda ref: ref.at[:, pl.ds(lax.axis_index("dp") * own_width, own_width)],
                )
            ],
        )

    def finish():
        v.t_keep, send, v.grad_mix = call(
            functools.partial(mix_finish, pixels),
            [((own_width // 2, padded), F32)] * 2 + [((3, own_width, head_width), F32)],
            [
                v.query_col,
                v.keys_t,
                patch_table,
                variable_table,
                v.mass,
                v.bias,
                v.mass_got,
                v.own_weights,
                variable_query,
            ],
            scratch=[pltpu.VMEM((own_width, padded), F32)],
        )
        v.t_far = swap_chip(send)

    def tables_1():
        v.t_keep, send = call(
            tables_next,
            [((final, padded), F32)] * 2,
            [v.t_keep, v.t_far],
            scratch=[pltpu.VMEM((own_width // 2, padded), F32)],
        )
        v.t_near = swap_core(send)

    def tables_2():
        v.patch_total, v.variable_total, v.query_total = call(
            functools.partial(tables_last, pixels, variables),
            [((pixels, final, variables), F32), ((final, variables), F32), ((8, final), F32)],
            [v.t_keep, v.t_near],
            final=True,
        )

    def down_4():
        (v.down_sum,) = call(
            last_turned, [((hidden_width, own_width), F32)], [v.down_keep, v.down_got], final=True
        )

    def up_4():
        (v.up_sum,) = call(
            last_plain, [((own_width, hidden_width), F32)], [v.up_keep, v.up_got], final=True
        )

    def mix_4():
        v.mix_out_sum, v.pos_sum, v.lead_total, v.small = call(
            functools.partial(mix_last, mesh_dp, quarter, final),
            [
                ((head_width, own_width), F32),
                ((quarter, own_width), F32),
                ((final, lead_table.shape[0]), F32),
                ((8, final), F32),
            ],
            [v.mix_keep, v.mix_got],
            final=True,
        )

    def attn_4():
        v.attn_sum, v.attn_out_sum = call(
            last_attn,
            [((3, own_width, head_width), F32), ((head_width, own_width), F32)],
            [v.attn_keep, v.attn_got],
            final=True,
        )

    steps = dict(locals())
    for name in ORDER:
        now[:] = [name]
        steps[name]()
    return (
        v.activations,
        v.field_grad,
        v.patch_total.transpose(2, 0, 1),
        v.variable_total.T,
        v.query_total[7],
        v.grad_mix.transpose(1, 0, 2),
        v.mix_out_sum,
        v.pos_sum,
        v.lead_total.T,
        v.small[0],
        v.small[1],
        v.attn_sum.transpose(1, 0, 2),
        v.attn_out_sum,
        v.small[2],
        v.small[3],
        v.up_sum,
        v.down_sum,
    )


def solution(mesh):
    in_specs = (
        P("dp", None, None),
        P(),
        P("dp"),
        P(),
        P(),
        P(),
        P(None, None, "mp"),
        P("mp", None),
        P(),
        P(),
        P(),
        P(),
        P(None, None, "mp"),
        P("mp", None),
        P(),
        P(),
        P(None, "mp"),
        P("mp", None),
        P(("dp", "mp"), None),
    )
    out_specs = (
        P(("dp", "mp"), None),
        P("dp", None, "mp"),
        P(None, None, ("dp", "mp")),
        P(None, ("dp", "mp")),
        P(("dp", "mp")),
        P("dp", None, "mp"),
        P("mp", "dp"),
        P("mp", "dp"),
        P(None, ("dp", "mp")),
        P(("dp", "mp")),
        P(("dp", "mp")),
        P("dp", None, "mp"),
        P("mp", "dp"),
        P(("dp", "mp")),
        P(("dp", "mp")),
        P("dp", "mp"),
        P("mp", "dp"),
    )
    step = functools.partial(body, mesh.shape["dp"], mesh.shape["mp"])
    return jax.shard_map(step, mesh=mesh, in_specs=in_specs, out_specs=out_specs, check_vma=False)
```

```python
import functools
import types

import jax
import jax.numpy as jnp
from jax import lax
from jax.experimental import pallas as pl
from jax.experimental.pallas import tpu as pltpu
from jax.sharding import PartitionSpec as P

HEAD_DIM = 64
LANES = 128
EPS = 1e-05
SCALE = HEAD_DIM ** (-0.5)
HIGH = lax.Precision.HIGHEST
F32 = jnp.float32
BF16 = jnp.bfloat16
VMEM = pl.BlockSpec(memory_space=pltpu.VMEM)
SMEM = pl.BlockSpec(memory_space=pltpu.SMEM)
ANY = pl.BlockSpec(memory_space=pl.ANY)
HBM = pl.BlockSpec(memory_space=pltpu.HBM)
MIB = 1024 * 1024
FIRST_LIMIT = 60
PIECES = 2
AXES = ((0, 1, 2), (1, 2, 0), (0, 1, 2), (0, 1, 2), (1, 0, 2))
ORDER = (
    "mix_a", "mix_b", "first_a", "first_b", "base", "norm_a", "proj", "norm_b", "attend_a", "second_a", "cot",
    "attend_b", "hidden_a", "second_b", "two_a", "hidden_b", "mlp_a", "third_a", "two_b", "mlp_b", "down_1",
    "up_1", "mid_a", "third_b", "back_a", "mid_b", "back_b", "attn_1", "fourth_a", "back_c", "fourth_b",
    "down_2", "up_2", "weights", "in_a", "in_b", "mass_1", "mix_1", "down_3", "attn_2", "up_3", "mass_2",
    "mass_3", "rows_1", "down_4", "rows_2", "mix_2", "field_1", "attn_3", "finish", "tables_1", "mix_3",
    "rows_3", "field_2", "up_4", "attn_4", "tables_2", "mix_4",
)
COSTS = {
    "norm_a": 12,
    "second_a": 0.5,
    "second_b": 1,
    "cot": 1,
    "hidden_b": 3,
    "weights": 1,
    "two_a": 6.4,
    "mlp_a": 0.4,
    "third_a": 1,
    "mlp_b": 1,
    "back_a": 1.6,
    "back_c": 0.5,
    "fourth_a": 0.5,
    "attn_1": 0.5,
    "up_2": 2,
    "mass_2": 0.5,
    "field_2": 0.4,
    "up_3": 0.5,
    "tables_1": 1,
    "tables_2": 0.5,
}


def dot(left, right, left_dim=1, right_dim=0, precision=None):
    return lax.dot_general(
        left,
        right,
        (((left_dim,), (right_dim,)), ((), ())),
        precision=precision,
        preferred_element_type=F32,
    )


class Rows:
    def __init__(self, refs):
        self.refs = refs
        self.shape = (sum(ref.shape[0] for ref in refs),) + refs[0].shape[1:]

    def __getitem__(self, at):
        return jnp.concatenate([ref[at] for ref in self.refs], axis=0)

    def __setitem__(self, at, value):
        step = self.refs[0].shape[0]
        for i, ref in enumerate(self.refs):
            ref[...] = value[i * step : (i + 1) * step]


def gather_refs(refs, counts):
    refs, grouped = list(refs), []
    for count in counts:
        grouped.append(refs.pop(0) if count is None else Rows([refs.pop(0) for _ in range(count)]))
    return grouped


def flat(items):
    out, counts = [], []
    for item in items:
        pieces = isinstance(item, list)
        out.extend(item if pieces else [item])
        counts.append(len(item) if pieces else None)
    return out, counts


def launch(kernel, outs, args, fetch=(), smem=(), after=(), limit=24, scratch=(), cost=0.1, name=None, lazy=False):
    fetch = [item if isinstance(item, tuple) else (item, item.shape, None) for item in fetch]
    args, arg_counts = flat(args)
    outs, out_counts = flat(outs)
    count = len(smem)

    def run(*refs):
        at = count + len(fetch)
        sources, rest = refs[count:at], refs[at:]
        inputs, rest = gather_refs(rest[: len(args)], arg_counts), rest[len(args) + len(after) :]
        results, rest = gather_refs(rest[: len(outs)], out_counts), rest[len(outs) :]
        if not fetch:
            kernel(*refs[:count], *inputs, *results, *rest)
            return
        *rest, marks = rest
        rest, places = rest[: len(rest) - len(fetch)], rest[len(rest) - len(fetch) :]
        copies = []
        for i, (_, _, pick) in enumerate(fetch):
            source = sources[i] if pick is None else pick(sources[i])
            copies.append(pltpu.make_async_copy(source, places[i], marks.at[i]))
        for copy in copies:
            copy.start()
        if lazy:
            kernel([copy.wait for copy in copies], *refs[:count], *places, *inputs, *results, *rest)
            return
        for copy in copies:
            copy.wait()
        kernel(*refs[:count], *places, *inputs, *results, *rest)

    places = [
        (pltpu.SMEM if array.dtype == jnp.int32 else pltpu.VMEM)(shape, array.dtype)
        for array, shape, _ in fetch
    ]
    marks = [pltpu.SemaphoreType.DMA((len(fetch),))] if fetch else []
    results = pl.pallas_call(
        run,
        out_shape=[jax.ShapeDtypeStruct(shape, kind) for shape, kind in outs],
        in_specs=[SMEM] * count + [HBM] * len(fetch) + [VMEM] * len(args) + [ANY] * len(after),
        out_specs=[VMEM] * len(outs),
        scratch_shapes=list(scratch) + places + marks,
        name=name,
        compiler_params=pltpu.CompilerParams(vmem_limit_bytes=limit * MIB),
        cost_estimate=pl.CostEstimate(
            flops=int(cost * 1e9), bytes_accessed=0, transcendentals=0
        ),
    )(*smem, *(array for array, _, _ in fetch), *args, *after)
    results, grouped = list(results), []
    for pieces in out_counts:
        grouped.append(results.pop(0) if pieces is None else [results.pop(0) for _ in range(pieces)])
    return grouped


def marked(kernel, *refs):
    *rest, mark_ref = refs
    mark_ref[...] = jnp.zeros_like(mark_ref)
    kernel(*rest)


def my_bit(bit):
    return (lax.axis_index("dp") // bit) % 2


def my_core():
    return lax.axis_index("mp") % 2


def my_chip():
    return lax.axis_index("mp") // 2


def iota(shape, dim):
    return lax.broadcasted_iota(jnp.int32, shape, dim)


def exact(mask):
    return mask.astype(F32).astype(BF16)


def lanes_of(rows, head):
    lane = iota((1, rows.shape[1]), 1)
    mine = (lane >= head * HEAD_DIM) & (lane < (head + 1) * HEAD_DIM)
    return jnp.where(mine, rows, jnp.zeros_like(rows))


def spread(rows, pixels, top, bottom):
    variables = top.shape[0]
    parts = [top * rows[p * variables : (p + 1) * variables] for p in range(pixels)]
    parts.append(top)
    if bottom:
        parts.append(jnp.zeros((bottom, top.shape[1]), top.dtype))
    return jnp.concatenate(parts, axis=0)


def pixel_major(channels, pixels):
    variables = channels // pixels
    row = iota((channels, channels), 0)
    major = jnp.zeros((channels, channels), jnp.int32)
    for p in range(pixels):
        inside = (row >= p * variables) & (row < (p + 1) * variables)
        major = jnp.where(inside, (row - p * variables) * pixels + p, major)
    return exact(iota((channels, channels), 1) == major)


def places(ids_ref, variables, pixels):
    channels = variables * pixels
    channel = iota((1, channels), 1)
    place = jnp.zeros((1, channels), jnp.int32)
    for v in range(variables):
        pixel = channel - v * pixels
        inside = (pixel >= 0) & (pixel < pixels)
        place = jnp.where(inside, pixel * variables + ids_ref[v], place)
    return place


def mix_forward(
    pixels,
    quarter,
    waits,
    ids_ref,
    x_ref,
    patch_ref,
    variable_ref,
    w_ref,
    query_ref,
    mixed_ref,
    xt_ref,
    probs_ref,
    values_ref,
    keys_t_ref,
    score_ref,
    query_col_ref,
    table_ref,
):
    channels = x_ref.shape[1]
    variables = channels // pixels
    rows, model_width = table_ref.shape
    width = w_ref.shape[2]
    heads = width // HEAD_DIM
    bottom = rows - channels - variables
    wait_ids, wait_field, wait_patch, wait_variable, wait_weights, wait_query = waits
    wait_patch()
    flat = patch_ref[...].reshape(channels, model_width)
    table_ref[0:channels] = dot(pixel_major(channels, pixels), flat).astype(BF16)
    wait_variable()
    table_ref[channels : channels + variables] = variable_ref[...]
    if bottom:
        table_ref[channels + variables :] = jnp.zeros((bottom, model_width), BF16)
    wait_ids()
    pick = (iota((channels, channels), 0) == places(ids_ref, variables, pixels)).astype(F32)
    wait_field()
    core = my_core()
    starts = [core, 1 - core, core + 2, 3 - core]
    field = jnp.concatenate(
        [x_ref[0, :, pl.ds(pl.multiple_of(s * quarter, LANES), quarter)] for s in starts], axis=1
    )
    xt = dot(pick.astype(BF16), field)
    xt_ref[...] = xt.astype(BF16)
    wait_weights()
    wait_query()
    query_rows = jnp.broadcast_to(query_ref[...].astype(F32)[None], (16, model_width)).astype(BF16)
    query = dot(query_rows, w_ref[0])[0:1].astype(BF16).astype(F32)
    table = table_ref[...]
    keys = dot(table, w_ref[1])
    values = dot(table, w_ref[2])
    values_ref[...] = values.astype(BF16)
    keys_t_ref[...] = keys.T
    query_col_ref[...] = jnp.broadcast_to(query, (LANES, width)).T
    lane = iota((width, LANES), 1) * HEAD_DIM
    row = iota((width, LANES), 0)
    same = ((row >= lane) & (row < lane + HEAD_DIM)).astype(F32)
    score = dot(keys * query, same, precision=HIGH) * SCALE
    score_ref[...] = score
    values_t = values.T.astype(BF16)
    for head in range(heads):
        column = score[:, head : head + 1]
        logits = jnp.broadcast_to(column[channels : channels + variables], (variables, xt.shape[1]))
        for p in range(pixels):
            part = slice(p * variables, (p + 1) * variables)
            logits = logits + column[part] * xt[part]
        weights = jnp.exp(logits - jnp.max(logits, axis=0, keepdims=True))
        probs = weights / jnp.sum(weights, axis=0, keepdims=True)
        probs_ref[head * variables : (head + 1) * variables] = probs
        low = probs.astype(BF16).astype(F32)
        mixing = spread(xt, pixels, low, bottom).astype(BF16)
        part = slice(head * HEAD_DIM, (head + 1) * HEAD_DIM)
        mixed_ref[part] = dot(values_t[part], mixing).astype(BF16)


def mix_out(mixed_ref, w_out_ref, send_a_ref, send_b_ref, keep_a_ref, keep_b_ref):
    quarter = keep_a_ref.shape[0]
    out = dot(mixed_ref[...], w_out_ref[...], 0, 0)
    keep_a_ref[...] = out[0:quarter]
    send_a_ref[...] = out[quarter : 2 * quarter].astype(BF16)
    keep_b_ref[...] = out[2 * quarter : 3 * quarter]
    send_b_ref[...] = out[3 * quarter :].astype(BF16)


def pack_mass(mass, bias, packed_ref):
    width = mass.shape[0]
    high = bias.astype(BF16).astype(F32)
    packed_ref[0:width] = mass.astype(BF16)
    packed_ref[width:] = jnp.concatenate([high, bias - high], axis=0).astype(BF16)


def add_mass(mass_ref, bias_ref, got_ref):
    width = mass_ref.shape[0]
    more = got_ref[width:].astype(F32)
    return mass_ref[...] + got_ref[0:width].astype(F32), bias_ref[...] + more[0:8] + more[8:16]


def mix_backward(
    pixels,
    pick_ref,
    xt_ref,
    probs_ref,
    values_ref,
    score_ref,
    w_out_ref,
    a0_ref,
    a1_ref,
    b0_ref,
    b1_ref,
    packed_ref,
    mass_ref,
    bias_ref,
    field_send_ref,
    field_keep_ref,
):
    channels, length = xt_ref.shape
    variables = channels // pixels
    rows, width = values_ref.shape
    heads = width // HEAD_DIM
    bottom = rows - channels - variables
    quarter = length // 4
    xt = xt_ref[...].astype(F32)
    grad = jnp.concatenate([a0_ref[...], a1_ref[...], b0_ref[...], b1_ref[...]], axis=0)
    grad_t = dot(w_out_ref[...], grad, 1, 1).astype(BF16)
    values = values_ref[...]
    score = score_ref[...]
    field = jnp.zeros(xt.shape, F32)
    lane = iota((rows, LANES), 1)
    sums = jnp.zeros((rows, LANES), F32)
    for head in range(heads):
        probs = probs_ref[head * variables : (head + 1) * variables]
        low = probs.astype(BF16).astype(F32)
        back = dot(lanes_of(values, head), grad_t)
        prob_grad = back[channels : channels + variables]
        for p in range(pixels):
            part = slice(p * variables, (p + 1) * variables)
            prob_grad = prob_grad + xt[part] * back[part]
        middle = jnp.sum(probs * prob_grad, axis=0, keepdims=True)
        score_grad = probs * (prob_grad - middle)
        column = score[:, head : head + 1]
        field = field + jnp.concatenate(
            [
                score_grad * column[p * variables : (p + 1) * variables]
                + low * back[p * variables : (p + 1) * variables]
                for p in range(pixels)
            ],
            axis=0,
        )
        spreading = spread(xt, pixels, score_grad * SCALE, bottom)
        sums = jnp.where(lane == head, jnp.sum(spreading, axis=1, keepdims=True), sums)
        mixing = spread(xt, pixels, low, bottom).astype(BF16)
        part = slice(head * HEAD_DIM, (head + 1) * HEAD_DIM)
        mass_ref[part] = dot(grad_t[part], mixing, 1, 1)
    bias_ref[...] = sums.T[0:8]
    pack_mass(mass_ref[...], bias_ref[...], packed_ref)
    field = dot(pick_ref[...], field.astype(BF16))
    field_keep_ref[:, 0:quarter] = field[:, 0:quarter]
    field_keep_ref[:, quarter:] = field[:, 2 * quarter : 3 * quarter]
    field_send_ref[:, 0:quarter] = field[:, quarter : 2 * quarter].astype(BF16)
    field_send_ref[:, quarter:] = field[:, 3 * quarter :].astype(BF16)


def norm_forward(*refs):
    *terms, gain_ref, bias_ref, out_ref, low_ref = refs
    total = terms[0][...].astype(F32)
    for term in terms[1:]:
        total = total + term[...].astype(F32)
    out_ref[...] = total
    centered = total - jnp.mean(total, axis=1, keepdims=True)
    inv_std = lax.rsqrt(jnp.mean(centered * centered, axis=1, keepdims=True) + EPS)
    low_ref[...] = (centered * inv_std * gain_ref[...] + bias_ref[...]).astype(BF16)


def norm_relay(pass_ref, *refs):
    *refs, out_ref = refs
    out_ref[...] = pass_ref[...]
    norm_forward(*refs)


def norm_backward(with_sum, add_refs, *refs):
    keep_ref, far_ref, rows_ref, gain_ref, above_ref = refs[:5]
    more = refs[5 : 5 + add_refs]
    out_ref, low_ref, sums_ref = refs[5 + add_refs :]
    grad = keep_ref[...] + far_ref[...].astype(F32)
    rows = rows_ref[...]
    centered = rows - jnp.mean(rows, axis=1, keepdims=True)
    inv_std = lax.rsqrt(jnp.mean(centered * centered, axis=1, keepdims=True) + EPS)
    normed = centered * inv_std
    scaled = grad * gain_ref[...]
    first = jnp.mean(scaled, axis=1, keepdims=True)
    second = jnp.mean(scaled * normed, axis=1, keepdims=True)
    out = above_ref[...].astype(F32) + inv_std * (scaled - first - normed * second)
    out_ref[...] = out
    low_ref[...] = out.astype(BF16)
    lines = [
        jnp.sum(grad * normed, axis=0, keepdims=True),
        jnp.sum(grad, axis=0, keepdims=True),
    ]
    lines.append(jnp.sum(out, axis=0, keepdims=True) if with_sum else jnp.zeros_like(lines[0]))
    if add_refs:
        one, two_a, two_b = (ref[...] for ref in more)
        lines = [
            lines[0] + one[0:1],
            lines[1] + one[1:2],
            two_a[0:1] + two_b[0:1],
            two_a[1:2] + two_b[1:2],
            lines[2] + one[2:3],
        ]
    lines.append(jnp.zeros((8 - len(lines), grad.shape[1]), F32))
    sums_ref[...] = jnp.concatenate(lines, axis=0)


def project(own_ref, near_ref, w_ref, out_ref):
    rows = jnp.concatenate([own_ref[...], near_ref[...]], axis=0)
    for i in range(3):
        out_ref[i] = dot(rows, w_ref[i]).astype(BF16)


def attend(query, keys, values_t, logs_ref):
    scaled = (query.astype(F32) * SCALE).astype(BF16)
    parts = []
    for head in range(keys.shape[1] // HEAD_DIM):
        scores = dot(keys, lanes_of(scaled, head), 1, 1)
        top = jnp.max(scores, axis=0, keepdims=True)
        weights = jnp.exp(scores - top)
        total = jnp.sum(weights, axis=0, keepdims=True)
        logs_ref[head : head + 1] = top + jnp.log(total)
        part = dot(values_t[head * HEAD_DIM : (head + 1) * HEAD_DIM], weights.astype(BF16))
        parts.append(part * (1.0 / total))
    return jnp.concatenate(parts, axis=0).T.astype(BF16)


def split_out(out, keep_ref, send_ref):
    quarter = out.shape[0] // 2
    keep_ref[...] = out[:quarter]
    send_ref[...] = out[quarter:].astype(BF16)


def attend_first(own_ref, near_ref, w_ref, first_ref, w_out_ref, second_ref, out_ref, logs_ref, keep_ref, send_ref):
    project(own_ref, near_ref, w_ref, second_ref)
    keys = jnp.concatenate([first_ref[1], second_ref[1]], axis=0)
    values = jnp.concatenate([first_ref[2], second_ref[2]], axis=0)
    out_ref[...] = attend(first_ref[0], keys, values.T, logs_ref)
    split_out(dot(out_ref[...], w_out_ref[...]), keep_ref, send_ref)


def attend_second(first_ref, second_ref, w_out_ref, out_ref, logs_ref, keep_ref, send_ref):
    keys = jnp.concatenate([first_ref[1], second_ref[1]], axis=0)
    values = jnp.concatenate([first_ref[2], second_ref[2]], axis=0)
    out_ref[...] = attend(second_ref[0], keys, values.T, logs_ref)
    split_out(dot(out_ref[...], w_out_ref[...]), keep_ref, send_ref)


def attend_grad(grad, query, keys, values, logs_ref):
    scaled = (query.astype(F32) * SCALE).astype(BF16)
    keys_t = keys.T
    query_parts = []
    key_grad = jnp.zeros(keys.shape, F32)
    value_grad = jnp.zeros(keys.shape, F32)
    for head in range(keys.shape[1] // HEAD_DIM):
        head_query, head_grad = lanes_of(scaled, head), lanes_of(grad, head)
        scores = dot(keys, head_query, 1, 1)
        probs = jnp.exp(scores - logs_ref[head : head + 1])
        prob_grad = dot(values, head_grad, 1, 1)
        middle = jnp.sum(probs * prob_grad, axis=0, keepdims=True)
        score_grad = (probs * (prob_grad - middle)).astype(BF16)
        query_parts.append(dot(keys_t[head * HEAD_DIM : (head + 1) * HEAD_DIM], score_grad))
        key_grad = key_grad + dot(score_grad, head_query)
        value_grad = value_grad + dot(probs.astype(BF16), head_grad)
    query_grad = (jnp.concatenate(query_parts, axis=0).T * SCALE).astype(BF16)
    return query_grad, key_grad, value_grad


def attend_back_first(own_ref, near_ref, w_out_ref, first_ref, second_ref, logs_ref, query_ref, key_ref, value_ref):
    rows = jnp.concatenate([own_ref[...], near_ref[...]], axis=0)
    grad = dot(rows, w_out_ref[...], 1, 1).astype(BF16)
    keys = jnp.concatenate([first_ref[1], second_ref[1]], axis=0)
    values = jnp.concatenate([first_ref[2], second_ref[2]], axis=0)
    query_ref[...], key_ref[...], value_ref[...] = attend_grad(
        grad, first_ref[0], keys, values, logs_ref
    )


def project_back(rows_ref, start, count, w_ref):
    total = dot(rows_ref[0, start : start + count], w_ref[0], 1, 1)
    for i in range(1, 3):
        total = total + dot(rows_ref[i, start : start + count], w_ref[i], 1, 1)
    return total


def attend_back_second(
    own_ref,
    near_ref,
    w_out_ref,
    first_ref,
    second_ref,
    logs_ref,
    query_ref,
    key_ref,
    value_ref,
    w_ref,
    out_ref,
    keep_ref,
    send_ref,
):
    rows = jnp.concatenate([own_ref[...], near_ref[...]], axis=0)
    half = rows.shape[0]
    grad = dot(rows, w_out_ref[...], 1, 1).astype(BF16)
    keys = jnp.concatenate([first_ref[1], second_ref[1]], axis=0)
    values = jnp.concatenate([first_ref[2], second_ref[2]], axis=0)
    query_grad, key_grad, value_grad = attend_grad(grad, second_ref[0], keys, values, logs_ref)
    out_ref[0, 0:half] = query_ref[...]
    out_ref[0, half:] = query_grad
    out_ref[1] = (key_ref[...] + key_grad).astype(BF16)
    out_ref[2] = (value_ref[...] + value_grad).astype(BF16)
    split_out(project_back(out_ref, 0, half, w_ref), keep_ref, send_ref)


def attend_back_last(rows_ref, w_ref, keep_ref, send_ref):
    half = rows_ref.shape[1] // 2
    split_out(project_back(rows_ref, half, half, w_ref), keep_ref, send_ref)


def hidden_back(own_ref, near_ref, w_ref, out_ref):
    rows = jnp.concatenate([own_ref[...], near_ref[...]], axis=0)
    out_ref[...] = dot(rows, w_ref[...], 1, 1)


ROOT = 0.7978845608028654
CUBE = 0.044715


def mlp(own_ref, near_ref, w_ref, grad_ref, hidden_ref, out_ref, keep_ref, send_ref):
    rows = jnp.concatenate([own_ref[...], near_ref[...]], axis=0)
    pre = dot(rows, w_ref[...])
    square = pre * pre
    bend = jnp.tanh(ROOT * pre * (1.0 + CUBE * square))
    half = 0.5 * (1.0 + bend)
    hidden_ref[...] = (pre * half).astype(BF16)
    slope = half + (0.5 * ROOT) * pre * (1.0 - bend * bend) * (1.0 + (3.0 * CUBE) * square)
    out_ref[...] = (slope * grad_ref[...]).astype(BF16)
    split_out(dot(out_ref[...], w_ref[...], 1, 1), keep_ref, send_ref)


def mlp_out(first_ref, second_ref, w_ref, keep_a_ref, send_a_ref, keep_b_ref, send_b_ref):
    split_out(dot(first_ref[...], w_ref[...]), keep_a_ref, send_a_ref)
    split_out(dot(second_ref[...], w_ref[...]), keep_b_ref, send_b_ref)


def grad_rows(parts, step, width, which):
    groups = width // (2 * step)
    outs = []
    for group in range(groups):
        start = pl.multiple_of((2 * group + which) * step, LANES)
        line = []
        for left, rights in parts:
            picked = jnp.concatenate([ref[:, pl.ds(start, step)] for ref in left], axis=0)
            line.extend(dot(picked, right, 0, 0) for right in rights)
        outs.append(line)
    return outs, groups


def write_half(ref, parts, step, width, which, dtype):
    outs, groups = grad_rows(parts, step, width, which)
    for group in range(groups):
        column = 0
        for value in outs[group]:
            ref[group * step : (group + 1) * step, column : column + value.shape[1]] = value.astype(dtype)
            column += value.shape[1]


def take_half(out_ref, source, step, which, dtype):
    for group in range(source.shape[0] // (2 * step)):
        start = pl.multiple_of((2 * group + which) * step, 16)
        out_ref[group * step : (group + 1) * step] = source[pl.ds(start, step)].astype(dtype)


def sum_start(load, step, bit, *refs):
    *inputs, out_ref = refs
    parts, width = load(inputs)
    write_half(out_ref, parts, step, width, 1 - my_bit(bit), BF16)


def sum_second(load, step, next_step, bit, next_bit, *refs):
    got_ref, *inputs, keep_ref, send_ref, total = refs
    parts, width = load(inputs)
    write_half(total, parts, step, width, my_bit(bit), F32)
    total[...] = total[...] + got_ref[...].astype(F32)
    take_half(send_ref, total, next_step, 1 - my_bit(next_bit), BF16)
    take_half(keep_ref, total, next_step, my_bit(next_bit), F32)


def sum_next(next_step, next_bit, kept_ref, got_ref, keep_ref, send_ref, total):
    total[...] = kept_ref[...] + got_ref[...].astype(F32)
    take_half(send_ref, total, next_step, 1 - my_bit(next_bit), BF16)
    take_half(keep_ref, total, next_step, my_bit(next_bit), F32)


def load_plain(inputs):
    *left, first, second = inputs
    right = jnp.concatenate([first[...], second[...]], axis=0)
    return [(left, [right])], left[0].shape[1]


def load_attn(inputs):
    left, middle = inputs[0:4], inputs[4:8]
    proj, first, second = inputs[8:]
    attended = jnp.concatenate([first[...], second[...]], axis=0)
    return [(left, [proj[0], proj[1], proj[2]]), (middle, [attended])], left[0].shape[1]


def last_plain(kept_ref, got_ref, out_ref):
    out_ref[...] = kept_ref[...] + got_ref[...].astype(F32)


def last_turned(kept_ref, got_ref, out_ref):
    out_ref[...] = (kept_ref[...] + got_ref[...].astype(F32)).T


def last_attn(kept_ref, got_ref, proj_ref, out_ref):
    total = kept_ref[...] + got_ref[...].astype(F32)
    width = proj_ref.shape[2]
    for i in range(3):
        proj_ref[i] = total[:, i * width : (i + 1) * width]
    out_ref[...] = total[:, 3 * width :].T


def mix_lines(samples, lines, bucket_ref, inputs, rest_ref):
    first_ref, second_ref, own_ref, near_ref = inputs
    quarter, width = first_ref.shape
    rest_ref[0:quarter] = jnp.where(my_chip() == 0, first_ref[...], second_ref[...])
    sample = lax.axis_index("dp")
    sums = own_ref[...] + near_ref[...]
    row = iota((lines, width), 0)
    filled = jnp.concatenate([sums, jnp.zeros((lines - 8, width), F32)], axis=0)
    filled = jnp.where(row < 4, filled, 0.0)
    filled = jnp.where(row == 4 + sample, sums[4:5], filled)
    bucket = bucket_ref[0].astype(F32)
    rest_ref[quarter:] = jnp.where(row == 4 + samples + sample, bucket, filled)


def write_mix(ref, step, which, left, mixed_ref, rest_ref, dtype):
    width = left[0].shape[1]
    heads_width = mixed_ref.shape[0]
    for group in range(width // (2 * step)):
        start = pl.multiple_of((2 * group + which) * step, LANES)
        picked = jnp.concatenate([part[:, pl.ds(start, step)] for part in left], axis=0)
        rows = slice(group * step, (group + 1) * step)
        ref[rows, 0:heads_width] = dot(picked, mixed_ref[...], 0, 1).astype(dtype)
        ref[rows, heads_width:] = rest_ref[:, pl.ds(start, step)].T.astype(dtype)


def mix_start(samples, lines, step, bit, bucket_ref, mixed_ref, *refs):
    *inputs, out_ref, rest = refs
    mix_lines(samples, lines, bucket_ref, inputs[4:], rest)
    write_mix(out_ref, step, 1 - my_bit(bit), inputs[:4], mixed_ref, rest, BF16)


def mix_second(samples, lines, step, next_step, bit, next_bit, bucket_ref, mixed_ref, *refs):
    got_ref, *inputs, keep_ref, send_ref, rest, total = refs
    mix_lines(samples, lines, bucket_ref, inputs[4:], rest)
    write_mix(total, step, my_bit(bit), inputs[:4], mixed_ref, rest, F32)
    total[...] = total[...] + got_ref[...].astype(F32)
    take_half(send_ref, total, next_step, 1 - my_bit(next_bit), BF16)
    take_half(keep_ref, total, next_step, my_bit(next_bit), F32)


def mix_last(samples, quarter, final, kept_ref, got_ref, out_ref, pos_ref, lead_ref, small_ref):
    total = kept_ref[...] + got_ref[...].astype(F32)
    heads_width = out_ref.shape[0]
    out_ref[...] = total[:, :heads_width].T
    pos_ref[...] = total[:, heads_width : heads_width + quarter].T
    rest = total[:, heads_width + quarter :]
    rows = max(final, 8)
    mine = iota((rows, rest.shape[0]), 1) == iota((rows, rest.shape[0]), 0) + lax.axis_index("mp") * final
    own = dot(mine.astype(F32), rest, precision=HIGH)
    bucket = iota((rows, lead_ref.shape[1]), 1).astype(F32)
    lead = jnp.zeros(bucket.shape, F32)
    for s in range(samples):
        mark = own[:, 4 + samples + s : 5 + samples + s]
        lead = jnp.where(bucket == mark, lead + own[:, 4 + s : 5 + s], lead)
    lead_ref[...] = lead[:final]
    small_ref[...] = own.T[0:8, :final]


def mass_add(mass_ref, bias_ref, got_ref, packed_ref, mass_out_ref, bias_out_ref):
    mass, bias = add_mass(mass_ref, bias_ref, got_ref)
    mass_out_ref[...] = mass
    bias_out_ref[...] = bias
    pack_mass(mass, bias, packed_ref)


def mix_finish(
    pixels,
    query_col_ref,
    keys_t_ref,
    patch_ref,
    variable_ref,
    mass_ref,
    bias_ref,
    got_ref,
    w_ref,
    query_ref,
    keep_ref,
    send_ref,
    grad_ref,
    scratch,
):
    width, rows = mass_ref.shape
    heads = width // HEAD_DIM
    mass, sums = add_mass(mass_ref, bias_ref, got_ref)
    mass = mass.astype(BF16)
    bias = jnp.concatenate(
        [jnp.broadcast_to(sums[head : head + 1], (HEAD_DIM, rows)) for head in range(heads)], axis=0
    )
    key_mass = (bias * query_col_ref[:, 0:1]).astype(BF16)
    total = jnp.sum(keys_t_ref[...] * bias, axis=1, keepdims=True)
    own = grad_ref.shape[1]
    start = lax.axis_index("dp") * own
    model_width = variable_ref.shape[1]
    channels = patch_ref.shape[0] * pixels
    mine = exact(iota((own, model_width), 1) == iota((own, model_width), 0) + start)
    total_row = jnp.broadcast_to(total, (width, LANES)).T[0:1]
    flat = patch_ref[...].reshape(channels, model_width)
    patch_t = dot(mine, flat, 1, 1).astype(BF16)
    patch_t = dot(patch_t, pixel_major(channels, pixels), 1, 1)
    variable_t = dot(mine, variable_ref[...], 1, 1)
    bottom = rows - channels - variable_ref.shape[0]
    table_t = jnp.concatenate([patch_t, variable_t, jnp.zeros((own, bottom), F32)], axis=1).astype(BF16)
    query_rows = jnp.broadcast_to(query_ref[...].astype(F32)[None], (16, model_width)).astype(BF16)
    grad_ref[0] = dot(mine, query_rows, 1, 1)[:, 0:1] * total_row
    grad_ref[1] = dot(table_t, key_mass, 1, 1)
    grad_ref[2] = dot(table_t, mass, 1, 1)
    back = dot(w_ref[1], key_mass) + dot(w_ref[2], mass)
    query_back = jnp.sum(w_ref[0].astype(F32) * total_row, axis=1, keepdims=True)
    scratch[...] = jnp.where(iota((own, rows), 1) == rows - 1, query_back, back)
    keep_part(scratch, keep_ref, send_ref, my_chip())


def keep_part(source, keep_ref, send_ref, which):
    step = keep_ref.shape[0]
    if step % 8:
        first, second = source[0:step], source[step : 2 * step]
        keep_ref[...] = jnp.where(which == 0, first, second)
        send_ref[...] = jnp.where(which == 0, second, first)
    else:
        keep_ref[...] = source[pl.ds(pl.multiple_of(which * step, 8), step)]
        send_ref[...] = source[pl.ds(pl.multiple_of((1 - which) * step, 8), step)]


def tables_next(kept_ref, got_ref, keep_ref, send_ref, scratch):
    scratch[...] = kept_ref[...] + got_ref[...]
    keep_part(scratch, keep_ref, send_ref, my_core())


def pair_sum(keep_ref, got_ref, out_ref, low_ref):
    total = keep_ref[...] + got_ref[...].astype(F32)
    out_ref[...] = total
    low_ref[...] = total.astype(BF16)


def take_rows(source_ref, out_ref):
    out_ref[...] = source_ref[...]


def take_weights(pixels, ids_ref, source_ref, out_ref, pick_ref):
    out_ref[...] = source_ref[...]
    channels = pick_ref.shape[0]
    pick = iota((channels, channels), 0) == places(ids_ref, channels // pixels, pixels)
    pick_ref[...] = pick.astype(F32).T.astype(BF16)


def by_chip(own_ref, far_ref, first_ref, second_ref):
    own, far = own_ref[...], far_ref[...]
    first = my_chip() == 0
    first_ref[...] = jnp.where(first, own, far)
    second_ref[...] = jnp.where(first, far, own)


def base_rows(bucket_ref, first_ref, second_ref, lead_ref, out_a_ref, out_b_ref):
    rows = lead_ref.shape[0]
    mark = exact(iota((16, rows), 1) == bucket_ref[0])
    lead = dot(mark, lead_ref[...])[0:1]
    out_a_ref[...] = first_ref[...].astype(F32) + lead
    out_b_ref[...] = second_ref[...].astype(F32) + lead


def field_sum(keep_ref, got_ref, own_ref, send_ref):
    total = keep_ref[...] + got_ref[...].astype(F32)
    quarter = own_ref.shape[1]
    first = my_chip() == 0
    own_ref[...] = jnp.where(first, total[:, :quarter], total[:, quarter:])
    send_ref[...] = jnp.where(first, total[:, quarter:], total[:, :quarter]).astype(BF16)


def field_last(own_ref, far_ref, out_ref):
    out_ref[0] = own_ref[...] + far_ref[...].astype(F32)


def rows_sum(keep_a_ref, got_a_ref, keep_b_ref, got_b_ref, mid_a_ref, mid_b_ref, own_ref, send_ref):
    part_a = keep_a_ref[...] + got_a_ref[...].astype(F32)
    part_b = keep_b_ref[...] + got_b_ref[...].astype(F32)
    first = my_chip() == 0
    own_ref[...] = jnp.where(first, part_a + mid_a_ref[...], part_b + mid_b_ref[...])
    send_ref[...] = jnp.where(first, part_b, part_a).astype(BF16)


def tables_last(pixels, variables, kept_ref, got_ref, patch_ref, variable_ref, query_ref):
    total = kept_ref[...] + got_ref[...]
    for p in range(pixels):
        patch_ref[p] = total[:, p * variables : (p + 1) * variables]
    variable_ref[...] = total[:, pixels * variables : (pixels + 1) * variables]
    query_ref[...] = total.T[total.shape[1] - 8 :]


def pairs(count, bit):
    return [(i, i ^ bit) for i in range(count)]


def body(
    mesh_dp,
    mesh_mp,
    input_field,
    variable_ids,
    lead_bucket,
    patch_table,
    variable_table,
    variable_query,
    mix_weights,
    mix_output,
    pos_table,
    lead_table,
    first_gain,
    first_bias,
    attn_weights,
    attn_output,
    second_gain,
    second_bias,
    up_weight,
    down_weight,
    cotangent,
):
    length = input_field.shape[2]
    channels = input_field.shape[1]
    variables = variable_ids.shape[0]
    pixels = channels // variables
    model_width = pos_table.shape[1]
    quarter = cotangent.shape[0]
    head_width = mix_weights.shape[2]
    hidden_width = up_weight.shape[1]
    heads = head_width // HEAD_DIM
    own_width = model_width // mesh_dp
    half = 2 * quarter
    latest, now = [], []
    v = types.SimpleNamespace()

    def call(kernel, outs, args, final=False, **options):
        if final:
            outs = outs + [((8, LANES), F32)]
            kernel = functools.partial(marked, kernel)
        known = flat(args)[0] + list(options.get("fetch", ()))
        after = [last for last in latest if all(last is not arg for arg in known)]
        cost = COSTS.get(now[0], 0.1)
        results = launch(kernel, outs, args, after=after, cost=cost, name=now[0], **options)
        latest[:] = results[-1:] if final else flat(results)[0][:1]
        return results[:-1] if final else results

    rows32 = ((quarter, model_width), F32)
    rows16 = ((quarter, model_width), BF16)
    cut16 = [((quarter // PIECES, model_width), BF16)] * PIECES

    def swap_core(value):
        if isinstance(value, list):
            return [swap_core(piece) for piece in value]
        return lax.ppermute(value, "mp", pairs(mesh_mp, 1))

    def swap_chip(value):
        return lax.ppermute(value, "mp", pairs(mesh_mp, 2))

    def swap_sample(value, bit):
        return lax.ppermute(value, "dp", pairs(mesh_dp, bit))

    def add_near(keep, near):
        kept, low = call(pair_sum, [rows32, rows16], [keep, near])
        return kept, swap_chip(low)

    all_bits = [1 << i for i in range(mesh_dp.bit_length() - 1)]
    wide = [bit for bit in all_bits if bit * own_width % LANES == 0]

    def order_from(axes):
        return [wide[i] for i in axes] + [bit for bit in all_bits if bit not in wide[:3]]

    def steps_of(order):
        left = list(all_bits)
        steps = []
        for bit in order:
            steps.append(own_width << left.index(bit))
            left.remove(bit)
        return steps

    def start_sum(load, inputs, width, order):
        step = steps_of(order)[0]
        (send,) = call(
            functools.partial(sum_start, load, step, order[0]),
            [((model_width // 2, width), BF16)],
            inputs,
        )
        return swap_sample(send, order[0])

    def halves(width, scratch_rows):
        kept = scratch_rows // 2
        return [((kept, width), F32), ((kept, width), BF16)]

    def second_sum(load, inputs, got, width, order):
        steps = steps_of(order)
        rows = model_width // 2
        keep, send = call(
            functools.partial(sum_second, load, steps[0], steps[1], order[0], order[1]),
            halves(width, rows),
            [got] + inputs,
            scratch=[pltpu.VMEM((rows, width), F32)],
        )
        return keep, swap_sample(send, order[1])

    def rest_sum(keep, got, order):
        steps = steps_of(order)
        for i in range(2, len(order)):
            rows, width = keep.shape
            keep, send = call(
                functools.partial(sum_next, steps[i], order[i]),
                halves(width, rows),
                [keep, got],
                scratch=[pltpu.VMEM((rows, width), F32)],
            )
            got = swap_sample(send, order[i])
        return keep, got

    def norm_rows(terms, gain, bias):
        return call(norm_forward, [rows32, cut16], terms + [gain, bias])

    w_mix = mix_weights.transpose(1, 0, 2)
    w_attn = attn_weights.transpose(1, 0, 2)
    gain_one, bias_one = first_gain[None], first_bias[None]
    gain_two, bias_two = second_gain[None], second_bias[None]
    table_rows = channels + variables
    padded = -(-(table_rows + 1) // LANES) * LANES
    lines = -(-(4 + 2 * mesh_dp) // LANES) * LANES
    mix_width = head_width + quarter + lines
    attn_width = 4 * head_width
    final = own_width // mesh_mp
    own_field = (channels, quarter)
    proj_kind = ((3, half, head_width), BF16)
    attend_kinds = [((half, head_width), BF16), ((8, half), F32), rows32, cut16]
    hidden_kind = ((half, hidden_width), F32)
    mlp_kinds = [((half, hidden_width), BF16)] * 2 + [rows32, cut16]
    back_kinds = [rows32, cut16, ((8, model_width), F32)]
    grad_kinds = [((half, head_width), BF16)] + [((length, head_width), F32)] * 2
    mass_kinds = [
        ((head_width + 16, padded), BF16),
        ((head_width, padded), F32),
        ((8, padded), F32),
    ]
    rest_rows = pltpu.VMEM((quarter + lines, model_width), F32)
    down_order, up_order, attn_order, mix_order, mass_bits = map(order_from, AXES)
    mix_steps = steps_of(mix_order)
    back_two = functools.partial(norm_backward, False, 0)

    def mix_a():
        v.mixed_t, v.field_t, v.probs, v.values, v.keys_t, v.score, v.query_col = call(
            functools.partial(mix_forward, pixels, quarter),
            [
                ((head_width, length), BF16),
                ((channels, length), BF16),
                ((heads * variables, length), F32),
                ((padded, head_width), BF16),
                ((head_width, padded), F32),
                ((padded, LANES), F32),
                ((head_width, LANES), F32),
            ],
            [],
            fetch=[variable_ids, input_field, patch_table, variable_table, w_mix, variable_query],
            limit=FIRST_LIMIT,
            lazy=True,
            scratch=[pltpu.VMEM((padded, model_width), BF16)],
        )

    def mix_b():
        send_a, send_b, v.keep_a, v.keep_b = call(
            mix_out, [rows16, rows16, rows32, rows32], [v.mixed_t, mix_output]
        )
        v.near_a, v.near_b = swap_core(send_a), swap_core(send_b)

    def first_a():
        v.kept_a, v.far_a = add_near(v.keep_a, v.near_a)

    def first_b():
        v.kept_b, v.far_b = add_near(v.keep_b, v.near_b)

    def second_a():
        first_a()

    def second_b():
        first_b()

    def base():
        blocks = [
            (
                pos_table,
                (quarter, model_width),
                lambda ref, k=k: ref.at[pl.ds((2 * k + my_core()) * quarter, quarter)],
            )
            for k in range(2)
        ]
        v.base_a, v.base_b = call(
            base_rows, [rows32] * 2, [], fetch=blocks + [lead_table], smem=[lead_bucket]
        )

    def norm_a():
        v.in_a, v.one_a0 = norm_rows([v.kept_a, v.far_a, v.base_a], gain_one, bias_one)
        v.one_a1 = swap_core(v.one_a0)

    def proj():
        (v.proj_a,) = call(project, [proj_kind], [v.one_a0, v.one_a1, w_attn])

    def norm_b():
        v.in_b, v.one_b0, v.cot_own = call(
            norm_relay,
            [rows32, cut16, rows16],
            [cotangent, v.kept_b, v.far_b, v.base_b, gain_one, bias_one],
        )
        v.one_b1 = swap_core(v.one_b0)
        v.cot_far = swap_chip(v.cot_own)

    def attend_a():
        v.proj_b, v.attended_a, v.logs_a, v.keep_a, send_a = call(
            attend_first,
            [proj_kind] + attend_kinds,
            [v.one_b0, v.one_b1, w_attn, v.proj_a, attn_output],
        )
        v.near_a = swap_core(send_a)

    def attend_b():
        v.attended_b, v.logs_b, v.keep_b, send_b = call(
            attend_second, attend_kinds, [v.proj_a, v.proj_b, attn_output]
        )
        v.near_b = swap_core(send_b)

    def cot():
        v.cot_a0, v.cot_b0 = call(by_chip, [cut16] * 2, [v.cot_own, v.cot_far])
        v.cot_a1, v.cot_b1 = swap_core(v.cot_a0), swap_core(v.cot_b0)

    def hidden_a():
        (v.grad_hidden_a,) = call(hidden_back, [hidden_kind], [v.cot_a0, v.cot_a1, down_weight])

    def hidden_b():
        (v.grad_hidden_b,) = call(hidden_back, [hidden_kind], [v.cot_b0, v.cot_b1, down_weight])

    def two_a():
        v.mid_a, v.two_a0 = norm_rows([v.kept_a, v.far_a, v.in_a], gain_two, bias_two)
        v.two_a1 = swap_core(v.two_a0)

    def two_b():
        v.mid_b, v.two_b0 = norm_rows([v.kept_b, v.far_b, v.in_b], gain_two, bias_two)
        v.two_b1 = swap_core(v.two_b0)

    def mlp_a():
        v.hidden_a, v.pre_a, v.m_keep_a, send_a = call(
            mlp, mlp_kinds, [v.two_a0, v.two_a1, up_weight, v.grad_hidden_a]
        )
        v.m_near_a = swap_core(send_a)

    def mlp_b():
        v.hidden_b, v.pre_b, v.m_keep_b, send_b = call(
            mlp, mlp_kinds, [v.two_b0, v.two_b1, up_weight, v.grad_hidden_b]
        )
        v.m_near_b = swap_core(send_b)

    def third_a():
        v.m_kept_a, v.m_far_a = add_near(v.m_keep_a, v.m_near_a)

    def third_b():
        v.m_kept_b, v.m_far_b = add_near(v.m_keep_b, v.m_near_b)

    def down_in():
        return [v.cot_a0, v.cot_a1, v.cot_b0, v.cot_b1, v.hidden_a, v.hidden_b]

    def up_in():
        return [v.two_a0, v.two_a1, v.two_b0, v.two_b1, v.pre_a, v.pre_b]

    def attn_in():
        one = [v.one_a0, v.one_a1, v.one_b0, v.one_b1]
        mid = [v.back_a0, v.back_a1, v.back_b0, v.back_b1]
        return one + mid + [v.grad_proj, v.attended_a, v.attended_b]

    def up_1():
        v.up_got = start_sum(load_plain, up_in(), hidden_width, up_order)

    def down_1():
        v.down_got = start_sum(load_plain, down_in(), hidden_width, down_order)

    def attn_1():
        v.attn_got = start_sum(load_attn, attn_in(), attn_width, attn_order)

    def up_2():
        v.up_keep, v.up_got = second_sum(load_plain, up_in(), v.up_got, hidden_width, up_order)

    def down_2():
        v.down_keep, v.down_got = second_sum(
            load_plain, down_in(), v.down_got, hidden_width, down_order
        )

    def attn_2():
        v.attn_keep, v.attn_got = second_sum(
            load_attn, attn_in(), v.attn_got, attn_width, attn_order
        )

    def up_3():
        v.up_keep, v.up_got = rest_sum(v.up_keep, v.up_got, up_order)

    def down_3():
        v.down_keep, v.down_got = rest_sum(v.down_keep, v.down_got, down_order)

    def attn_3():
        v.attn_keep, v.attn_got = rest_sum(v.attn_keep, v.attn_got, attn_order)

    def mid_a():
        v.grad_mid_a, v.back_a0, v.sums_two_a = call(
            back_two, back_kinds, [v.m_kept_a, v.m_far_a, v.mid_a, gain_two, v.cot_a0]
        )
        v.back_a1 = swap_core(v.back_a0)

    def mid_b():
        v.grad_mid_b, v.back_b0, v.sums_two_b = call(
            back_two, back_kinds, [v.m_kept_b, v.m_far_b, v.mid_b, gain_two, v.cot_b0]
        )
        v.back_b1 = swap_core(v.back_b0)

    def back_a():
        v.query_grad, v.key_grad, v.value_grad = call(
            attend_back_first,
            grad_kinds,
            [v.back_a0, v.back_a1, attn_output, v.proj_a, v.proj_b, v.logs_a],
        )

    def back_b():
        v.grad_proj, v.p_keep_a, send_a = call(
            attend_back_second,
            [((3, length, head_width), BF16), rows32, cut16],
            [
                v.back_b0,
                v.back_b1,
                attn_output,
                v.proj_a,
                v.proj_b,
                v.logs_b,
                v.query_grad,
                v.key_grad,
                v.value_grad,
                w_attn,
            ],
        )
        v.p_near_a = swap_core(send_a)

    def back_c():
        v.p_keep_b, send_b = call(attend_back_last, [rows32, cut16], [v.grad_proj, w_attn])
        v.p_near_b = swap_core(send_b)

    def fourth_a():
        v.p_kept_a, v.p_far_a = add_near(v.p_keep_a, v.p_near_a)

    def fourth_b():
        v.p_kept_b, v.p_far_b = add_near(v.p_keep_b, v.p_near_b)

    def in_a():
        v.grad_in_a, v.in_a0, v.sums_one_a = call(
            functools.partial(norm_backward, True, 0),
            back_kinds,
            [v.p_kept_a, v.p_far_a, v.in_a, gain_one, v.grad_mid_a],
        )
        v.in_a1 = swap_core(v.in_a0)

    def in_b():
        v.grad_in_b, v.in_b0, v.sums = call(
            functools.partial(norm_backward, True, 3),
            back_kinds,
            [
                v.p_kept_b,
                v.p_far_b,
                v.in_b,
                gain_one,
                v.grad_mid_b,
                v.sums_one_a,
                v.sums_two_a,
                v.sums_two_b,
            ],
        )
        v.in_b1 = swap_core(v.in_b0)
        v.near_sums = swap_core(v.sums)

    def mass_1():
        packed, v.mass, v.bias, v.field_send, v.field_keep = call(
            functools.partial(mix_backward, pixels),
            mass_kinds + [((channels, half), BF16), ((channels, half), F32)],
            [v.pick, v.field_t, v.probs, v.values, v.score, mix_output, v.in_a0, v.in_a1, v.in_b0, v.in_b1],
        )
        v.mass_got = swap_sample(packed, mass_bits[0])
        v.field_near = swap_core(v.field_send)

    def add_masses(bits):
        for bit in bits:
            packed, v.mass, v.bias = call(mass_add, mass_kinds, [v.mass, v.bias, v.mass_got])
            v.mass_got = swap_sample(packed, bit)

    def mass_2():
        add_masses(mass_bits[1:2])

    def mass_3():
        add_masses(mass_bits[2:])

    def mix_in():
        rows = [v.in_a0, v.in_a1, v.in_b0, v.in_b1]
        return rows + [v.grad_in_a, v.grad_in_b, v.sums, v.near_sums]

    def mix_1():
        (send,) = call(
            functools.partial(mix_start, mesh_dp, lines, mix_steps[0], mix_order[0]),
            [((model_width // 2, mix_width), BF16)],
            [v.mixed_t] + mix_in(),
            smem=[lead_bucket],
            scratch=[rest_rows],
        )
        v.mix_got = swap_sample(send, mix_order[0])

    def mix_2():
        v.mix_keep, send = call(
            functools.partial(
                mix_second, mesh_dp, lines, mix_steps[0], mix_steps[1], mix_order[0], mix_order[1]
            ),
            halves(mix_width, model_width // 2),
            [v.mixed_t, v.mix_got] + mix_in(),
            smem=[lead_bucket],
            scratch=[rest_rows, pltpu.VMEM((model_width // 2, mix_width), F32)],
        )
        v.mix_got = swap_sample(send, mix_order[1])

    def mix_3():
        v.mix_keep, v.mix_got = rest_sum(v.mix_keep, v.mix_got, mix_order)

    def field_1():
        v.field_own, far = call(
            field_sum, [(own_field, F32), (own_field, BF16)], [v.field_keep, v.field_near]
        )
        v.field_got = swap_chip(far)

    def field_2():
        (v.field_grad,) = call(
            field_last, [((1,) + own_field, F32)], [v.field_own, v.field_got], final=True
        )

    def rows_1():
        v.r_keep_a, send_a, v.r_keep_b, send_b = call(
            mlp_out, [rows32, cut16] * 2, [v.hidden_a, v.hidden_b, down_weight]
        )
        v.r_near_a, v.r_near_b = swap_core(send_a), swap_core(send_b)

    def rows_2():
        v.rows_own, far = call(
            rows_sum,
            [rows32, rows16],
            [v.r_keep_a, v.r_near_a, v.r_keep_b, v.r_near_b, v.mid_a, v.mid_b],
        )
        v.rows_got = swap_chip(far)

    def rows_3():
        (v.activations,) = call(last_plain, [rows32], [v.rows_own, v.rows_got], final=True)

    def weights():
        v.own_weights, v.pick = call(
            functools.partial(take_weights, pixels),
            [((3, own_width, head_width), BF16), ((channels, channels), BF16)],
            [],
            smem=[variable_ids],
            fetch=[
                (
                    w_mix,
                    (3, own_width, head_width),
                    lambda ref: ref.at[:, pl.ds(lax.axis_index("dp") * own_width, own_width)],
                )
            ],
        )

    def finish():
        v.t_keep, send, v.grad_mix = call(
            functools.partial(mix_finish, pixels),
            [((own_width // 2, padded), F32)] * 2 + [((3, own_width, head_width), F32)],
            [
                v.query_col,
                v.keys_t,
                patch_table,
                variable_table,
                v.mass,
                v.bias,
                v.mass_got,
                v.own_weights,
                variable_query,
            ],
            scratch=[pltpu.VMEM((own_width, padded), F32)],
        )
        v.t_far = swap_chip(send)

    def tables_1():
        v.t_keep, send = call(
            tables_next,
            [((final, padded), F32)] * 2,
            [v.t_keep, v.t_far],
            scratch=[pltpu.VMEM((own_width // 2, padded), F32)],
        )
        v.t_near = swap_core(send)

    def tables_2():
        v.patch_total, v.variable_total, v.query_total = call(
            functools.partial(tables_last, pixels, variables),
            [((pixels, final, variables), F32), ((final, variables), F32), ((8, final), F32)],
            [v.t_keep, v.t_near],
            final=True,
        )

    def down_4():
        (v.down_sum,) = call(
            last_turned, [((hidden_width, own_width), F32)], [v.down_keep, v.down_got], final=True
        )

    def up_4():
        (v.up_sum,) = call(
            last_plain, [((own_width, hidden_width), F32)], [v.up_keep, v.up_got], final=True
        )

    def mix_4():
        v.mix_out_sum, v.pos_sum, v.lead_total, v.small = call(
            functools.partial(mix_last, mesh_dp, quarter, final),
            [
                ((head_width, own_width), F32),
                ((quarter, own_width), F32),
                ((final, lead_table.shape[0]), F32),
                ((8, final), F32),
            ],
            [v.mix_keep, v.mix_got],
            final=True,
        )

    def attn_4():
        v.attn_sum, v.attn_out_sum = call(
            last_attn,
            [((3, own_width, head_width), F32), ((head_width, own_width), F32)],
            [v.attn_keep, v.attn_got],
            final=True,
        )

    steps = dict(locals())
    for name in ORDER:
        now[:] = [name]
        steps[name]()
    return (
        v.activations,
        v.field_grad,
        v.patch_total.transpose(2, 0, 1),
        v.variable_total.T,
        v.query_total[7],
        v.grad_mix.transpose(1, 0, 2),
        v.mix_out_sum,
        v.pos_sum,
        v.lead_total.T,
        v.small[0],
        v.small[1],
        v.attn_sum.transpose(1, 0, 2),
        v.attn_out_sum,
        v.small[2],
        v.small[3],
        v.up_sum,
        v.down_sum,
    )


def solution(mesh):
    in_specs = (
        P("dp", None, None),
        P(),
        P("dp"),
        P(),
        P(),
        P(),
        P(None, None, "mp"),
        P("mp", None),
        P(),
        P(),
        P(),
        P(),
        P(None, None, "mp"),
        P("mp", None),
        P(),
        P(),
        P(None, "mp"),
        P("mp", None),
        P(("dp", "mp"), None),
    )
    out_specs = (
        P(("dp", "mp"), None),
        P("dp", None, "mp"),
        P(None, None, ("dp", "mp")),
        P(None, ("dp", "mp")),
        P(("dp", "mp")),
        P("dp", None, "mp"),
        P("mp", "dp"),
        P("mp", "dp"),
        P(None, ("dp", "mp")),
        P(("dp", "mp")),
        P(("dp", "mp")),
        P("dp", None, "mp"),
        P("mp", "dp"),
        P(("dp", "mp")),
        P(("dp", "mp")),
        P("dp", "mp"),
        P("mp", "dp"),
    )
    step = functools.partial(body, mesh.shape["dp"], mesh.shape["mp"])
    return jax.shard_map(step, mesh=mesh, in_specs=in_specs, out_specs=out_specs, check_vma=False)
```
